512 devices in a mesh: tm: 64 (over y_lo, z, x), head: 8 (over y_hi, core).
Axes of the slice: x: 4, y: 8 (y_hi: 4, y_lo: 2; y = y_hi * 2 + y_lo), z: 8, core: 2. Of those that a mesh axis runs over, the one named last changes fastest.
Arguments:
- frames: bfloat16 [8192, 1920], P('tm', 'head'), may hold values from -6 to 6
- conv_weight: bfloat16 [64, 16, 120, 120], P('tm', 'head'), may hold values from -0.0625 to 0.0625
- w_qkv: bfloat16 [1920, 2880], P(None, 'head'), may hold values from -0.5 to 0.5
- lengths: int32 [4], replicated, may hold values from 1 to 4096, 8192 in all
- grad_out: bfloat16 [8192, 960], P('tm', 'head'), may hold values from -6 to 6
Outputs:
- attn_out: bfloat16 [8192, 960], P('tm', 'head')
- frame_grad: bfloat16 [8192, 1920], P('tm', 'head')
- weight_grad: float32 [1920, 2880], P('tm', 'head')
The draws below stay inside these ranges and needn't reach their ends.
Inputs may be any that keep to these rules, and one draw needn't show every extreme that they name: 4 positive lengths summing to 8192; the longest is exactly 4096.
All inputs are finite; a program needn't handle non-finite values.
Results may differ from the reference program's by a relative error of at most 0.022.
Values may be sent and summed in bfloat16 or wider, within the bound.
No kernel may reach another device: no remote copies, remote signals or barrier semaphores. Data moves between devices by JAX's collectives and lax.ppermute only.
A program may use at most 64 MiB of HBM per device.

```python
import math
import jax
import jax.numpy as jnp
import numpy as np
from jax import lax

D = 1920
GROUPS = 16
HD = 120
HEADS = 8
KERNEL = 64
UTTS = 4
GC = 120
TOKENS = 8192
MOST = 4096


def draw_w_qkv(key, part):
    key = jax.random.fold_in(key, 11)
    drawn_key = jax.random.fold_in(key, 0)
    spread = D ** (-0.5)
    bound_value = min(0.5, 6.0 * spread)
    drawn_draw = jnp.clip(jax.random.normal(drawn_key, (D, HEADS, 3, HD), jnp.float32) * spread, -bound_value, bound_value)
    return drawn_draw.reshape(D, HEADS * 3 * HD).astype(jnp.bfloat16)


def steps_of(key, shape, shards, smallest, high):
    level = 1.0
    for position, shards_of in shards:
        steps = jax.random.uniform(jax.random.fold_in(jax.random.fold_in(key, 6), position), (shards_of,), jnp.float32, smallest / len(shards), high / len(shards))
        level = level * jnp.repeat(jnp.exp(steps), shape[position] // shards_of).reshape((-1,) + (1,) * (len(shape) - 1 - position))
    return level


def profile(count, total, bound, skew):
    weights = [(1 << 20) // math.isqrt(rank ** skew) + 1 for rank in range(2, count + 1)]
    rest, given = total - bound - (count - 1), [1] * (count - 1)
    while rest > 0:
        free = [i for i in range(count - 1) if given[i] < bound]
        whole, left = sum([weights[i] for i in free]), rest
        for i in free:
            addition = min(bound - given[i], max(1, left * weights[i] // whole), rest)
            given[i] = given[i] + addition
            rest = rest - addition
    return np.array([bound] + given)


def ragged(own_key, amount, total, reach, skew):
    if amount == 2:
        one = jax.random.randint(own_key, (), max(1, total - reach), min(reach, total - 1) + 1)
        return jnp.stack([one, total - one])
    tallies = jnp.asarray(profile(amount, total, reach, skew), jnp.int32)
    couples = (amount - 1) // 2
    donor, taker = tallies[1:1 + 2 * couples:2], tallies[2:2 + 2 * couples:2]
    margin = jnp.minimum(donor - 1, reach - taker)
    passed = jax.random.randint(jax.random.fold_in(own_key, 1), (couples,), 0, 1 << 20) % (margin + 1)
    tallies = tallies.at[1:1 + 2 * couples:2].set(donor - passed).at[2:2 + 2 * couples:2].set(taker + passed)
    return tallies[jax.random.permutation(jax.random.fold_in(own_key, 2), amount)]


def bell_draw(key, extent, width, most, pieces=(), kind=jnp.bfloat16):
    level = steps_of(key, extent, pieces, -0.22, 0.18) if pieces else 1.0
    entries = jax.random.normal(key, extent, jnp.float32) * width * level
    return jnp.minimum(jnp.maximum(entries, -most), most).astype(kind)


def setup_inputs(seed: int = 0) -> dict:
    key_list = jax.random.split(jax.random.key(seed), 6)
    frames = bell_draw(key_list[0], (TOKENS, D), 1.0, 6.0, ((0, 64), (1, 8)))
    conv_weight = bell_draw(key_list[1], (KERNEL, GROUPS, GC, GC), (KERNEL * GC) ** -0.5, 0.0625, ((0, 64), (1, 8)))
    w_qkv = draw_w_qkv(jax.random.fold_in(key_list[5], 71), 0)
    lengths = ragged(key_list[3], UTTS, TOKENS, MOST, 2).astype(jnp.int32)
    grad_out = bell_draw(key_list[4], (TOKENS, HEADS * HD), 1.0, 6.0, ((0, 64), (1, 8)))
    return {"frames": frames, "conv_weight": conv_weight, "w_qkv": w_qkv, "lengths": lengths, "grad_out": grad_out}


inv_root_two = 0.7071067811865476
inv_root_tau = 0.3989422804014327
epsilon = 1e-05

def segment_of(positions, lengths):
    boundary = jnp.cumsum(lengths)
    return lax.optimization_barrier(jnp.sum((positions[:, None] >= boundary[None, :]).astype(jnp.int32), axis=1))

def gelu_parts(inputs):
    normal_cdf = 0.5 * (1.0 + lax.erf(inputs * inv_root_two))
    density = jnp.exp(-0.5 * inputs * inputs) * inv_root_tau
    return (inputs * normal_cdf, normal_cdf + inputs * density)

def conv_sweep(padded, seg_pad, seg_rows, weights, forward):

    def one_tap(running, offset):
        start = offset if forward else KERNEL - offset
        piece = lax.dynamic_slice_in_dim(padded, start, TOKENS, 0).astype(jnp.float32)
        keep = (lax.dynamic_slice_in_dim(seg_pad, start, TOKENS, 0) == seg_rows).astype(jnp.float32)
        piece = (piece * keep[:, None]).reshape(TOKENS, GROUPS, GC)
        tap_weight = weights[offset]
        if forward:
            term = jnp.einsum('tgi,gio->tgo', piece, tap_weight, precision=lax.Precision.HIGHEST)
        else:
            term = jnp.einsum('tgo,gio->tgi', piece, tap_weight, precision=lax.Precision.HIGHEST)
        return (running + term, None)
    start_value = jnp.zeros((TOKENS, GROUPS, GC), jnp.float32)
    result, _ = lax.scan(one_tap, start_value, jnp.arange(KERNEL, dtype=jnp.int32))
    return result.reshape(TOKENS, D)

def reference(frames, conv_weight, w_qkv, lengths, grad_out):
    half_kernel = KERNEL // 2
    score_scale = HD ** (-0.5)
    seg_rows = segment_of(jnp.arange(TOKENS, dtype=jnp.int32), lengths)
    seg_pad = segment_of(jnp.arange(TOKENS + KERNEL, dtype=jnp.int32) - half_kernel, lengths)
    weights = conv_weight.astype(jnp.float32)
    frames_pad = jnp.pad(frames, ((half_kernel, half_kernel), (0, 0)))
    conv_out = conv_sweep(frames_pad, seg_pad, seg_rows, weights, True)
    activated, slope = gelu_parts(conv_out)
    hidden = frames.astype(jnp.float32) + activated
    center = lax.optimization_barrier(jnp.sum(hidden, axis=1)) / D
    inv_std = lax.rsqrt(lax.optimization_barrier(jnp.sum(hidden * hidden, axis=1)) / D - center * center + epsilon)
    unit_rows = (hidden - center[:, None]) * inv_std[:, None]
    normed = unit_rows.astype(jnp.bfloat16)
    projected = jnp.dot(normed, w_qkv, preferred_element_type=jnp.float32).astype(jnp.bfloat16)
    projected = projected.reshape(TOKENS, HEADS, 3, HD)
    query_heads = jnp.transpose(projected[:, :, 0], (1, 0, 2))
    key_heads = jnp.transpose(projected[:, :, 1], (1, 0, 2))
    value_heads = jnp.transpose(projected[:, :, 2], (1, 0, 2))
    upstream_heads = jnp.transpose(grad_out.reshape(TOKENS, HEADS, HD), (1, 0, 2))
    same_rows = seg_rows[:, None] == seg_rows[None, :]

    def head_pass(inputs):
        query_rows, key_rows, value_rows, upstream = inputs
        scores = jnp.dot(query_rows, key_rows.T, preferred_element_type=jnp.float32) * score_scale
        scores = jnp.where(same_rows, scores, -jnp.inf)
        peak = lax.optimization_barrier(jnp.max(scores, axis=1, keepdims=True))
        denominator = lax.optimization_barrier(jnp.sum(jnp.exp(scores - peak), axis=1, keepdims=True))
        log_total = peak + jnp.log(denominator)
        attention = jnp.exp(scores - log_total)
        attention_b = attention.astype(jnp.bfloat16)
        attended = jnp.dot(attention_b, value_rows, preferred_element_type=jnp.float32).astype(jnp.bfloat16)
        delta = lax.optimization_barrier(jnp.sum(upstream.astype(jnp.float32) * attended.astype(jnp.float32), axis=1, keepdims=True))
        dprobs = jnp.dot(upstream, value_rows.T, preferred_element_type=jnp.float32)
        dscores = (attention * (dprobs - delta) * score_scale).astype(jnp.bfloat16)
        grad_q = jnp.dot(dscores, key_rows, preferred_element_type=jnp.float32).astype(jnp.bfloat16)
        grad_k = jnp.dot(dscores.T, query_rows, preferred_element_type=jnp.float32).astype(jnp.bfloat16)
        grad_v = jnp.dot(attention_b.T, upstream, preferred_element_type=jnp.float32).astype(jnp.bfloat16)
        return (attended, grad_q, grad_k, grad_v)
    attended, grad_q, grad_k, grad_v = lax.map(head_pass, (query_heads, key_heads, value_heads, upstream_heads))
    attn_out = jnp.transpose(attended, (1, 0, 2)).reshape(TOKENS, HEADS * HD)
    grad_joined = jnp.stack([grad_q, grad_k, grad_v], axis=2)
    grad_joined = jnp.transpose(grad_joined, (1, 0, 2, 3)).reshape(TOKENS, HEADS * 3 * HD)
    weight_grad = jnp.dot(normed.T, grad_joined, preferred_element_type=jnp.float32)
    feature_grad = jnp.dot(grad_joined, w_qkv.T, preferred_element_type=jnp.float32)
    plain_mean = lax.optimization_barrier(jnp.sum(feature_grad, axis=1)) / D
    unit_mean = lax.optimization_barrier(jnp.sum(feature_grad * unit_rows, axis=1)) / D
    hidden_grad = inv_std[:, None] * (feature_grad - plain_mean[:, None] - unit_rows * unit_mean[:, None])
    error_rows = (slope * hidden_grad).astype(jnp.bfloat16)
    error_pad = jnp.pad(error_rows, ((half_kernel, half_kernel), (0, 0)))
    conv_back = conv_sweep(error_pad, seg_pad, seg_rows, weights, False)
    frame_grad = (hidden_grad + conv_back).astype(jnp.bfloat16)
    return (attn_out, frame_grad, weight_grad)
```

```python
import functools
import math

import jax
import jax.numpy as jnp
from jax import lax
from jax.experimental import pallas as pl
from jax.experimental.pallas import tpu as pltpu
from jax.sharding import PartitionSpec as P

HD = 120
KERNEL = 64
HALF = KERNEL // 2
ROWS = 128
LANES = 128
SCALE = HD ** (-0.5)
SCALE2 = SCALE * math.log2(math.e)
FAR = -(2.0**100)
EPS = 1e-05
INV_ROOT_TWO = 0.7071067811865476
INV_ROOT_TAU = 0.3989422804014327

BF = jnp.bfloat16
F32 = jnp.float32

XY_GROUPS = [[y * 32 + z * 4 + x for y in range(2) for x in range(4)] for z in range(8)]
Z_GROUPS = [[y * 32 + z * 4 + x for z in range(8)] for y in range(2) for x in range(4)]


def exchange_xy(parts):
    return lax.all_to_all(parts, "tm", 0, 0, axis_index_groups=XY_GROUPS)


def exchange_z(parts):
    return lax.all_to_all(parts, "tm", 0, 0, axis_index_groups=Z_GROUPS)


def everyone(array):
    return jnp.broadcast_to(array[None], (8,) + array.shape)


def vmem_call(body, out_shape, scratch=(), scalars=0, inputs=0, flops=0):
    return pl.pallas_call(
        body,
        out_shape=out_shape,
        in_specs=[pl.BlockSpec(memory_space=pltpu.SMEM)] * scalars
        + [pl.BlockSpec(memory_space=pltpu.VMEM)] * inputs,
        out_specs=jax.tree.map(lambda _: pl.BlockSpec(memory_space=pltpu.VMEM), out_shape),
        scratch_shapes=list(scratch),
        compiler_params=pltpu.CompilerParams(vmem_limit_bytes=48 * 1024 * 1024),
        cost_estimate=pl.CostEstimate(flops=flops, bytes_accessed=1 << 20, transcendentals=0),
    )


def conv_body(forward, sc_ref, x_ref, w_ref, out_ref):
    first = sc_ref[0]
    row = lax.broadcasted_iota(jnp.int32, (ROWS, HD), 0)

    def block(b, carry):
        shard = (b // 4) * 32 + sc_ref[1] + b % 4
        pos = shard * ROWS + row
        low = jnp.zeros_like(pos)
        high = jnp.full_like(pos, sc_ref[2])
        for u in range(3):
            end = sc_ref[2 + u]
            inside = pos >= end
            low = jnp.where(inside, end, low)
            high = jnp.where(inside, sc_ref[3 + u], high)
        source = pos - HALF + first
        keep = [
            ((source + 4 * s) >= low) & ((source + 4 * s) < high) for s in range(8)
        ]
        for g in range(2):
            x = x_ref[b, g].astype(F32)
            even = pltpu.roll(x, ROWS + KERNEL - first, 0)
            odd = pltpu.roll(x, ROWS + KERNEL - first - 4, 0)
            total = jnp.zeros((ROWS, HD), F32)
            for s in range(8):
                rolled = odd if s % 2 else even
                start = 8 * (s // 2)
                piece = jnp.where(keep[s], rolled[start : start + ROWS], 0.0).astype(BF)
                if forward:
                    total += jnp.dot(piece, w_ref[s, g], preferred_element_type=F32)
                else:
                    total += lax.dot_general(
                        piece,
                        w_ref[7 - s, g],
                        (((1,), (1,)), ((), ())),
                        preferred_element_type=F32,
                    )
            out_ref[b, g] = total.astype(BF)
        return carry

    lax.fori_loop(0, 8, block, 0)


def conv_partial(forward, scalars, padded, taps):
    return vmem_call(
        functools.partial(conv_body, forward),
        jax.ShapeDtypeStruct((8, 2, ROWS, HD), BF),
        scalars=1,
        inputs=2,
        flops=8 * 2 * 8 * 2 * ROWS * HD * HD,
    )(scalars, padded, taps)


def with_halo(rows):
    devices = 64
    up = [(i, i + 1) for i in range(devices - 1)]
    down = [(i + 1, i) for i in range(devices - 1)]
    before = lax.ppermute(rows[:, ROWS - HALF :], "tm", up)
    after = lax.ppermute(rows[:, :HALF], "tm", down)
    return jnp.concatenate([before, rows, after], axis=1)


CHUNK = 256


def stats_body(qd_ref, kv_ref, out_ref):
    keys = kv_ref[:, :, :LANES].reshape(8 * ROWS, LANES)
    values = kv_ref[:, :, LANES:].reshape(8 * ROWS, LANES)
    out_ref[...] = jnp.zeros_like(out_ref)
    for c in range(8 * ROWS // CHUNK):
        n = CHUNK // ROWS
        q = qd_ref[c * n : (c + 1) * n, :, :LANES].reshape(CHUNK, LANES)
        d = qd_ref[c * n : (c + 1) * n, :, LANES:].reshape(CHUNK, LANES)
        contract = (((1,), (1,)), ((), ()))
        scores = lax.dot_general(keys, q, contract, preferred_element_type=F32)
        dprobs = lax.dot_general(values, d, contract, preferred_element_type=F32)
        peak = jnp.max(scores, axis=0, keepdims=True) * SCALE2
        weight = jnp.exp2(scores * SCALE2 - peak)
        columns = slice(c * CHUNK, (c + 1) * CHUNK)
        out_ref[0:1, columns] = peak
        out_ref[1:2, columns] = jnp.sum(weight, axis=0, keepdims=True)
        out_ref[2:3, columns] = jnp.sum(weight * dprobs, axis=0, keepdims=True)


def grads_body(qd_ref, kv_ref, stats_ref, od_ref, dkv_ref, dk_ref, dv_ref):
    keys = kv_ref[:, :, :LANES].reshape(8 * ROWS, LANES)
    values = kv_ref[:, :, LANES:].reshape(8 * ROWS, LANES)
    peaks = stats_ref[:, 0, :]
    top = jnp.max(peaks, axis=0, keepdims=True)
    factor = jnp.exp2(peaks - top)
    total = jnp.sum(stats_ref[:, 1, :] * factor, axis=0, keepdims=True)
    delta = jnp.sum(stats_ref[:, 2, :] * factor, axis=0, keepdims=True) / total
    lse = top + jnp.log2(total)
    for c in range(8 * ROWS // CHUNK):
        n = CHUNK // ROWS
        q = qd_ref[c * n : (c + 1) * n, :, :LANES].reshape(CHUNK, LANES)
        d = qd_ref[c * n : (c + 1) * n, :, LANES:].reshape(CHUNK, LANES)
        columns = slice(c * CHUNK, (c + 1) * CHUNK)
        contract = (((1,), (1,)), ((), ()))
        scores = lax.dot_general(keys, q, contract, preferred_element_type=F32)
        dprobs = lax.dot_general(values, d, contract, preferred_element_type=F32)
        probs = jnp.exp2(scores * SCALE2 - lse[:, columns])
        dscores = (probs * (dprobs - delta[:, columns])).astype(BF)
        probs = probs.astype(BF)
        dv = jnp.dot(probs, d, preferred_element_type=F32)
        dk = jnp.dot(dscores, q, preferred_element_type=F32)
        if c == 0:
            dv_ref[...] = dv
            dk_ref[...] = dk
        else:
            dv_ref[...] += dv
            dk_ref[...] += dk
        inner = (((0,), (0,)), ((), ()))
        out_t = lax.dot_general(values, probs, inner, preferred_element_type=F32)
        dq_t = lax.dot_general(keys, dscores, inner, preferred_element_type=F32) * SCALE
        for i in range(n):
            od_ref[c * n + i, 0] = out_t[:HD, i * ROWS : (i + 1) * ROWS].astype(BF)
            od_ref[c * n + i, 1] = dq_t[:HD, i * ROWS : (i + 1) * ROWS].astype(BF)
    for i in range(8):
        piece = slice(i * ROWS, (i + 1) * ROWS)
        dkv_ref[i, :, :LANES] = (dk_ref[piece] * SCALE).astype(BF)
        dkv_ref[i, :, LANES:] = dv_ref[piece].astype(BF)


def attention_stats(queries, keys):
    return vmem_call(
        stats_body,
        jax.ShapeDtypeStruct((8, 8 * ROWS), F32),
        inputs=2,
        flops=2 * 2 * (8 * ROWS) ** 2 * LANES,
    )(queries, keys)


def attention_grads(queries, keys, stats):
    return vmem_call(
        grads_body,
        (
            jax.ShapeDtypeStruct((8, 2, HD, ROWS), BF),
            jax.ShapeDtypeStruct((8, ROWS, 2 * LANES), BF),
        ),
        scratch=[pltpu.VMEM((8 * ROWS, LANES), F32)] * 2,
        inputs=3,
        flops=6 * 2 * (8 * ROWS) ** 2 * LANES,
    )(queries, keys, stats)


def gelu_parts(inputs):
    normal_cdf = 0.5 * (1.0 + lax.erf(inputs * INV_ROOT_TWO))
    density = jnp.exp(-0.5 * inputs * inputs) * INV_ROOT_TAU
    return inputs * normal_cdf, normal_cdf + inputs * density


def on_device(frames, conv_weight, w_qkv, lengths, grad_out):
    index = lax.axis_index("tm")
    tap_base = (index // 32) * 32 + index % 4
    z_base = index % 32 - index % 4
    ends = jnp.cumsum(lengths).astype(jnp.int32)
    groups = 2
    width = w_qkv.shape[0]

    def scalars(first):
        return jnp.concatenate([jnp.stack([first, z_base]).astype(jnp.int32), ends])

    frames_g = frames.reshape(ROWS, groups, HD).transpose(1, 0, 2)
    frames_pad = with_halo(frames_g)
    taps = exchange_z(everyone(conv_weight[0]))
    frames_all = exchange_xy(everyone(frames_pad))
    conv = exchange_xy(conv_partial(True, scalars(tap_base), frames_all, taps))
    conv = jnp.sum(conv.astype(F32), axis=0)
    activated, slope = gelu_parts(conv)
    hidden = frames_g.astype(F32) + activated

    hidden_all = lax.all_gather(hidden.astype(BF), "head", axis=0, tiled=True).astype(F32)
    center = jnp.sum(hidden_all, axis=(0, 2)) / width
    square = jnp.sum(hidden_all * hidden_all, axis=(0, 2)) / width
    inv_std = lax.rsqrt(square - center * center + EPS)
    normed = ((hidden_all - center[:, None]) * inv_std[:, None]).astype(BF)
    unit = (hidden - center[:, None]) * inv_std[:, None]
    weights = w_qkv.reshape(16, HD, 3 * HD)
    normed_rows = normed.transpose(1, 0, 2).reshape(ROWS, width)
    projected = jnp.dot(normed_rows, w_qkv, preferred_element_type=F32).astype(BF)

    pos = index * ROWS + jnp.arange(ROWS, dtype=jnp.int32)
    seg = jnp.sum((pos[:, None] >= ends[None, :3]).astype(jnp.int32), axis=1)
    same = seg[:, None] == jnp.arange(8, dtype=jnp.int32)[None]
    q_mark = same.astype(BF)
    k_mark = jnp.where(same, 0.0, FAR).astype(BF)
    nil = jnp.zeros((ROWS, 8), BF)
    queries = jnp.concatenate([projected[:, :HD], q_mark, grad_out, nil], axis=1)
    keys = jnp.concatenate(
        [projected[:, HD : 2 * HD], k_mark, projected[:, 2 * HD :], nil], axis=1
    )
    queries_all = exchange_xy(everyone(queries))
    keys_all = exchange_z(everyone(keys))
    stats = exchange_xy(everyone(attention_stats(queries_all, keys_all)))
    od, dkv = attention_grads(queries_all, keys_all, stats)
    od = jnp.sum(exchange_xy(od).astype(F32), axis=0).astype(BF)
    dkv = jnp.sum(exchange_z(dkv).astype(F32), axis=0).astype(BF)
    attended = od[0].T
    grad_joined = jnp.concatenate([od[1].T, dkv[:, :HD], dkv[:, LANES : LANES + HD]], axis=1)

    share = jnp.einsum("tj,gcj->gtc", grad_joined, weights, preferred_element_type=F32)
    plain = jnp.sum(share, axis=(0, 2))
    along = jnp.sum(share * normed.astype(F32), axis=(0, 2))
    sums = jnp.stack([plain, along], axis=1)
    sums_high = sums.astype(BF)
    sums_low = (sums - sums_high.astype(F32)).astype(BF)
    sums = jnp.concatenate([sums_high, sums_low, jnp.zeros((ROWS, 4), BF)], axis=1)
    parts = jnp.concatenate(
        [share.astype(BF), jnp.broadcast_to(sums[None], (16, ROWS, 8))], axis=2
    ).reshape(8, groups, ROWS, LANES)
    parts = lax.all_to_all(parts, "head", 0, 0)
    parts = jnp.sum(parts.astype(F32), axis=0)
    feature = parts[:, :, :HD]
    plain = parts[0, :, HD] + parts[0, :, HD + 2]
    along = parts[0, :, HD + 1] + parts[0, :, HD + 3]
    hidden_grad = inv_std[:, None] * (
        feature - plain[:, None] / width - unit * (along[:, None] / width)
    )

    error = (slope * hidden_grad).astype(BF)
    error_all = exchange_xy(everyone(with_halo(error)))
    back = exchange_xy(conv_partial(False, scalars(36 - tap_base), error_all, taps))
    frame_grad = hidden_grad + jnp.sum(back.astype(F32), axis=0)
    frame_grad = frame_grad.astype(BF).transpose(1, 0, 2).reshape(ROWS, groups * HD)

    wide = lax.dot_general(
        normed_rows, grad_joined, (((0,), (0,)), ((), ())), preferred_element_type=F32
    ).astype(BF)
    slab = width // 64
    wide = wide.reshape(2, 8, 4, slab, 3 * HD).transpose(0, 2, 1, 3, 4)
    wide = exchange_xy(wide.reshape(8, 8, slab, 3 * HD))
    wide = jnp.sum(wide.astype(F32), axis=0).astype(BF)
    weight_grad = jnp.sum(exchange_z(wide).astype(F32), axis=0)
    return attended, frame_grad, weight_grad


def solution(mesh):
    return jax.shard_map(
        on_device,
        mesh=mesh,
        in_specs=(
            P("tm", "head"),
            P("tm", "head", None, None),
            P(None, "head"),
            P(),
            P("tm", "head"),
        ),
        out_specs=(P("tm", "head"), P("tm", "head"), P("tm", "head")),
        check_vma=False,
    )
```

```python
import functools
import math

import jax
import jax.numpy as jnp
from jax import lax
from jax.experimental import pallas as pl
from jax.experimental.pallas import tpu as pltpu
from jax.sharding import PartitionSpec as P

HD = 120
KERNEL = 64
HALF = KERNEL // 2
ROWS = 128
LANES = 128
SCALE = HD ** (-0.5)
SCALE2 = SCALE * math.log2(math.e)
FAR = -(2.0**100)
EPS = 1e-05
INV_ROOT_TWO = 0.7071067811865476
INV_ROOT_TAU = 0.3989422804014327

BF = jnp.bfloat16
F32 = jnp.float32

XY_GROUPS = [[y * 32 + z * 4 + x for y in range(2) for x in range(4)] for z in range(8)]
X_GROUPS = [[y * 32 + z * 4 + x for x in range(4)] for y in range(2) for z in range(8)]
Z_GROUPS = [[y * 32 + z * 4 + x for z in range(8)] for y in range(2) for x in range(4)]


def exchange_xy(parts):
    return lax.all_to_all(parts, "tm", 0, 0, axis_index_groups=XY_GROUPS)


def exchange_x(parts):
    return lax.all_to_all(parts, "tm", 0, 0, axis_index_groups=X_GROUPS)


def swap(array, bit):
    return lax.ppermute(array, "tm", [(i, i ^ bit) for i in range(64)])


def exchange_z(parts):
    return lax.all_to_all(parts, "tm", 0, 0, axis_index_groups=Z_GROUPS)


def everyone(array, count=8):
    return jnp.broadcast_to(array[None], (count,) + array.shape)


BITS = (32, 2, 1)
SLOTS = (0, 4, 2, 6, 1, 5, 3, 7)


def doubled(array):
    array = array[None]
    for bit in BITS:
        array = jnp.concatenate([array, swap(array, bit)], axis=0)
    return array


def halved(array):
    for bit in BITS[::-1]:
        half = array.shape[0] // 2
        array = array[:half] + swap(array[half:], bit)
    return array[0]


def vmem_call(body, out_shape, scratch=(), scalars=0, inputs=0, flops=0):
    return pl.pallas_call(
        body,
        out_shape=out_shape,
        in_specs=[pl.BlockSpec(memory_space=pltpu.SMEM)] * scalars
        + [pl.BlockSpec(memory_space=pltpu.VMEM)] * inputs,
        out_specs=jax.tree.map(lambda _: pl.BlockSpec(memory_space=pltpu.VMEM), out_shape),
        scratch_shapes=list(scratch),
        compiler_params=pltpu.CompilerParams(vmem_limit_bytes=48 * 1024 * 1024),
        cost_estimate=pl.CostEstimate(flops=flops, bytes_accessed=1 << 20, transcendentals=0),
    )


def bounds_of(pos, ends):
    low = jnp.zeros_like(pos)
    high = jnp.full_like(pos, ends[0])
    for u in range(3):
        inside = pos >= ends[u]
        low = jnp.where(inside, ends[u], low)
        high = jnp.where(inside, ends[u + 1], high)
    return low, high


PADDED = ROWS + KERNEL


def conv_body(sc_ref, x_ref, w_ref, out_ref):
    first = sc_ref[0]
    ends = [sc_ref[4 + u] for u in range(4)]
    row = lax.broadcasted_iota(jnp.int32, (ROWS, HD), 0)

    def block(b, carry):
        y = (b // 4) ^ sc_ref[2]
        x_at = b % 4
        pos = (y * 32 + sc_ref[1] + x_at) * ROWS + row
        low, high = bounds_of(pos, ends)
        source = pos - HALF + first
        keep = [
            ((source + 4 * s) >= low) & ((source + 4 * s) < high) for s in range(8)
        ]
        for g in range(2):
            x = x_ref[x_at, b // 4, g * PADDED : (g + 1) * PADDED].astype(F32)
            even = pltpu.roll(x, PADDED - first, 0)
            odd = pltpu.roll(x, PADDED - first - 4, 0)
            total = jnp.zeros((ROWS, HD), F32)
            for s in range(8):
                rolled = odd if s % 2 else even
                start = 8 * (s // 2)
                piece = jnp.where(keep[s], rolled[start : start + ROWS], 0.0).astype(BF)
                total += jnp.dot(piece, w_ref[s, g], preferred_element_type=F32)
            out_ref[y * 4 + x_at, g] = total.astype(BF)
        return carry

    lax.fori_loop(0, 8, block, 0)


def conv_partial(scalars, gathered, taps):
    return vmem_call(
        conv_body,
        jax.ShapeDtypeStruct((8, 2, ROWS, HD), BF),
        scalars=1,
        inputs=2,
        flops=8 * 2 * 8 * 2 * ROWS * HD * HD,
    )(scalars, gathered, taps)


def back_body(sc_ref, e_ref, w_ref, out_ref):
    ends = [sc_ref[1 + u] for u in range(4)]
    pos = sc_ref[0] * ROWS + lax.broadcasted_iota(jnp.int32, (ROWS, HD), 0)
    low, high = bounds_of(pos, ends)
    errors = [e_ref[g].astype(F32) for g in range(2)]
    totals = [jnp.zeros((ROWS, HD), F32) for g in range(2)]
    for rest in range(8):
        rolled = [pltpu.roll(e, PADDED - rest, 0) if rest else e for e in errors]
        for start in range(0, KERNEL + 1, 8):
            tap = KERNEL - start - rest
            if not 0 <= tap < KERNEL:
                continue
            source = pos + (HALF - tap)
            keep = (source >= low) & (source < high)
            y, z, x = tap // 32, tap % 32 // 4, tap % 4
            for g in range(2):
                piece = jnp.where(keep, rolled[g][start : start + ROWS], 0.0).astype(BF)
                totals[g] += lax.dot_general(
                    piece,
                    w_ref[y * 4 + x, z, g],
                    (((1,), (1,)), ((), ())),
                    preferred_element_type=F32,
                )
    for g in range(2):
        out_ref[g] = totals[g]


def conv_back(scalars, errors, taps):
    return vmem_call(
        back_body,
        jax.ShapeDtypeStruct((2, ROWS, HD), F32),
        scalars=1,
        inputs=2,
        flops=64 * 2 * 2 * ROWS * HD * HD,
    )(scalars, errors, taps)


def with_halo(rows):
    devices = 64
    up = [(i, i + 1) for i in range(devices - 1)]
    down = [(i + 1, i) for i in range(devices - 1)]
    before = lax.ppermute(rows[:, ROWS - HALF :], "tm", up)
    after = lax.ppermute(rows[:, :HALF], "tm", down)
    return jnp.concatenate([before, rows, after], axis=1)


CHUNK = 256


N = CHUNK // ROWS
ALL = 8 * ROWS
CONTRACT = (((1,), (1,)), ((), ()))


def upstream_rows(sc_ref, f_ref, d_ref):
    for i, e in enumerate(SLOTS):
        d_ref[i * ROWS : (i + 1) * ROWS] = f_ref[sc_ref[1] ^ (e % 4), e // 4, 2 * PADDED :]


def scored(c, q_ref, kv_ref, d_ref):
    keys = kv_ref[:, :, :LANES].reshape(ALL, LANES)
    values = kv_ref[:, :, LANES : LANES + HD].reshape(ALL, HD)
    q = q_ref[c * N : (c + 1) * N].reshape(CHUNK, LANES)
    d = d_ref[c * CHUNK : (c + 1) * CHUNK]
    scores = lax.dot_general(keys, q, CONTRACT, preferred_element_type=F32)
    dprobs = lax.dot_general(values, d, CONTRACT, preferred_element_type=F32)
    return keys, values, q, d, scores * SCALE2, dprobs


def stats_body(sc_ref, q_ref, kv_ref, f_ref, out_ref, d_ref):
    upstream_rows(sc_ref, f_ref, d_ref)
    for c in range(ALL // CHUNK):
        _, _, _, _, scores, dprobs = scored(c, q_ref, kv_ref, d_ref)
        peak = jnp.max(scores, axis=0, keepdims=True)
        weight = jnp.exp2(scores - peak)
        total = jnp.sum(weight, axis=0, keepdims=True)
        along = jnp.sum(weight * dprobs, axis=0, keepdims=True)
        rows = jnp.concatenate([peak, total, along, jnp.zeros((5, CHUNK), F32)], axis=0)
        for i in range(N):
            out_ref[sc_ref[0] ^ SLOTS[c * N + i]] = rows[:, i * ROWS : (i + 1) * ROWS]


def grads_body(
    sc_ref, q_ref, kv_ref, f_ref, stats_ref, od_ref, dkv_ref, d_ref, dk_ref, dv_ref
):
    upstream_rows(sc_ref, f_ref, d_ref)
    for c in range(ALL // CHUNK):
        stats = jnp.concatenate(
            [stats_ref[:, sc_ref[0] ^ SLOTS[c * N + i]] for i in range(N)], axis=2
        )
        peaks = stats[:, 0]
        top = jnp.max(peaks, axis=0, keepdims=True)
        factor = jnp.exp2(peaks - top)
        total = jnp.sum(stats[:, 1] * factor, axis=0, keepdims=True)
        delta = jnp.sum(stats[:, 2] * factor, axis=0, keepdims=True) / total
        lse = top + jnp.log2(total)
        keys, values, q, d, scores, dprobs = scored(c, q_ref, kv_ref, d_ref)
        probs = jnp.exp2(scores - lse)
        dscores = (probs * (dprobs - delta)).astype(BF)
        probs = probs.astype(BF)
        dv = jnp.dot(probs, d, preferred_element_type=F32)
        dk = jnp.dot(dscores, q, preferred_element_type=F32)
        if c == 0:
            dv_ref[...] = dv
            dk_ref[...] = dk
        else:
            dv_ref[...] += dv
            dk_ref[...] += dk
        inner = (((0,), (0,)), ((), ()))
        out_t = lax.dot_general(values, probs, inner, preferred_element_type=F32)
        dq_t = lax.dot_general(keys, dscores, inner, preferred_element_type=F32) * SCALE
        for i in range(N):
            od_ref[0, c * N + i] = out_t[:, i * ROWS : (i + 1) * ROWS].astype(BF)
            od_ref[1, c * N + i] = dq_t[:HD, i * ROWS : (i + 1) * ROWS].astype(BF)
    for i in range(8):
        piece = slice(i * ROWS, (i + 1) * ROWS)
        dkv_ref[i, :, :LANES] = (dk_ref[piece] * SCALE).astype(BF)
        dkv_ref[i, :, LANES : LANES + HD] = dv_ref[piece].astype(BF)
        dkv_ref[i, :, LANES + HD :] = jnp.zeros((ROWS, LANES - HD), BF)


def attention_stats(scalars, queries, keys, gathered):
    return vmem_call(
        stats_body,
        jax.ShapeDtypeStruct((8, 8, ROWS), F32),
        scratch=[pltpu.VMEM((ALL, HD), BF)],
        scalars=1,
        inputs=3,
        flops=2 * 2 * ALL * ALL * LANES,
    )(scalars, queries, keys, gathered)


def attention_grads(scalars, queries, keys, gathered, stats):
    return vmem_call(
        grads_body,
        (
            jax.ShapeDtypeStruct((2, 8, HD, ROWS), BF),
            jax.ShapeDtypeStruct((8, ROWS, 2 * LANES), BF),
        ),
        scratch=[
            pltpu.VMEM((ALL, HD), BF),
            pltpu.VMEM((ALL, LANES), F32),
            pltpu.VMEM((ALL, HD), F32),
        ],
        scalars=1,
        inputs=4,
        flops=6 * 2 * ALL * ALL * LANES,
    )(scalars, queries, keys, gathered, stats)


def gelu_parts(inputs):
    normal_cdf = 0.5 * (1.0 + lax.erf(inputs * INV_ROOT_TWO))
    density = jnp.exp(-0.5 * inputs * inputs) * INV_ROOT_TAU
    return inputs * normal_cdf, normal_cdf + inputs * density


def on_device(frames, conv_weight, w_qkv, lengths, grad_out):
    index = lax.axis_index("tm")
    y, x = index // 32, index % 4
    z_base = index % 32 - x
    place = y * 4 + x
    ends = jnp.cumsum(lengths).astype(jnp.int32)
    groups = 2
    width = w_qkv.shape[0]

    def scalars(*first):
        return jnp.concatenate([jnp.stack(first).astype(jnp.int32), ends])

    frames_g = frames.reshape(ROWS, groups, HD).transpose(1, 0, 2)
    frames_pad = with_halo(frames_g).reshape(groups * PADDED, HD)
    taps = exchange_z(everyone(conv_weight[0]))
    pair = jnp.concatenate([frames_pad, grad_out], axis=0)
    pair = jnp.stack([pair, swap(pair, 32)])
    gathered = exchange_x(everyone(pair, 4))
    conv = conv_partial(scalars(y * 32 + x, z_base, y, x), gathered, taps)
    conv = exchange_xy(conv)
    conv = jnp.sum(conv.astype(F32), axis=0)
    activated, slope = gelu_parts(conv)
    hidden = frames_g.astype(F32) + activated
    all_taps = lax.all_gather(taps, "tm", axis=0, axis_index_groups=XY_GROUPS)

    hidden_all = lax.all_gather(hidden.astype(BF), "head", axis=0, tiled=True).astype(F32)
    center = jnp.sum(hidden_all, axis=(0, 2)) / width
    square = jnp.sum(hidden_all * hidden_all, axis=(0, 2)) / width
    inv_std = lax.rsqrt(square - center * center + EPS)
    normed = ((hidden_all - center[:, None]) * inv_std[:, None]).astype(BF)
    unit = (hidden - center[:, None]) * inv_std[:, None]
    weights = w_qkv.reshape(16, HD, 3 * HD)
    normed_rows = normed.transpose(1, 0, 2).reshape(ROWS, width)
    projected = jnp.dot(normed_rows, w_qkv, preferred_element_type=F32).astype(BF)

    pos = index * ROWS + jnp.arange(ROWS, dtype=jnp.int32)
    seg = jnp.sum((pos[:, None] >= ends[None, :3]).astype(jnp.int32), axis=1)
    same = seg[:, None] == jnp.arange(8, dtype=jnp.int32)[None]
    q_mark = same.astype(BF)
    k_mark = jnp.where(same, 0.0, FAR).astype(BF)
    nil = jnp.zeros((ROWS, 8), BF)
    queries = jnp.concatenate([projected[:, :HD], q_mark], axis=1)
    keys = jnp.concatenate(
        [projected[:, HD : 2 * HD], k_mark, projected[:, 2 * HD :], nil], axis=1
    )
    keys_all = exchange_z(everyone(keys))
    queries_all = doubled(queries)
    where = scalars(place, x)
    stats = attention_stats(where, queries_all, keys_all, gathered)
    stats = exchange_xy(everyone(stats))
    od, dkv = attention_grads(where, queries_all, keys_all, gathered, stats)
    dkv = jnp.sum(exchange_z(dkv).astype(F32), axis=0).astype(BF)
    grad_q = halved(od[1])
    attended = halved(od[0]).T
    grad_joined = jnp.concatenate([grad_q.T, dkv[:, :HD], dkv[:, LANES : LANES + HD]], axis=1)

    share = jnp.einsum("tj,gcj->gtc", grad_joined, weights, preferred_element_type=F32)
    plain = jnp.sum(share, axis=(0, 2))
    along = jnp.sum(share * normed.astype(F32), axis=(0, 2))
    sums = jnp.stack([plain, along], axis=1)
    sums_high = sums.astype(BF)
    sums_low = (sums - sums_high.astype(F32)).astype(BF)
    sums = jnp.concatenate([sums_high, sums_low, jnp.zeros((ROWS, 4), BF)], axis=1)
    parts = jnp.concatenate(
        [share.astype(BF), jnp.broadcast_to(sums[None], (16, ROWS, 8))], axis=2
    ).reshape(8, groups, ROWS, LANES)
    parts = lax.all_to_all(parts, "head", 0, 0)
    parts = jnp.sum(parts.astype(F32), axis=0)
    feature = parts[:, :, :HD]
    plain = parts[0, :, HD] + parts[0, :, HD + 2]
    along = parts[0, :, HD + 1] + parts[0, :, HD + 3]
    hidden_grad = inv_std[:, None] * (
        feature - plain[:, None] / width - unit * (along[:, None] / width)
    )

    error = (slope * hidden_grad).astype(BF)
    back = conv_back(scalars(index), with_halo(error), all_taps)
    frame_grad = hidden_grad + back
    frame_grad = frame_grad.astype(BF).transpose(1, 0, 2).reshape(ROWS, groups * HD)

    wide = lax.dot_general(
        normed_rows, grad_joined, (((0,), (0,)), ((), ())), preferred_element_type=F32
    ).astype(BF)
    slab = width // 64
    wide = wide.reshape(2, 8, 4, slab, 3 * HD).transpose(0, 2, 1, 3, 4)
    wide = exchange_xy(wide.reshape(8, 8, slab, 3 * HD))
    wide = jnp.sum(wide.astype(F32), axis=0).astype(BF)
    weight_grad = jnp.sum(exchange_z(wide).astype(F32), axis=0)
    return attended, frame_grad, weight_grad


def solution(mesh):
    return jax.shard_map(
        on_device,
        mesh=mesh,
        in_specs=(
            P("tm", "head"),
            P("tm", "head", None, None),
            P(None, "head"),
            P(),
            P("tm", "head"),
        ),
        out_specs=(P("tm", "head"), P("tm", "head"), P("tm", "head")),
        check_vma=False,
    )
```

```python
import functools
import math

import jax
import jax.numpy as jnp
from jax import lax
from jax.experimental import pallas as pl
from jax.experimental.pallas import tpu as pltpu
from jax.sharding import PartitionSpec as P

HD = 120
KERNEL = 64
HALF = KERNEL // 2
ROWS = 128
LANES = 128
SCALE = HD ** (-0.5)
SCALE2 = SCALE * math.log2(math.e)
FAR = -(2.0**100)
EPS = 1e-05
INV_ROOT_TWO = 0.7071067811865476
INV_ROOT_TAU = 0.3989422804014327

BF = jnp.bfloat16
F32 = jnp.float32

XY_GROUPS = [[y * 32 + z * 4 + x for y in range(2) for x in range(4)] for z in range(8)]
X_GROUPS = [[y * 32 + z * 4 + x for x in range(4)] for y in range(2) for z in range(8)]
Z_GROUPS = [[y * 32 + z * 4 + x for z in range(8)] for y in range(2) for x in range(4)]


def exchange_xy(parts):
    return lax.all_to_all(parts, "tm", 0, 0, axis_index_groups=XY_GROUPS)


def exchange_x(parts):
    return lax.all_to_all(parts, "tm", 0, 0, axis_index_groups=X_GROUPS)


def swap(array, bit):
    return lax.ppermute(array, "tm", [(i, i ^ bit) for i in range(64)])


def exchange_z(parts):
    return lax.all_to_all(parts, "tm", 0, 0, axis_index_groups=Z_GROUPS)


def everyone(array, count=8):
    return jnp.broadcast_to(array[None], (count,) + array.shape)


def after(array, earlier):
    return array + 0 * earlier.reshape(-1)[0].astype(array.dtype)


BITS = (32, 2, 1)
SLOTS = (0, 4, 2, 6, 1, 5, 3, 7)


def doubled(array):
    array = array[None]
    for bit in BITS:
        array = jnp.concatenate([array, swap(array, bit)], axis=0)
    return array


def halved(array):
    for bit in BITS[::-1]:
        half = array.shape[0] // 2
        array = array[:half] + swap(array[half:], bit)
    return array[0]


def vmem_call(body, out_shape, scratch=(), scalars=0, inputs=0, flops=0):
    return pl.pallas_call(
        body,
        out_shape=out_shape,
        in_specs=[pl.BlockSpec(memory_space=pltpu.SMEM)] * scalars
        + [pl.BlockSpec(memory_space=pltpu.VMEM)] * inputs,
        out_specs=jax.tree.map(lambda _: pl.BlockSpec(memory_space=pltpu.VMEM), out_shape),
        scratch_shapes=list(scratch),
        compiler_params=pltpu.CompilerParams(vmem_limit_bytes=48 * 1024 * 1024),
        cost_estimate=pl.CostEstimate(flops=flops, bytes_accessed=1 << 20, transcendentals=0),
    )


def bounds_of(pos, ends):
    low = jnp.zeros_like(pos)
    high = jnp.full_like(pos, ends[0])
    for u in range(3):
        inside = pos >= ends[u]
        low = jnp.where(inside, ends[u], low)
        high = jnp.where(inside, ends[u + 1], high)
    return low, high


PADDED = ROWS + KERNEL
TAPS = KERNEL // 2
SPAN = ROWS + TAPS


def conv_body(forward, sc_ref, x_ref, w_ref, own_ref, other_ref):
    ends = [sc_ref[2 + u] for u in range(4)]
    first = TAPS * (sc_ref[0] if forward else 1 - sc_ref[0])
    row = lax.broadcasted_iota(jnp.int32, (ROWS, HD), 0)
    for b in range(2):
        shard = sc_ref[1] if b == 0 else sc_ref[1] ^ 32
        pos = shard * ROWS + row
        low, high = bounds_of(pos, ends)
        source = pos + (first - HALF)
        spans = [
            x_ref[b, g, pl.ds(pl.multiple_of(first, TAPS), SPAN)].astype(F32) for g in range(2)
        ]
        totals = [jnp.zeros((ROWS, HD), F32) for g in range(2)]
        for rest in range(8):
            rolled = [pltpu.roll(e, SPAN - rest, 0) if rest else e for e in spans]
            for start in range(0, TAPS + 1, 8):
                tap = start + rest if forward else TAPS - start - rest
                if not 0 <= tap < TAPS:
                    continue
                at = source + (start + rest)
                keep = (at >= low) & (at < high)
                for g in range(2):
                    piece = jnp.where(keep, rolled[g][start : start + ROWS], 0.0).astype(BF)
                    totals[g] += lax.dot_general(
                        piece,
                        w_ref[tap % 4, tap // 4, g],
                        (((1,), (0 if forward else 1,)), ((), ())),
                        preferred_element_type=F32,
                    )
        for g in range(2):
            if b == 0:
                own_ref[g] = totals[g]
            else:
                other_ref[g] = totals[g].astype(BF)


def convolved(forward, scalars, rows, taps):
    padded = with_halo(rows)
    pair = jnp.stack([padded, swap(padded, 32)])
    own, other = vmem_call(
        functools.partial(conv_body, forward),
        (
            jax.ShapeDtypeStruct((2, ROWS, HD), F32),
            jax.ShapeDtypeStruct((2, ROWS, HD), BF),
        ),
        scalars=1,
        inputs=2,
        flops=32 * 2 * 2 * 2 * ROWS * HD * HD,
    )(scalars, pair, taps)
    return own + swap(other, 32).astype(F32)


def with_halo(rows):
    devices = 64
    up = [(i, i + 1) for i in range(devices - 1)]
    down = [(i + 1, i) for i in range(devices - 1)]
    before = lax.ppermute(rows[:, ROWS - HALF :], "tm", up)
    after = lax.ppermute(rows[:, :HALF], "tm", down)
    return jnp.concatenate([before, rows, after], axis=1)


CHUNK = 256


N = CHUNK // ROWS
ALL = 8 * ROWS
CONTRACT = (((1,), (1,)), ((), ()))


def scored(c, q_ref, kv_ref, d_ref):
    keys = kv_ref[:, :, :LANES].reshape(ALL, LANES)
    values = kv_ref[:, :, LANES : LANES + HD].reshape(ALL, HD)
    q = q_ref[c * N : (c + 1) * N].reshape(CHUNK, LANES)
    d = d_ref[c * N : (c + 1) * N].reshape(CHUNK, HD)
    scores = lax.dot_general(keys, q, CONTRACT, preferred_element_type=F32)
    dprobs = lax.dot_general(values, d, CONTRACT, preferred_element_type=F32)
    return keys, values, q, d, scores * SCALE2, dprobs


def stats_body(sc_ref, q_ref, kv_ref, d_ref, out_ref):
    for c in range(ALL // CHUNK):
        _, _, _, _, scores, dprobs = scored(c, q_ref, kv_ref, d_ref)
        peak = jnp.max(scores, axis=0, keepdims=True)
        weight = jnp.exp2(scores - peak)
        total = jnp.sum(weight, axis=0, keepdims=True)
        along = jnp.sum(weight * dprobs, axis=0, keepdims=True)
        for i in range(N):
            columns = slice(i * ROWS, (i + 1) * ROWS)
            shard = pl.ds(sc_ref[0] ^ SLOTS[c * N + i], 1)
            for j, value in enumerate((peak, total, along)):
                out_ref[j, shard] = value[:, columns]


def grads_body(sc_ref, q_ref, kv_ref, d_ref, stats_ref, od_ref, dkv_ref, dk_ref, dv_ref):
    for c in range(ALL // CHUNK):
        peaks, totals, alongs = (
            jnp.concatenate(
                [stats_ref[:, j, pl.ds(sc_ref[0] ^ SLOTS[c * N + i], 1)] for i in range(N)],
                axis=2,
            )
            for j in range(3)
        )
        top = jnp.max(peaks, axis=0)
        factor = jnp.exp2(peaks - top[None])
        total = jnp.sum(totals * factor, axis=0)
        delta = jnp.sum(alongs * factor, axis=0) / total
        lse = top + jnp.log2(total)
        keys, values, q, d, scores, dprobs = scored(c, q_ref, kv_ref, d_ref)
        probs = jnp.exp2(scores - lse)
        dscores = (probs * (dprobs - delta)).astype(BF)
        probs = probs.astype(BF)
        dv = jnp.dot(probs, d, preferred_element_type=F32)
        dk = jnp.dot(dscores, q, preferred_element_type=F32)
        if c == 0:
            dv_ref[...] = dv
            dk_ref[...] = dk
        else:
            dv_ref[...] += dv
            dk_ref[...] += dk
        inner = (((0,), (0,)), ((), ()))
        out_t = lax.dot_general(values, probs, inner, preferred_element_type=F32)
        dq_t = lax.dot_general(keys, dscores, inner, preferred_element_type=F32) * SCALE
        for i in range(N):
            od_ref[0, c * N + i] = out_t[:, i * ROWS : (i + 1) * ROWS].astype(BF)
            od_ref[1, c * N + i] = dq_t[:HD, i * ROWS : (i + 1) * ROWS].astype(BF)
    for i in range(8):
        piece = slice(i * ROWS, (i + 1) * ROWS)
        dkv_ref[i, :, :LANES] = (dk_ref[piece] * SCALE).astype(BF)
        dkv_ref[i, :, LANES : LANES + HD] = dv_ref[piece].astype(BF)
        dkv_ref[i, :, LANES + HD :] = jnp.zeros((ROWS, LANES - HD), BF)


def attention_stats(scalars, queries, keys, upstream):
    return vmem_call(
        stats_body,
        jax.ShapeDtypeStruct((3, 8, ROWS), F32),
        scalars=1,
        inputs=3,
        flops=2 * 2 * ALL * ALL * LANES,
    )(scalars, queries, keys, upstream)


def attention_grads(scalars, queries, keys, upstream, stats):
    return vmem_call(
        grads_body,
        (
            jax.ShapeDtypeStruct((2, 8, HD, ROWS), BF),
            jax.ShapeDtypeStruct((8, ROWS, 2 * LANES), BF),
        ),
        scratch=[
            pltpu.VMEM((ALL, LANES), F32),
            pltpu.VMEM((ALL, HD), F32),
        ],
        scalars=1,
        inputs=4,
        flops=6 * 2 * ALL * ALL * LANES,
    )(scalars, queries, keys, upstream, stats)


def gelu_parts(inputs):
    normal_cdf = 0.5 * (1.0 + lax.erf(inputs * INV_ROOT_TWO))
    density = jnp.exp(-0.5 * inputs * inputs) * INV_ROOT_TAU
    return inputs * normal_cdf, normal_cdf + inputs * density


def on_device(frames, conv_weight, w_qkv, lengths, grad_out):
    index = lax.axis_index("tm")
    y, x = index // 32, index % 4
    ends = jnp.cumsum(lengths).astype(jnp.int32)
    groups = 2
    width = w_qkv.shape[0]

    def scalars(*first):
        return jnp.concatenate([jnp.stack(first).astype(jnp.int32), ends])

    frames_g = frames.reshape(ROWS, groups, HD).transpose(1, 0, 2)
    taps = exchange_x(everyone(exchange_z(everyone(conv_weight[0])), 4))
    where = scalars(y, index)
    conv = convolved(True, where, frames_g, taps)
    upstream = doubled(grad_out)
    activated, slope = gelu_parts(conv)
    hidden = frames_g.astype(F32) + activated

    hidden_all = lax.all_gather(hidden.astype(BF), "head", axis=0, tiled=True).astype(F32)
    center = jnp.sum(hidden_all, axis=(0, 2)) / width
    square = jnp.sum(hidden_all * hidden_all, axis=(0, 2)) / width
    inv_std = lax.rsqrt(square - center * center + EPS)
    normed = ((hidden_all - center[:, None]) * inv_std[:, None]).astype(BF)
    unit = (hidden - center[:, None]) * inv_std[:, None]
    weights = w_qkv.reshape(16, HD, 3 * HD)
    normed_rows = normed.transpose(1, 0, 2).reshape(ROWS, width)
    projected = jnp.dot(normed_rows, w_qkv, preferred_element_type=F32).astype(BF)

    pos = index * ROWS + jnp.arange(ROWS, dtype=jnp.int32)
    seg = jnp.sum((pos[:, None] >= ends[None, :3]).astype(jnp.int32), axis=1)
    same = seg[:, None] == jnp.arange(8, dtype=jnp.int32)[None]
    q_mark = same.astype(BF)
    k_mark = jnp.where(same, 0.0, FAR).astype(BF)
    nil = jnp.zeros((ROWS, 8), BF)
    queries = jnp.concatenate([projected[:, :HD], q_mark], axis=1)
    keys = jnp.concatenate(
        [projected[:, HD : 2 * HD], k_mark, projected[:, 2 * HD :], nil], axis=1
    )
    keys_all = exchange_z(everyone(keys))
    queries_all = doubled(queries)
    order = scalars(y * 4 + x)
    stats = attention_stats(order, queries_all, keys_all, upstream)
    stats = exchange_xy(everyone(stats))
    od, dkv = attention_grads(order, queries_all, keys_all, upstream, stats)
    dkv = jnp.sum(exchange_z(dkv).astype(F32), axis=0).astype(BF)
    grad_q = halved(od[1])
    attended = halved(after(od[0], grad_q)).T
    grad_joined = jnp.concatenate([grad_q.T, dkv[:, :HD], dkv[:, LANES : LANES + HD]], axis=1)

    share = jnp.einsum("tj,gcj->gtc", grad_joined, weights, preferred_element_type=F32)
    plain = jnp.sum(share, axis=(0, 2))
    along = jnp.sum(share * normed.astype(F32), axis=(0, 2))
    sums = jnp.stack([plain, along], axis=1)
    sums_high = sums.astype(BF)
    sums_low = (sums - sums_high.astype(F32)).astype(BF)
    sums = jnp.concatenate([sums_high, sums_low, jnp.zeros((ROWS, 4), BF)], axis=1)
    parts = jnp.concatenate(
        [share.astype(BF), jnp.broadcast_to(sums[None], (16, ROWS, 8))], axis=2
    ).reshape(8, groups, ROWS, LANES)
    parts = lax.all_to_all(parts, "head", 0, 0)
    parts = jnp.sum(parts.astype(F32), axis=0)
    feature = parts[:, :, :HD]
    plain = parts[0, :, HD] + parts[0, :, HD + 2]
    along = parts[0, :, HD + 1] + parts[0, :, HD + 3]
    hidden_grad = inv_std[:, None] * (
        feature - plain[:, None] / width - unit * (along[:, None] / width)
    )

    error = (slope * hidden_grad).astype(BF)
    frame_grad = hidden_grad + convolved(False, where, error, taps)
    frame_grad = frame_grad.astype(BF).transpose(1, 0, 2).reshape(ROWS, groups * HD)

    wide = lax.dot_general(
        normed_rows, grad_joined, (((0,), (0,)), ((), ())), preferred_element_type=F32
    ).astype(BF)
    slab = width // 64
    wide = wide.reshape(2, 8, 4, slab, 3 * HD).transpose(0, 2, 1, 3, 4)
    wide = exchange_xy(wide.reshape(8, 8, slab, 3 * HD))
    wide = jnp.sum(wide.astype(F32), axis=0).astype(BF)
    weight_grad = jnp.sum(exchange_z(wide).astype(F32), axis=0)
    return attended, frame_grad, weight_grad


def solution(mesh):
    return jax.shard_map(
        on_device,
        mesh=mesh,
        in_specs=(
            P("tm", "head"),
            P("tm", "head", None, None),
            P(None, "head"),
            P(),
            P("tm", "head"),
        ),
        out_specs=(P("tm", "head"), P("tm", "head"), P("tm", "head")),
        check_vma=False,
    )
```

```python
import functools
import math

import jax
import jax.numpy as jnp
from jax import lax
from jax.experimental import pallas as pl
from jax.experimental.pallas import tpu as pltpu
from jax.sharding import PartitionSpec as P

HD = 120
KERNEL = 64
HALF = KERNEL // 2
ROWS = 128
LANES = 128
SCALE = HD ** (-0.5)
SCALE2 = SCALE * math.log2(math.e)
FAR = -(2.0**100)
EPS = 1e-05
INV_ROOT_TWO = 0.7071067811865476
INV_ROOT_TAU = 0.3989422804014327

BF = jnp.bfloat16
F32 = jnp.float32

XY_GROUPS = [[y * 32 + z * 4 + x for y in range(2) for x in range(4)] for z in range(8)]
X_GROUPS = [[y * 32 + z * 4 + x for x in range(4)] for y in range(2) for z in range(8)]
Z_GROUPS = [[y * 32 + z * 4 + x for z in range(8)] for y in range(2) for x in range(4)]


def exchange_xy(parts):
    return lax.all_to_all(parts, "tm", 0, 0, axis_index_groups=XY_GROUPS)


def exchange_x(parts):
    return lax.all_to_all(parts, "tm", 0, 0, axis_index_groups=X_GROUPS)


def swap(array, bit):
    return lax.ppermute(array, "tm", [(i, i ^ bit) for i in range(64)])


def exchange_z(parts):
    return lax.all_to_all(parts, "tm", 0, 0, axis_index_groups=Z_GROUPS)


def everyone(array, count=8):
    return jnp.broadcast_to(array[None], (count,) + array.shape)


def after(array, earlier):
    return array + 0 * earlier.reshape(-1)[0].astype(array.dtype)


BITS = (32, 2, 1)
SLOTS = (0, 4, 2, 6, 1, 5, 3, 7)


def doubled(array):
    array = array[None]
    for bit in BITS:
        array = jnp.concatenate([array, swap(array, bit)], axis=0)
    return array


def halved(array):
    for bit in BITS[::-1]:
        half = array.shape[0] // 2
        array = array[:half] + swap(array[half:], bit)
    return array[0]


def vmem_call(body, out_shape, scratch=(), scalars=0, inputs=0, flops=0):
    return pl.pallas_call(
        body,
        out_shape=out_shape,
        in_specs=[pl.BlockSpec(memory_space=pltpu.SMEM)] * scalars
        + [pl.BlockSpec(memory_space=pltpu.VMEM)] * inputs,
        out_specs=jax.tree.map(lambda _: pl.BlockSpec(memory_space=pltpu.VMEM), out_shape),
        scratch_shapes=list(scratch),
        compiler_params=pltpu.CompilerParams(vmem_limit_bytes=48 * 1024 * 1024),
        cost_estimate=pl.CostEstimate(flops=flops, bytes_accessed=1 << 20, transcendentals=0),
    )


def bounds_of(pos, ends):
    low = jnp.zeros_like(pos)
    high = jnp.full_like(pos, ends[0])
    for u in range(3):
        inside = pos >= ends[u]
        low = jnp.where(inside, ends[u], low)
        high = jnp.where(inside, ends[u + 1], high)
    return low, high


PADDED = ROWS + KERNEL
TAPS = KERNEL // 2
SPAN = ROWS + TAPS


def conv_body(forward, sc_ref, x_ref, w_ref, own_ref, other_ref):
    ends = [sc_ref[2 + u] for u in range(4)]
    first = TAPS * (sc_ref[0] if forward else 1 - sc_ref[0])
    row = lax.broadcasted_iota(jnp.int32, (ROWS, HD), 0)
    for b in range(2):
        shard = sc_ref[1] if b == 0 else sc_ref[1] ^ 32
        pos = shard * ROWS + row
        low, high = bounds_of(pos, ends)
        source = pos + (first - HALF)
        spans = [
            x_ref[b, g, pl.ds(pl.multiple_of(first, TAPS), SPAN)].astype(F32) for g in range(2)
        ]
        totals = [jnp.zeros((ROWS, HD), F32) for g in range(2)]
        for rest in range(8):
            rolled = [pltpu.roll(e, SPAN - rest, 0) if rest else e for e in spans]
            for start in range(0, TAPS + 1, 8):
                tap = start + rest if forward else TAPS - start - rest
                if not 0 <= tap < TAPS:
                    continue
                at = source + (start + rest)
                keep = (at >= low) & (at < high)
                for g in range(2):
                    piece = jnp.where(keep, rolled[g][start : start + ROWS], 0.0).astype(BF)
                    totals[g] += lax.dot_general(
                        piece,
                        w_ref[tap % 4, tap // 4, g],
                        (((1,), (0 if forward else 1,)), ((), ())),
                        preferred_element_type=F32,
                    )
        for g in range(2):
            if b == 0:
                own_ref[g] = totals[g]
            else:
                other_ref[g] = totals[g].astype(BF)


def paired(padded):
    return jnp.stack([padded, swap(padded, 32)])


def convolved(forward, scalars, pair, taps):
    own, other = vmem_call(
        functools.partial(conv_body, forward),
        (
            jax.ShapeDtypeStruct((2, ROWS, HD), F32),
            jax.ShapeDtypeStruct((2, ROWS, HD), BF),
        ),
        scalars=1,
        inputs=2,
        flops=32 * 2 * 2 * 2 * ROWS * HD * HD,
    )(scalars, pair, taps)
    return own + swap(other, 32).astype(F32)


def with_halo(rows):
    devices = 64
    up = [(i, i + 1) for i in range(devices - 1)]
    down = [(i + 1, i) for i in range(devices - 1)]
    before = lax.ppermute(rows[:, ROWS - HALF :], "tm", up)
    after = lax.ppermute(rows[:, :HALF], "tm", down)
    return jnp.concatenate([before, rows, after], axis=1)


CHUNK = 256


N = CHUNK // ROWS
ALL = 8 * ROWS
CONTRACT = (((1,), (1,)), ((), ()))


def scored(c, q_ref, kv_ref, d_ref):
    keys = kv_ref[:, :, :LANES].reshape(ALL, LANES)
    values = kv_ref[:, :, LANES : LANES + HD].reshape(ALL, HD)
    q = q_ref[c * N : (c + 1) * N].reshape(CHUNK, LANES)
    d = d_ref[c * N : (c + 1) * N].reshape(CHUNK, HD)
    scores = lax.dot_general(keys, q, CONTRACT, preferred_element_type=F32)
    dprobs = lax.dot_general(values, d, CONTRACT, preferred_element_type=F32)
    return keys, values, q, d, scores * SCALE2, dprobs


def stats_body(sc_ref, q_ref, kv_ref, d_ref, out_ref):
    for c in range(ALL // CHUNK):
        _, _, _, _, scores, dprobs = scored(c, q_ref, kv_ref, d_ref)
        peak = jnp.max(scores, axis=0, keepdims=True)
        weight = jnp.exp2(scores - peak)
        total = jnp.sum(weight, axis=0, keepdims=True)
        along = jnp.sum(weight * dprobs, axis=0, keepdims=True)
        for i in range(N):
            columns = slice(i * ROWS, (i + 1) * ROWS)
            shard = pl.ds(sc_ref[0] ^ SLOTS[c * N + i], 1)
            for j, value in enumerate((peak, total, along)):
                out_ref[j, shard] = value[:, columns]


def grads_body(sc_ref, q_ref, kv_ref, d_ref, stats_ref, od_ref, dkv_ref, dk_ref, dv_ref):
    for c in range(ALL // CHUNK):
        peaks, totals, alongs = (
            jnp.concatenate(
                [stats_ref[:, j, pl.ds(sc_ref[0] ^ SLOTS[c * N + i], 1)] for i in range(N)],
                axis=2,
            )
            for j in range(3)
        )
        top = jnp.max(peaks, axis=0)
        factor = jnp.exp2(peaks - top[None])
        total = jnp.sum(totals * factor, axis=0)
        delta = jnp.sum(alongs * factor, axis=0) / total
        lse = top + jnp.log2(total)
        keys, values, q, d, scores, dprobs = scored(c, q_ref, kv_ref, d_ref)
        probs = jnp.exp2(scores - lse)
        dscores = (probs * (dprobs - delta)).astype(BF)
        probs = probs.astype(BF)
        dv = jnp.dot(probs, d, preferred_element_type=F32)
        dk = jnp.dot(dscores, q, preferred_element_type=F32)
        if c == 0:
            dv_ref[...] = dv
            dk_ref[...] = dk
        else:
            dv_ref[...] += dv
            dk_ref[...] += dk
        inner = (((0,), (0,)), ((), ()))
        out_t = lax.dot_general(values, probs, inner, preferred_element_type=F32)
        dq_t = lax.dot_general(keys, dscores, inner, preferred_element_type=F32) * SCALE
        for i in range(N):
            od_ref[0, c * N + i] = out_t[:, i * ROWS : (i + 1) * ROWS].astype(BF)
            od_ref[1, c * N + i] = dq_t[:HD, i * ROWS : (i + 1) * ROWS].astype(BF)
    for i in range(8):
        piece = slice(i * ROWS, (i + 1) * ROWS)
        dkv_ref[i, :, :LANES] = (dk_ref[piece] * SCALE).astype(BF)
        dkv_ref[i, :, LANES : LANES + HD] = dv_ref[piece].astype(BF)
        dkv_ref[i, :, LANES + HD :] = jnp.zeros((ROWS, LANES - HD), BF)


def attention_stats(scalars, queries, keys, upstream):
    return vmem_call(
        stats_body,
        jax.ShapeDtypeStruct((3, 8, ROWS), F32),
        scalars=1,
        inputs=3,
        flops=2 * 2 * ALL * ALL * LANES,
    )(scalars, queries, keys, upstream)


def attention_grads(scalars, queries, keys, upstream, stats):
    return vmem_call(
        grads_body,
        (
            jax.ShapeDtypeStruct((2, 8, HD, ROWS), BF),
            jax.ShapeDtypeStruct((8, ROWS, 2 * LANES), BF),
        ),
        scratch=[
            pltpu.VMEM((ALL, LANES), F32),
            pltpu.VMEM((ALL, HD), F32),
        ],
        scalars=1,
        inputs=4,
        flops=6 * 2 * ALL * ALL * LANES,
    )(scalars, queries, keys, upstream, stats)


GROUPS = 16
SLAB = 32


def share_body(dq_ref, dkv_ref, normed_ref, w_ref, parts_ref, grad_ref):
    dkv = dkv_ref[0].astype(F32)
    for i in range(1, 8):
        dkv += dkv_ref[i].astype(F32)
    grad_ref[:, :HD] = dq_ref[...].astype(F32).T.astype(BF)
    grad_ref[:, HD : 2 * HD] = dkv[:, :HD].astype(BF)
    grad_ref[:, 2 * HD :] = dkv[:, LANES : LANES + HD].astype(BF)
    grad = grad_ref[...]
    plain = jnp.zeros((ROWS, HD), F32)
    along = jnp.zeros((ROWS, HD), F32)
    for g in range(GROUPS):
        share = lax.dot_general(
            grad, w_ref[g * HD : (g + 1) * HD], CONTRACT, preferred_element_type=F32
        )
        plain += share
        along += share * normed_ref[g].astype(F32)
        parts_ref[g, :, :HD] = share.astype(BF)
    plain = jnp.sum(plain, axis=1, keepdims=True)
    along = jnp.sum(along, axis=1, keepdims=True)
    lane = lax.broadcasted_iota(jnp.int32, (ROWS, LANES - HD), 1)
    plain_high = plain.astype(BF).astype(F32)
    along_high = along.astype(BF).astype(F32)
    sums = jnp.where(lane == 0, plain_high, 0.0)
    sums = jnp.where(lane == 1, along_high, sums)
    sums = jnp.where(lane == 2, plain - plain_high, sums)
    sums = jnp.where(lane == 3, along - along_high, sums).astype(BF)
    for g in range(GROUPS):
        parts_ref[g, :, HD:] = sums


def shares(dq, dkv, normed, w_qkv):
    return vmem_call(
        share_body,
        (
            jax.ShapeDtypeStruct((GROUPS, ROWS, LANES), BF),
            jax.ShapeDtypeStruct((ROWS, 3 * HD), BF),
        ),
        inputs=4,
        flops=2 * ROWS * GROUPS * HD * 3 * HD,
    )(dq, dkv, normed, w_qkv)


def slabs_body(normed_ref, grad_ref, out_ref):
    slab = HD // 4
    grad = grad_ref[...]
    for g in range(GROUPS):
        wide = lax.dot_general(
            normed_ref[g], grad, (((0,), (0,)), ((), ())), preferred_element_type=F32
        )
        for x in range(4):
            at, row = g // 8 * 4 + x, g % 8 * SLAB
            out_ref[at, row : row + slab] = wide[x * slab : (x + 1) * slab].astype(BF)
            out_ref[at, row + slab : row + SLAB] = jnp.zeros((SLAB - slab, 3 * HD), BF)


def slabs(normed, grad):
    return vmem_call(
        slabs_body,
        jax.ShapeDtypeStruct((8, 8 * SLAB, 3 * HD), BF),
        inputs=2,
        flops=2 * ROWS * GROUPS * HD * 3 * HD,
    )(normed, grad)


def gelu_parts(inputs):
    normal_cdf = 0.5 * (1.0 + lax.erf(inputs * INV_ROOT_TWO))
    density = jnp.exp(-0.5 * inputs * inputs) * INV_ROOT_TAU
    return inputs * normal_cdf, normal_cdf + inputs * density


def on_device(frames, conv_weight, w_qkv, lengths, grad_out):
    index = lax.axis_index("tm")
    y, x = index // 32, index % 4
    ends = jnp.cumsum(lengths).astype(jnp.int32)
    groups = 2
    width = w_qkv.shape[0]

    def scalars(*first):
        return jnp.concatenate([jnp.stack(first).astype(jnp.int32), ends])

    frames_g = frames.reshape(ROWS, groups, HD).transpose(1, 0, 2)
    pair = paired(with_halo(frames_g))
    taps = exchange_z(everyone(conv_weight[0]))
    taps = exchange_x(everyone(after(taps, pair), 4))
    where = scalars(y, index)
    conv = convolved(True, where, pair, taps)
    upstream = doubled(grad_out)
    activated, slope = gelu_parts(conv)
    hidden = frames_g.astype(F32) + activated

    hidden_all = lax.all_gather(
        after(hidden.astype(BF), upstream), "head", axis=0, tiled=True
    ).astype(F32)
    center = jnp.sum(hidden_all, axis=(0, 2)) / width
    square = jnp.sum(hidden_all * hidden_all, axis=(0, 2)) / width
    inv_std = lax.rsqrt(square - center * center + EPS)
    normed = ((hidden_all - center[:, None]) * inv_std[:, None]).astype(BF)
    unit = (hidden - center[:, None]) * inv_std[:, None]
    normed_rows = normed.transpose(1, 0, 2).reshape(ROWS, width)
    projected = jnp.dot(normed_rows, w_qkv, preferred_element_type=F32).astype(BF)

    pos = index * ROWS + jnp.arange(ROWS, dtype=jnp.int32)
    seg = jnp.sum((pos[:, None] >= ends[None, :3]).astype(jnp.int32), axis=1)
    same = seg[:, None] == jnp.arange(8, dtype=jnp.int32)[None]
    q_mark = same.astype(BF)
    k_mark = jnp.where(same, 0.0, FAR).astype(BF)
    nil = jnp.zeros((ROWS, 8), BF)
    queries = jnp.concatenate([projected[:, :HD], q_mark], axis=1)
    keys = jnp.concatenate(
        [projected[:, HD : 2 * HD], k_mark, projected[:, 2 * HD :], nil], axis=1
    )
    keys_all = exchange_z(everyone(keys))
    queries_all = doubled(queries)
    order = scalars(y * 4 + x)
    stats = attention_stats(order, queries_all, keys_all, upstream)
    stats = exchange_xy(everyone(stats))
    od, dkv = attention_grads(order, queries_all, keys_all, upstream, stats)
    dkv = exchange_z(dkv)
    grad_q = halved(od[1])
    attended = halved(after(od[0], grad_q)).T

    parts, grad_joined = shares(grad_q, dkv, normed, w_qkv)
    parts = parts.reshape(8, groups, ROWS, LANES)
    parts = lax.all_to_all(parts, "head", 0, 0)
    parts = jnp.sum(parts.astype(F32), axis=0)
    feature = parts[:, :, :HD]
    plain = parts[0, :, HD] + parts[0, :, HD + 2]
    along = parts[0, :, HD + 1] + parts[0, :, HD + 3]
    hidden_grad = inv_std[:, None] * (
        feature - plain[:, None] / width - unit * (along[:, None] / width)
    )

    error = after((slope * hidden_grad).astype(BF), attended)
    padded = with_halo(error)
    wide = exchange_xy(after(slabs(normed, grad_joined), padded))
    wide = jnp.sum(wide.astype(F32), axis=0).astype(BF).reshape(8, SLAB, 3 * HD)
    pair = after(paired(padded), wide)
    frame_grad = hidden_grad + convolved(False, where, pair, taps)
    frame_grad = frame_grad.astype(BF).transpose(1, 0, 2).reshape(ROWS, groups * HD)
    weight_grad = jnp.sum(exchange_z(wide)[:, : HD // 4].astype(F32), axis=0)
    return attended, frame_grad, weight_grad


def solution(mesh):
    return jax.shard_map(
        on_device,
        mesh=mesh,
        in_specs=(
            P("tm", "head"),
            P("tm", "head", None, None),
            P(None, "head"),
            P(),
            P("tm", "head"),
        ),
        out_specs=(P("tm", "head"), P("tm", "head"), P("tm", "head")),
        check_vma=False,
    )
```

```python
import functools
import math

import jax
import jax.numpy as jnp
from jax import lax
from jax.experimental import pallas as pl
from jax.experimental.pallas import tpu as pltpu
from jax.sharding import PartitionSpec as P

HD = 120
KERNEL = 64
HALF = KERNEL // 2
ROWS = 128
LANES = 128
SCALE = HD ** (-0.5)
SCALE2 = SCALE * math.log2(math.e)
FAR = -(2.0**100)
EPS = 1e-05
INV_ROOT_TWO = 0.7071067811865476
INV_ROOT_TAU = 0.3989422804014327

BF = jnp.bfloat16
F32 = jnp.float32

XY_GROUPS = [[y * 32 + z * 4 + x for y in range(2) for x in range(4)] for z in range(8)]
X_GROUPS = [[y * 32 + z * 4 + x for x in range(4)] for y in range(2) for z in range(8)]
Z_GROUPS = [[y * 32 + z * 4 + x for z in range(8)] for y in range(2) for x in range(4)]


def exchange_xy(parts):
    return lax.all_to_all(parts, "tm", 0, 0, axis_index_groups=XY_GROUPS)


def exchange_x(parts):
    return lax.all_to_all(parts, "tm", 0, 0, axis_index_groups=X_GROUPS)


def swap(array, bit):
    return lax.ppermute(array, "tm", [(i, i ^ bit) for i in range(64)])


def exchange_z(parts):
    return lax.all_to_all(parts, "tm", 0, 0, axis_index_groups=Z_GROUPS)


def everyone(array, count=8):
    return jnp.broadcast_to(array[None], (count,) + array.shape)


def after(array, earlier):
    return array + 0 * earlier[(0,) * earlier.ndim].astype(array.dtype)


BITS = (32, 2, 1)
SLOTS = (0, 4, 2, 6, 1, 5, 3, 7)


def doubled(array):
    array = array[None]
    for bit in BITS:
        array = jnp.concatenate([array, swap(array, bit)], axis=0)
    return array


def nothing(array):
    return (0 * array[(0,) * array.ndim].astype(F32)).astype(jnp.int32)


def vmem_call(body, out_shape, scratch=(), scalars=0, inputs=0, flops=0):
    return pl.pallas_call(
        body,
        out_shape=out_shape,
        in_specs=[pl.BlockSpec(memory_space=pltpu.SMEM)] * scalars
        + [pl.BlockSpec(memory_space=pltpu.VMEM)] * inputs,
        out_specs=jax.tree.map(lambda _: pl.BlockSpec(memory_space=pltpu.VMEM), out_shape),
        scratch_shapes=list(scratch),
        compiler_params=pltpu.CompilerParams(vmem_limit_bytes=48 * 1024 * 1024),
        cost_estimate=pl.CostEstimate(flops=flops, bytes_accessed=1 << 20, transcendentals=0),
    )


def bounds_of(pos, ends):
    low = jnp.zeros_like(pos)
    high = jnp.full_like(pos, ends[0])
    for u in range(3):
        inside = pos >= ends[u]
        low = jnp.where(inside, ends[u], low)
        high = jnp.where(inside, ends[u + 1], high)
    return low, high


PADDED = ROWS + KERNEL
TAPS = KERNEL // 2
SPAN = ROWS + TAPS


def conv_body(forward, sc_ref, x_ref, w_ref, own_ref, other_ref):
    ends = [sc_ref[2 + u] for u in range(4)]
    first = TAPS * (sc_ref[0] if forward else 1 - sc_ref[0])
    row = lax.broadcasted_iota(jnp.int32, (ROWS, HD), 0)
    for b in range(2):
        shard = sc_ref[1] if b == 0 else sc_ref[1] ^ 32
        pos = shard * ROWS + row
        low, high = bounds_of(pos, ends)
        source = pos + (first - HALF)
        spans = [
            x_ref[b, g, pl.ds(pl.multiple_of(first, TAPS), SPAN)].astype(F32) for g in range(2)
        ]
        totals = [jnp.zeros((ROWS, HD), F32) for g in range(2)]
        for rest in range(8):
            rolled = [pltpu.roll(e, SPAN - rest, 0) if rest else e for e in spans]
            for start in range(0, TAPS + 1, 8):
                tap = start + rest if forward else TAPS - start - rest
                if not 0 <= tap < TAPS:
                    continue
                at = source + (start + rest)
                keep = (at >= low) & (at < high)
                for g in range(2):
                    piece = jnp.where(keep, rolled[g][start : start + ROWS], 0.0).astype(BF)
                    totals[g] += lax.dot_general(
                        piece,
                        w_ref[tap % 4, tap // 4, g],
                        (((1,), (0 if forward else 1,)), ((), ())),
                        preferred_element_type=F32,
                    )
        for g in range(2):
            if b == 0:
                own_ref[g] = totals[g]
            else:
                other_ref[g] = totals[g].astype(BF)


def paired(padded):
    return jnp.stack([padded, swap(padded, 32)])


def convolved(forward, scalars, pair, taps):
    own, other = vmem_call(
        functools.partial(conv_body, forward),
        (
            jax.ShapeDtypeStruct((2, ROWS, HD), F32),
            jax.ShapeDtypeStruct((2, ROWS, HD), BF),
        ),
        scalars=1,
        inputs=2,
        flops=32 * 2 * 2 * 2 * ROWS * HD * HD,
    )(scalars, pair, taps)
    return own, swap(other, 32)


def with_halo(rows):
    devices = 64
    up = [(i, i + 1) for i in range(devices - 1)]
    down = [(i + 1, i) for i in range(devices - 1)]
    before = lax.ppermute(rows[:, ROWS - HALF :], "tm", up)
    after = lax.ppermute(rows[:, :HALF], "tm", down)
    return jnp.concatenate([before, rows, after], axis=1)


CHUNK = 256


N = CHUNK // ROWS
ALL = 8 * ROWS
CONTRACT = (((1,), (1,)), ((), ()))


def scored(c, q_ref, kv_ref):
    keys = kv_ref[:, :, :LANES].reshape(ALL, LANES)
    values = kv_ref[:, :, LANES : LANES + HD].reshape(ALL, HD)
    q = q_ref[c * N : (c + 1) * N, :, :LANES].reshape(CHUNK, LANES)
    d = q_ref[c * N : (c + 1) * N, :, LANES : LANES + HD].reshape(CHUNK, HD)
    scores = lax.dot_general(keys, q, CONTRACT, preferred_element_type=F32)
    dprobs = lax.dot_general(values, d, CONTRACT, preferred_element_type=F32)
    return keys, values, q, d, scores * SCALE2, dprobs


def stats_body(sc_ref, q_ref, kv_ref, out_ref):
    for c in range(ALL // CHUNK):
        _, _, _, _, scores, dprobs = scored(c, q_ref, kv_ref)
        peak = jnp.max(scores, axis=0, keepdims=True)
        weight = jnp.exp2(scores - peak)
        total = jnp.sum(weight, axis=0, keepdims=True)
        along = jnp.sum(weight * dprobs, axis=0, keepdims=True)
        for i in range(N):
            columns = slice(i * ROWS, (i + 1) * ROWS)
            shard = pl.ds(sc_ref[0] ^ SLOTS[c * N + i], 1)
            for j, value in enumerate((peak, total, along)):
                out_ref[j, shard] = value[:, columns]


def grads_body(sc_ref, q_ref, kv_ref, stats_ref, od_ref, dkv_ref, dk_ref, dv_ref):
    for c in range(ALL // CHUNK):
        peaks, totals, alongs = (
            jnp.concatenate(
                [stats_ref[:, j, pl.ds(sc_ref[0] ^ SLOTS[c * N + i], 1)] for i in range(N)],
                axis=2,
            )
            for j in range(3)
        )
        top = jnp.max(peaks, axis=0)
        factor = jnp.exp2(peaks - top[None])
        total = jnp.sum(totals * factor, axis=0)
        delta = jnp.sum(alongs * factor, axis=0) / total
        lse = top + jnp.log2(total)
        keys, values, q, d, scores, dprobs = scored(c, q_ref, kv_ref)
        probs = jnp.exp2(scores - lse)
        dscores = (probs * (dprobs - delta)).astype(BF)
        probs = probs.astype(BF)
        dv = jnp.dot(probs, d, preferred_element_type=F32)
        dk = jnp.dot(dscores, q, preferred_element_type=F32)
        if c == 0:
            dv_ref[...] = dv
            dk_ref[...] = dk
        else:
            dv_ref[...] += dv
            dk_ref[...] += dk
        inner = (((0,), (0,)), ((), ()))
        out_t = lax.dot_general(values, probs, inner, preferred_element_type=F32)
        dq_t = lax.dot_general(keys, dscores, inner, preferred_element_type=F32) * SCALE
        for i in range(N):
            e = SLOTS[c * N + i]
            at = (sc_ref[0] % 4) ^ (e % 4)
            od_ref[e // 4, at, 0] = out_t[:, i * ROWS : (i + 1) * ROWS].astype(BF)
            od_ref[e // 4, at, 1] = dq_t[:HD, i * ROWS : (i + 1) * ROWS].astype(BF)
    for i in range(8):
        piece = slice(i * ROWS, (i + 1) * ROWS)
        dkv_ref[i, :, :LANES] = (dk_ref[piece] * SCALE).astype(BF)
        dkv_ref[i, :, LANES : LANES + HD] = dv_ref[piece].astype(BF)
        dkv_ref[i, :, LANES + HD :] = jnp.zeros((ROWS, LANES - HD), BF)


def attention_stats(scalars, queries, keys):
    return vmem_call(
        stats_body,
        jax.ShapeDtypeStruct((3, 8, ROWS), F32),
        scalars=1,
        inputs=2,
        flops=2 * 2 * ALL * ALL * LANES,
    )(scalars, queries, keys)


def attention_grads(scalars, queries, keys, stats):
    return vmem_call(
        grads_body,
        (
            jax.ShapeDtypeStruct((2, 4, 2, HD, ROWS), BF),
            jax.ShapeDtypeStruct((8, ROWS, 2 * LANES), BF),
        ),
        scratch=[
            pltpu.VMEM((ALL, LANES), F32),
            pltpu.VMEM((ALL, HD), F32),
        ],
        scalars=1,
        inputs=3,
        flops=6 * 2 * ALL * ALL * LANES,
    )(scalars, queries, keys, stats)


GROUPS = 16
WIDTH = GROUPS * HD
SLAB = 32


def gelu_parts(inputs):
    normal_cdf = 0.5 * (1.0 + lax.erf(inputs * INV_ROOT_TWO))
    density = jnp.exp(-0.5 * inputs * inputs) * INV_ROOT_TAU
    return inputs * normal_cdf, normal_cdf + inputs * density


def hidden_body(own_ref, other_ref, frames_ref, hidden_ref, slope_ref, sent_ref):
    for g in range(2):
        conv = own_ref[g] + other_ref[g].astype(F32)
        activated, slope = gelu_parts(conv)
        hidden = (frames_ref[g].astype(F32) + activated).T
        hidden_ref[g] = hidden
        slope_ref[g] = slope.T
        sent_ref[g] = hidden.astype(BF)


def hidden_rows(own, other, frames_g):
    shape = jax.ShapeDtypeStruct((2, HD, ROWS), F32)
    return vmem_call(
        hidden_body, (shape, shape, jax.ShapeDtypeStruct((2, HD, ROWS), BF)), inputs=3
    )(own, other, frames_g)


def project_body(
    sc_ref, all_ref, hidden_ref, w_ref, up_ref, kv_ref, q_ref, normed_ref, unit_ref, inv_ref
):
    total = jnp.zeros((HD, ROWS), F32)
    square = jnp.zeros((HD, ROWS), F32)
    for g in range(GROUPS):
        hidden = all_ref[g].astype(F32)
        total += hidden
        square += hidden * hidden
    center = jnp.sum(total, axis=0, keepdims=True) / WIDTH
    square = jnp.sum(square, axis=0, keepdims=True) / WIDTH
    inv_std = lax.rsqrt(square - center * center + EPS)
    inv_ref[...] = inv_std
    projected = jnp.zeros((ROWS, 3 * HD), F32)
    for g in range(GROUPS):
        normed = ((all_ref[g].astype(F32) - center) * inv_std).astype(BF)
        normed_ref[g] = normed
        projected += lax.dot_general(
            normed,
            w_ref[g * HD : (g + 1) * HD],
            (((0,), (0,)), ((), ())),
            preferred_element_type=F32,
        )
    for g in range(2):
        unit_ref[g] = (hidden_ref[g] - center) * inv_std
    projected = projected.astype(BF)
    pos = sc_ref[0] * ROWS + lax.broadcasted_iota(jnp.int32, (ROWS, LANES - HD), 0)
    lane = lax.broadcasted_iota(jnp.int32, (ROWS, LANES - HD), 1)
    seg = jnp.zeros_like(pos)
    for u in range(3):
        seg += jnp.where(pos >= sc_ref[1 + u], 1, 0)
    nil = jnp.zeros((ROWS, LANES - HD), BF)
    q_ref[0, :, :HD] = projected[:, :HD]
    q_ref[0, :, HD:LANES] = jnp.where(seg == lane, 1.0, 0.0).astype(BF)
    q_ref[0, :, LANES : LANES + HD] = up_ref[...]
    q_ref[0, :, LANES + HD :] = nil
    k_mark = jnp.where(seg == lane, 0.0, FAR).astype(BF)
    for i in range(8):
        kv_ref[i, :, :HD] = projected[:, HD : 2 * HD]
        kv_ref[i, :, HD:LANES] = k_mark
        kv_ref[i, :, LANES : LANES + HD] = projected[:, 2 * HD :]
        kv_ref[i, :, LANES + HD :] = nil


def project(scalars, all_t, hidden_t, w_qkv, grad_out):
    return vmem_call(
        project_body,
        (
            jax.ShapeDtypeStruct((8, ROWS, 2 * LANES), BF),
            jax.ShapeDtypeStruct((1, ROWS, 2 * LANES), BF),
            jax.ShapeDtypeStruct((GROUPS, HD, ROWS), BF),
            jax.ShapeDtypeStruct((2, HD, ROWS), F32),
            jax.ShapeDtypeStruct((1, ROWS), F32),
        ),
        scalars=1,
        inputs=4,
        flops=2 * ROWS * WIDTH * 3 * HD,
    )(scalars, all_t, hidden_t, w_qkv, grad_out)


def share_body(od_ref, dkv_ref, normed_ref, w_ref, parts_ref, grad_ref, out_ref):
    out, dq = od_ref[0, 0].astype(F32), od_ref[0, 1].astype(F32)
    for i in range(1, 4):
        out += od_ref[i, 0].astype(F32)
        dq += od_ref[i, 1].astype(F32)
    dkv = dkv_ref[0].astype(F32)
    for i in range(1, 8):
        dkv += dkv_ref[i].astype(F32)
    out_ref[...] = out.T.astype(BF)
    grad_ref[:, :HD] = dq.T.astype(BF)
    grad_ref[:, HD : 2 * HD] = dkv[:, :HD].astype(BF)
    grad_ref[:, 2 * HD :] = dkv[:, LANES : LANES + HD].astype(BF)
    grad = grad_ref[...]
    plain = jnp.zeros((HD, ROWS), F32)
    along = jnp.zeros((HD, ROWS), F32)
    for g in range(GROUPS):
        share = lax.dot_general(
            w_ref[g * HD : (g + 1) * HD], grad, CONTRACT, preferred_element_type=F32
        )
        plain += share
        along += share * normed_ref[g].astype(F32)
        parts_ref[g, :HD] = share.astype(BF)
    plain = jnp.sum(plain, axis=0, keepdims=True)
    along = jnp.sum(along, axis=0, keepdims=True)
    plain_high = plain.astype(BF).astype(F32)
    along_high = along.astype(BF).astype(F32)
    rows = [plain_high, along_high, plain - plain_high, along - along_high]
    sums = jnp.concatenate(rows + [jnp.zeros((4, ROWS), F32)], axis=0).astype(BF)
    for g in range(GROUPS):
        parts_ref[g, HD:] = sums


def shares(od, dkv, normed_t, w_qkv):
    return vmem_call(
        share_body,
        (
            jax.ShapeDtypeStruct((GROUPS, LANES, ROWS), BF),
            jax.ShapeDtypeStruct((ROWS, 3 * HD), BF),
            jax.ShapeDtypeStruct((ROWS, HD), BF),
        ),
        inputs=4,
        flops=2 * ROWS * WIDTH * 3 * HD,
    )(od, dkv, normed_t, w_qkv)


def slabs_body(normed_ref, grad_ref, out_ref):
    slab = HD // 4
    grad = grad_ref[...]
    out_ref[...] = jnp.zeros_like(out_ref)
    for g in range(GROUPS):
        wide = jnp.dot(normed_ref[g], grad, preferred_element_type=F32)
        row = g % 8 * SLAB
        for x in range(4):
            piece = wide[x * slab : (x + 1) * slab].astype(BF)
            out_ref[g // 8 * 4 + x, row : row + slab, : 3 * HD] = piece


def slabs(normed_t, grad):
    return vmem_call(
        slabs_body,
        jax.ShapeDtypeStruct((8, 8 * SLAB, 3 * LANES), BF),
        inputs=2,
        flops=2 * ROWS * WIDTH * 3 * HD,
    )(normed_t, grad)


def error_body(parts_ref, unit_ref, inv_ref, slope_ref, grad_ref, error_ref):
    sums = []
    for g in range(2):
        total = parts_ref[0, g].astype(F32)
        for i in range(1, 8):
            total += parts_ref[i, g].astype(F32)
        sums.append(total)
    plain = (sums[0][HD : HD + 1] + sums[0][HD + 2 : HD + 3]) / WIDTH
    along = (sums[0][HD + 1 : HD + 2] + sums[0][HD + 3 : HD + 4]) / WIDTH
    for g in range(2):
        grad = inv_ref[...] * (sums[g][:HD] - plain - unit_ref[g] * along)
        grad_ref[g] = grad.T
        error_ref[g] = (slope_ref[g] * grad).T.astype(BF)


def errors(parts, unit_t, inv_std, slope_t):
    return vmem_call(
        error_body,
        (
            jax.ShapeDtypeStruct((2, ROWS, HD), F32),
            jax.ShapeDtypeStruct((2, ROWS, HD), BF),
        ),
        inputs=4,
    )(parts, unit_t, inv_std, slope_t)


def on_device(frames, conv_weight, w_qkv, lengths, grad_out):
    index = lax.axis_index("tm")
    y, x = index // 32, index % 4
    ends = jnp.cumsum(lengths).astype(jnp.int32)

    def scalars(*first):
        return jnp.concatenate([jnp.stack(first).astype(jnp.int32), ends])

    where = scalars(y, index)
    order = scalars(y * 4 + x)

    frames_g = frames.reshape(ROWS, 2, HD).transpose(1, 0, 2)
    pair = paired(with_halo(frames_g))
    taps = exchange_z(everyone(conv_weight[0]))
    taps = exchange_x(everyone(after(taps, pair), 4))
    own, other = convolved(True, where, pair, taps)
    hidden_t, slope_t, sent = hidden_rows(own, other, frames_g)

    all_t = lax.all_gather(sent, "head", axis=0, tiled=True)
    keys, queries, normed_t, unit_t, inv_std = project(
        scalars(index), all_t, hidden_t, w_qkv, grad_out
    )

    keys = exchange_z(keys)
    queries = doubled(queries[0])
    stats = exchange_xy(everyone(attention_stats(order, queries, keys)))
    od, dkv = attention_grads(order, queries, keys, stats)
    dkv = exchange_z(dkv)
    od = exchange_x(after(od[0] + swap(od[1], 32), dkv))

    parts, grad, attended = shares(od, dkv, normed_t, w_qkv)
    parts = lax.all_to_all(parts.reshape(8, 2, LANES, ROWS), "head", 0, 0)
    hidden_grad, error = errors(parts, unit_t, inv_std, slope_t)
    wide = exchange_xy(slabs(normed_t, grad))
    wide = jnp.sum(wide.astype(F32), axis=0).astype(BF)

    pair = paired(with_halo(error))
    own, other = convolved(False, where + nothing(wide), pair, taps)
    frame_grad = (hidden_grad + own + other.astype(F32)).astype(BF)
    wide = exchange_z(wide.reshape(8, SLAB, 3 * LANES))
    weight_grad = jnp.sum(wide[:, : HD // 4, : 3 * HD].astype(F32), axis=0)
    return attended, frame_grad.transpose(1, 0, 2).reshape(ROWS, 2 * HD), weight_grad


def solution(mesh):
    return jax.shard_map(
        on_device,
        mesh=mesh,
        in_specs=(
            P("tm", "head"),
            P("tm", "head", None, None),
            P(None, "head"),
            P(),
            P("tm", "head"),
        ),
        out_specs=(P("tm", "head"), P("tm", "head"), P("tm", "head")),
        check_vma=False,
    )
```

```python
import functools
import math

import jax
import jax.numpy as jnp
from jax import lax
from jax.experimental import pallas as pl
from jax.experimental.pallas import tpu as pltpu
from jax.sharding import PartitionSpec as P

HD = 120
KERNEL = 64
HALF = KERNEL // 2
ROWS = 128
LANES = 128
SCALE = HD ** (-0.5)
SCALE2 = SCALE * math.log2(math.e)
FAR = -(2.0**100)
EPS = 1e-05
INV_ROOT_TWO = 0.7071067811865476
INV_ROOT_TAU = 0.3989422804014327

BF = jnp.bfloat16
F32 = jnp.float32

XY_GROUPS = [[y * 32 + z * 4 + x for y in range(2) for x in range(4)] for z in range(8)]
X_GROUPS = [[y * 32 + z * 4 + x for x in range(4)] for y in range(2) for z in range(8)]
Z_GROUPS = [[y * 32 + z * 4 + x for z in range(8)] for y in range(2) for x in range(4)]


def exchange_xy(parts):
    return lax.all_to_all(parts, "tm", 0, 0, axis_index_groups=XY_GROUPS)


def exchange_x(parts):
    return lax.all_to_all(parts, "tm", 0, 0, axis_index_groups=X_GROUPS)


def swap(array, bit):
    return lax.ppermute(array, "tm", [(i, i ^ bit) for i in range(64)])


def exchange_z(parts):
    return lax.all_to_all(parts, "tm", 0, 0, axis_index_groups=Z_GROUPS)


def everyone(array, count=8):
    return jnp.broadcast_to(array[None], (count,) + array.shape)


def after(array, earlier):
    return array + 0 * earlier[(0,) * earlier.ndim].astype(array.dtype)


BITS = (32, 2, 1)
SLOTS = (0, 4, 2, 6, 1, 5, 3, 7)


def doubled(array):
    array = array[None]
    for bit in BITS:
        array = jnp.concatenate([array, swap(array, bit)], axis=0)
    return array


def vmem_call(body, out_shape, scratch=(), scalars=0, inputs=0, flops=0):
    return pl.pallas_call(
        body,
        out_shape=out_shape,
        in_specs=[pl.BlockSpec(memory_space=pltpu.SMEM)] * scalars
        + [pl.BlockSpec(memory_space=pltpu.VMEM)] * inputs,
        out_specs=jax.tree.map(lambda _: pl.BlockSpec(memory_space=pltpu.VMEM), out_shape),
        scratch_shapes=list(scratch),
        compiler_params=pltpu.CompilerParams(vmem_limit_bytes=48 * 1024 * 1024),
        cost_estimate=pl.CostEstimate(flops=flops, bytes_accessed=1 << 20, transcendentals=0),
    )


def bounds_of(pos, ends):
    low = jnp.zeros_like(pos)
    high = jnp.full_like(pos, ends[0])
    for u in range(3):
        inside = pos >= ends[u]
        low = jnp.where(inside, ends[u], low)
        high = jnp.where(inside, ends[u + 1], high)
    return low, high


PADDED = ROWS + KERNEL
TAPS = KERNEL // 2
SPAN = ROWS + TAPS


def conv_body(forward, sc_ref, x_ref, w_ref, own_ref, other_ref):
    ends = [sc_ref[2 + u] for u in range(4)]
    first = TAPS * (sc_ref[0] if forward else 1 - sc_ref[0])
    row = lax.broadcasted_iota(jnp.int32, (ROWS, LANES), 0)
    for b in range(2):
        shard = sc_ref[1] if b == 0 else sc_ref[1] ^ 32
        pos = shard * ROWS + row
        low, high = bounds_of(pos, ends)
        source = pos + (first - HALF)
        spans = [
            x_ref[b, pl.ds(pl.multiple_of(g * PADDED + first, TAPS), SPAN)].astype(F32)
            for g in range(2)
        ]
        totals = [jnp.zeros((ROWS, LANES), F32) for g in range(2)]
        for rest in range(8):
            rolled = [pltpu.roll(e, SPAN - rest, 0) if rest else e for e in spans]
            for start in range(0, TAPS + 1, 8):
                tap = start + rest if forward else TAPS - start - rest
                if not 0 <= tap < TAPS:
                    continue
                key = source + (start + rest)
                keep = (key >= low) & (key < high)
                for g in range(2):
                    at = (tap // 4 * 2 + g) * LANES
                    piece = jnp.where(keep, rolled[g][start : start + ROWS], 0.0).astype(BF)
                    totals[g] += lax.dot_general(
                        piece,
                        w_ref[tap % 4, at : at + LANES],
                        (((1,), (0 if forward else 1,)), ((), ())),
                        preferred_element_type=F32,
                    )
        for g in range(2):
            if b == 0:
                own_ref[g] = totals[g]
            else:
                other_ref[g] = totals[g].astype(BF)


def taps_body(w_ref, out_ref):
    out_ref[0] = jnp.zeros((2 * LANES, LANES), BF)
    for g in range(2):
        out_ref[0, g * LANES : g * LANES + HD, :HD] = w_ref[g]
    for i in range(1, 8):
        out_ref[i] = out_ref[0]


def taps_sent(weight):
    return vmem_call(
        taps_body, jax.ShapeDtypeStruct((8, 2 * LANES, LANES), BF), inputs=1
    )(weight)


def joined_body(w_ref, pair_ref, out_ref):
    for i in range(4):
        for z in range(8):
            out_ref[i, z * 2 * LANES : (z + 1) * 2 * LANES] = w_ref[z]
        for b in range(2):
            start = 16 * LANES + b * ROWS
            out_ref[i, start : start + ROWS] = pair_ref[b, 2 * PADDED :]


def joined(taps, pair):
    return vmem_call(
        joined_body, jax.ShapeDtypeStruct((4, 16 * LANES + 2 * ROWS, LANES), BF), inputs=2
    )(taps, pair)


def paired(padded):
    return jnp.stack([padded, swap(padded, 32)])


def convolved(forward, scalars, pair, taps):
    own, other = vmem_call(
        functools.partial(conv_body, forward),
        (
            jax.ShapeDtypeStruct((2, ROWS, LANES), F32),
            jax.ShapeDtypeStruct((2, ROWS, LANES), BF),
        ),
        scalars=1,
        inputs=2,
        flops=32 * 2 * 2 * 2 * ROWS * HD * HD,
    )(scalars, pair, taps)
    return own, swap(other, 32)


def with_halo(rows):
    devices = 64
    up = [(i, i + 1) for i in range(devices - 1)]
    down = [(i + 1, i) for i in range(devices - 1)]
    before = lax.ppermute(rows[:, ROWS - HALF :], "tm", up)
    after = lax.ppermute(rows[:, :HALF], "tm", down)
    return jnp.concatenate([before, rows, after], axis=1)


CHUNK = 256


N = CHUNK // ROWS
ALL = 8 * ROWS
CONTRACT = (((1,), (1,)), ((), ()))


def upstream_rows(sc_ref, f_ref, d_ref):
    for i, e in enumerate(SLOTS):
        row = 16 * LANES + e // 4 * ROWS
        d_ref[i * ROWS : (i + 1) * ROWS] = f_ref[(sc_ref[0] % 4) ^ (e % 4), row : row + ROWS]


def scored(c, q_ref, kv_ref, d_ref):
    keys = kv_ref[:, :, :LANES].reshape(ALL, LANES)
    values = kv_ref[:, :, LANES:].reshape(ALL, LANES)
    q = q_ref[c * N : (c + 1) * N].reshape(CHUNK, LANES)
    d = d_ref[c * CHUNK : (c + 1) * CHUNK]
    scores = lax.dot_general(keys, q, CONTRACT, preferred_element_type=F32)
    dprobs = lax.dot_general(values, d, CONTRACT, preferred_element_type=F32)
    return keys, values, q, d, scores * SCALE2, dprobs


def stats_body(sc_ref, q_ref, kv_ref, f_ref, out_ref, d_ref):
    upstream_rows(sc_ref, f_ref, d_ref)
    for c in range(ALL // CHUNK):
        _, _, _, _, scores, dprobs = scored(c, q_ref, kv_ref, d_ref)
        peak = jnp.max(scores, axis=0, keepdims=True)
        weight = jnp.exp2(scores - peak)
        total = jnp.sum(weight, axis=0, keepdims=True)
        along = jnp.sum(weight * dprobs, axis=0, keepdims=True)
        for i in range(N):
            columns = slice(i * ROWS, (i + 1) * ROWS)
            shard = pl.ds(sc_ref[0] ^ SLOTS[c * N + i], 1)
            for j, value in enumerate((peak, total, along)):
                out_ref[j, shard] = value[:, columns]


def grads_body(
    sc_ref, q_ref, kv_ref, f_ref, stats_ref, od_ref, dkv_ref, d_ref, dk_ref, dv_ref
):
    upstream_rows(sc_ref, f_ref, d_ref)
    for c in range(ALL // CHUNK):
        peaks, totals, alongs = (
            jnp.concatenate(
                [stats_ref[:, j, pl.ds(sc_ref[0] ^ SLOTS[c * N + i], 1)] for i in range(N)],
                axis=2,
            )
            for j in range(3)
        )
        top = jnp.max(peaks, axis=0)
        factor = jnp.exp2(peaks - top[None])
        total = jnp.sum(totals * factor, axis=0)
        delta = jnp.sum(alongs * factor, axis=0) / total
        lse = top + jnp.log2(total)
        keys, values, q, d, scores, dprobs = scored(c, q_ref, kv_ref, d_ref)
        probs = jnp.exp2(scores - lse)
        dscores = (probs * (dprobs - delta)).astype(BF)
        probs = probs.astype(BF)
        dv = jnp.dot(probs, d, preferred_element_type=F32)
        dk = jnp.dot(dscores, q, preferred_element_type=F32)
        if c == 0:
            dv_ref[...] = dv
            dk_ref[...] = dk
        else:
            dv_ref[...] += dv
            dk_ref[...] += dk
        inner = (((0,), (0,)), ((), ()))
        out_t = lax.dot_general(values, probs, inner, preferred_element_type=F32)
        dq_t = lax.dot_general(keys, dscores, inner, preferred_element_type=F32) * SCALE
        for i in range(N):
            at = sc_ref[0] ^ SLOTS[c * N + i]
            od_ref[at, 0] = out_t[:HD, i * ROWS : (i + 1) * ROWS].astype(BF)
            od_ref[at, 1] = dq_t[:HD, i * ROWS : (i + 1) * ROWS].astype(BF)
    for i in range(8):
        piece = slice(i * ROWS, (i + 1) * ROWS)
        dkv_ref[i, :, :LANES] = (dk_ref[piece] * SCALE).astype(BF)
        dkv_ref[i, :, LANES:] = dv_ref[piece].astype(BF)


def attention_stats(scalars, queries, keys, gathered):
    return vmem_call(
        stats_body,
        jax.ShapeDtypeStruct((3, 8, ROWS), F32),
        scratch=[pltpu.VMEM((ALL, LANES), BF)],
        scalars=1,
        inputs=3,
        flops=2 * 2 * ALL * ALL * LANES,
    )(scalars, queries, keys, gathered)


def attention_grads(scalars, queries, keys, gathered, stats):
    return vmem_call(
        grads_body,
        (
            jax.ShapeDtypeStruct((8, 2, HD, ROWS), BF),
            jax.ShapeDtypeStruct((8, ROWS, 2 * LANES), BF),
        ),
        scratch=[
            pltpu.VMEM((ALL, LANES), BF),
            pltpu.VMEM((ALL, LANES), F32),
            pltpu.VMEM((ALL, LANES), F32),
        ],
        scalars=1,
        inputs=4,
        flops=6 * 2 * ALL * ALL * LANES,
    )(scalars, queries, keys, gathered, stats)


GROUPS = 16
WIDTH = GROUPS * HD
SLAB = 32


def gelu_parts(inputs):
    normal_cdf = 0.5 * (1.0 + lax.erf(inputs * INV_ROOT_TWO))
    density = jnp.exp(-0.5 * inputs * inputs) * INV_ROOT_TAU
    return inputs * normal_cdf, normal_cdf + inputs * density


def hidden_body(own_ref, other_ref, frames_ref, hidden_ref, slope_ref, sent_ref):
    for g in range(2):
        conv = own_ref[g] + other_ref[g].astype(F32)
        activated, slope = gelu_parts(conv)
        hidden = (frames_ref[g].astype(F32) + activated).T[:HD]
        hidden_ref[g] = hidden
        slope_ref[g] = slope.T[:HD]
        sent_ref[g] = hidden.astype(BF)


def hidden_rows(own, other, frames_g):
    shape = jax.ShapeDtypeStruct((2, HD, ROWS), F32)
    return vmem_call(
        hidden_body, (shape, shape, jax.ShapeDtypeStruct((2, HD, ROWS), BF)), inputs=3
    )(own, other, frames_g)


def project_body(
    sc_ref, all_ref, hidden_ref, w_ref, kv_ref, q_ref, normed_ref, unit_ref, inv_ref
):
    total = jnp.zeros((HD, ROWS), F32)
    square = jnp.zeros((HD, ROWS), F32)
    for g in range(GROUPS):
        hidden = all_ref[g].astype(F32)
        total += hidden
        square += hidden * hidden
    center = jnp.sum(total, axis=0, keepdims=True) / WIDTH
    square = jnp.sum(square, axis=0, keepdims=True) / WIDTH
    inv_std = lax.rsqrt(square - center * center + EPS)
    inv_ref[...] = inv_std
    projected = jnp.zeros((ROWS, 3 * HD), F32)
    for g in range(GROUPS):
        normed = ((all_ref[g].astype(F32) - center) * inv_std).astype(BF)
        normed_ref[g] = normed
        projected += lax.dot_general(
            normed,
            w_ref[g * HD : (g + 1) * HD],
            (((0,), (0,)), ((), ())),
            preferred_element_type=F32,
        )
    for g in range(2):
        unit_ref[g] = (hidden_ref[g] - center) * inv_std
    projected = projected.astype(BF)
    pos = sc_ref[0] * ROWS + lax.broadcasted_iota(jnp.int32, (ROWS, LANES - HD), 0)
    lane = lax.broadcasted_iota(jnp.int32, (ROWS, LANES - HD), 1)
    seg = jnp.zeros_like(pos)
    for u in range(3):
        seg += jnp.where(pos >= sc_ref[1 + u], 1, 0)
    nil = jnp.zeros((ROWS, LANES - HD), BF)
    q_ref[:, :HD] = projected[:, :HD]
    q_ref[:, HD:] = jnp.where(seg == lane, 1.0, 0.0).astype(BF)
    k_mark = jnp.where(seg == lane, 0.0, FAR).astype(BF)
    for i in range(8):
        kv_ref[i, :, :HD] = projected[:, HD : 2 * HD]
        kv_ref[i, :, HD:LANES] = k_mark
        kv_ref[i, :, LANES : LANES + HD] = projected[:, 2 * HD :]
        kv_ref[i, :, LANES + HD :] = nil


def project(scalars, all_t, hidden_t, w_qkv):
    return vmem_call(
        project_body,
        (
            jax.ShapeDtypeStruct((8, ROWS, 2 * LANES), BF),
            jax.ShapeDtypeStruct((ROWS, LANES), BF),
            jax.ShapeDtypeStruct((GROUPS, HD, ROWS), BF),
            jax.ShapeDtypeStruct((2, HD, ROWS), F32),
            jax.ShapeDtypeStruct((1, ROWS), F32),
        ),
        scalars=1,
        inputs=3,
        flops=2 * ROWS * WIDTH * 3 * HD,
    )(scalars, all_t, hidden_t, w_qkv)


def share_body(od_ref, dkv_ref, normed_ref, w_ref, parts_ref, grad_ref, out_ref):
    out, dq = od_ref[0, 0].astype(F32), od_ref[0, 1].astype(F32)
    for i in range(1, 8):
        out += od_ref[i, 0].astype(F32)
        dq += od_ref[i, 1].astype(F32)
    dkv = dkv_ref[0].astype(F32)
    for i in range(1, 8):
        dkv += dkv_ref[i].astype(F32)
    out_ref[...] = out.T.astype(BF)
    grad_ref[:, :HD] = dq.T.astype(BF)
    grad_ref[:, HD : 2 * HD] = dkv[:, :HD].astype(BF)
    grad_ref[:, 2 * HD :] = dkv[:, LANES : LANES + HD].astype(BF)
    grad = grad_ref[...]
    plain = jnp.zeros((HD, ROWS), F32)
    along = jnp.zeros((HD, ROWS), F32)
    for g in range(GROUPS):
        share = lax.dot_general(
            w_ref[g * HD : (g + 1) * HD], grad, CONTRACT, preferred_element_type=F32
        )
        plain += share
        along += share * normed_ref[g].astype(F32)
        parts_ref[g, :HD] = share.astype(BF)
    plain = jnp.sum(plain, axis=0, keepdims=True)
    along = jnp.sum(along, axis=0, keepdims=True)
    plain_high = plain.astype(BF).astype(F32)
    along_high = along.astype(BF).astype(F32)
    rows = [plain_high, along_high, plain - plain_high, along - along_high]
    sums = jnp.concatenate(rows + [jnp.zeros((4, ROWS), F32)], axis=0).astype(BF)
    for g in range(GROUPS):
        parts_ref[g, HD:] = sums


def shares(od, dkv, normed_t, w_qkv):
    return vmem_call(
        share_body,
        (
            jax.ShapeDtypeStruct((GROUPS, LANES, ROWS), BF),
            jax.ShapeDtypeStruct((ROWS, 3 * HD), BF),
            jax.ShapeDtypeStruct((ROWS, HD), BF),
        ),
        inputs=4,
        flops=2 * ROWS * WIDTH * 3 * HD,
    )(od, dkv, normed_t, w_qkv)


def slabs_body(normed_ref, grad_ref, out_ref):
    slab = HD // 4
    grad = grad_ref[...]
    out_ref[...] = jnp.zeros_like(out_ref)
    for g in range(GROUPS):
        wide = jnp.dot(normed_ref[g], grad, preferred_element_type=F32)
        row = g % 8 * SLAB
        for x in range(4):
            piece = wide[x * slab : (x + 1) * slab].astype(BF)
            out_ref[g // 8 * 4 + x, row : row + slab, : 3 * HD] = piece


def slabs(normed_t, grad):
    return vmem_call(
        slabs_body,
        jax.ShapeDtypeStruct((8, 8 * SLAB, 3 * LANES), BF),
        inputs=2,
        flops=2 * ROWS * WIDTH * 3 * HD,
    )(normed_t, grad)


def error_body(parts_ref, unit_ref, inv_ref, slope_ref, grad_ref, error_ref):
    sums = []
    for g in range(2):
        total = parts_ref[0, g].astype(F32)
        for i in range(1, 8):
            total += parts_ref[i, g].astype(F32)
        sums.append(total)
    plain = (sums[0][HD : HD + 1] + sums[0][HD + 2 : HD + 3]) / WIDTH
    along = (sums[0][HD + 1 : HD + 2] + sums[0][HD + 3 : HD + 4]) / WIDTH
    for g in range(2):
        grad = inv_ref[...] * (sums[g][:HD] - plain - unit_ref[g] * along)
        nil = jnp.zeros((LANES - HD, ROWS), F32)
        grad_ref[g] = jnp.concatenate([grad, nil], axis=0).T
        error_ref[g] = jnp.concatenate([slope_ref[g] * grad, nil], axis=0).T.astype(BF)


def errors(parts, unit_t, inv_std, slope_t):
    return vmem_call(
        error_body,
        (
            jax.ShapeDtypeStruct((2, ROWS, LANES), F32),
            jax.ShapeDtypeStruct((2, ROWS, LANES), BF),
        ),
        inputs=4,
    )(parts, unit_t, inv_std, slope_t)


def on_device(frames, conv_weight, w_qkv, lengths, grad_out):
    index = lax.axis_index("tm")
    y, x = index // 32, index % 4
    ends = jnp.cumsum(lengths).astype(jnp.int32)

    def scalars(*first):
        return jnp.concatenate([jnp.stack(first).astype(jnp.int32), ends])

    where = scalars(y, index)
    order = scalars(y * 4 + x)

    frames_g = frames.reshape(ROWS, 2, HD).transpose(1, 0, 2)
    frames_g = jnp.pad(frames_g, ((0, 0), (0, 0), (0, LANES - HD)))
    upstream = jnp.pad(grad_out, ((0, 0), (0, LANES - HD)))
    rows = with_halo(frames_g).reshape(2 * PADDED, LANES)
    pair = paired(jnp.concatenate([rows, upstream], axis=0))
    taps = exchange_z(taps_sent(conv_weight[0]))
    taps = exchange_x(joined(taps, pair))
    own, other = convolved(True, where, pair, taps)
    hidden_t, slope_t, sent = hidden_rows(own, other, frames_g)

    all_t = lax.all_gather(sent, "head", axis=0, tiled=True)
    keys, queries, normed_t, unit_t, inv_std = project(
        scalars(index), all_t, hidden_t, w_qkv
    )

    keys = exchange_z(keys)
    queries = doubled(queries)
    stats = exchange_xy(everyone(attention_stats(order, queries, keys, taps)))
    od, dkv = attention_grads(order, queries, keys, taps, stats)
    od = exchange_xy(od)
    dkv = exchange_z(dkv)

    parts, grad, attended = shares(od, dkv, normed_t, w_qkv)
    parts = lax.all_to_all(parts.reshape(8, 2, LANES, ROWS), "head", 0, 0)
    hidden_grad, error = errors(parts, unit_t, inv_std, slope_t)
    wide = exchange_xy(slabs(normed_t, grad))
    wide = jnp.sum(wide.astype(F32), axis=0).astype(BF)

    rows = after(with_halo(error).reshape(2 * PADDED, LANES), wide)
    own, other = convolved(False, where, paired(rows), taps)
    frame_grad = (hidden_grad + own + other.astype(F32)).astype(BF)[:, :, :HD]
    wide = exchange_z(wide.reshape(8, SLAB, 3 * LANES))
    weight_grad = jnp.sum(wide[:, : HD // 4, : 3 * HD].astype(F32), axis=0)
    return attended, frame_grad.transpose(1, 0, 2).reshape(ROWS, 2 * HD), weight_grad


def solution(mesh):
    return jax.shard_map(
        on_device,
        mesh=mesh,
        in_specs=(
            P("tm", "head"),
            P("tm", "head", None, None),
            P(None, "head"),
            P(),
            P("tm", "head"),
        ),
        out_specs=(P("tm", "head"), P("tm", "head"), P("tm", "head")),
        check_vma=False,
    )
```

```python
import functools
import math

import jax
import jax.numpy as jnp
from jax import lax
from jax.experimental import pallas as pl
from jax.experimental.pallas import tpu as pltpu
from jax.sharding import PartitionSpec as P

HD = 120
KERNEL = 64
HALF = KERNEL // 2
ROWS = 128
LANES = 128
SCALE = HD ** (-0.5)
SCALE2 = SCALE * math.log2(math.e)
FAR = -(2.0**100)
EPS = 1e-05
INV_ROOT_TWO = 0.7071067811865476
INV_ROOT_TAU = 0.3989422804014327

BF = jnp.bfloat16
F32 = jnp.float32

XY_GROUPS = [[y * 32 + z * 4 + x for y in range(2) for x in range(4)] for z in range(8)]
X_GROUPS = [[y * 32 + z * 4 + x for x in range(4)] for y in range(2) for z in range(8)]
CORE_GROUPS = [[h * 2 + c for c in range(2)] for h in range(4)]
HIGH_GROUPS = [[h * 2 + c for h in range(4)] for c in range(2)]
Z_GROUPS = [[y * 32 + z * 4 + x for z in range(8)] for y in range(2) for x in range(4)]


def exchange_xy(parts):
    return lax.all_to_all(parts, "tm", 0, 0, axis_index_groups=XY_GROUPS)


def exchange_x(parts):
    return lax.all_to_all(parts, "tm", 0, 0, axis_index_groups=X_GROUPS)


def swap(array, bit):
    return lax.ppermute(array, "tm", [(i, i ^ bit) for i in range(64)])


def exchange_z(parts):
    return lax.all_to_all(parts, "tm", 0, 0, axis_index_groups=Z_GROUPS)


def exchange_head(parts, groups):
    return lax.all_to_all(parts, "head", 0, 0, axis_index_groups=groups)


def vmem_call(body, out_shape, scratch=(), scalars=0, inputs=0, earlier=0, flops=0):
    return pl.pallas_call(
        body,
        out_shape=out_shape,
        in_specs=[pl.BlockSpec(memory_space=pltpu.SMEM)] * scalars
        + [pl.BlockSpec(memory_space=pltpu.VMEM)] * inputs
        + [pl.BlockSpec(memory_space=pl.ANY)] * earlier,
        out_specs=jax.tree.map(lambda _: pl.BlockSpec(memory_space=pltpu.VMEM), out_shape),
        scratch_shapes=list(scratch),
        compiler_params=pltpu.CompilerParams(vmem_limit_bytes=48 * 1024 * 1024),
        cost_estimate=pl.CostEstimate(flops=flops, bytes_accessed=1 << 20, transcendentals=0),
    )


def bounds_of(pos, ends):
    low = jnp.zeros_like(pos)
    high = jnp.full_like(pos, ends[0])
    for u in range(3):
        inside = pos >= ends[u]
        low = jnp.where(inside, ends[u], low)
        high = jnp.where(inside, ends[u + 1], high)
    return low, high


PADDED = ROWS + KERNEL
TAPS = KERNEL // 2
SPAN = ROWS + TAPS


def conv_body(forward, sc_ref, x_ref, w_ref, own_ref, other_ref):
    ends = [sc_ref[2 + u] for u in range(4)]
    first = TAPS * (sc_ref[0] if forward else 1 - sc_ref[0])
    row = lax.broadcasted_iota(jnp.int32, (ROWS, LANES), 0)
    for b in range(2):
        shard = sc_ref[1] if b == 0 else sc_ref[1] ^ 32
        pos = shard * ROWS + row
        low, high = bounds_of(pos, ends)
        source = pos + (first - HALF)
        spans = [
            x_ref[b, pl.ds(pl.multiple_of(g * PADDED + first, TAPS), SPAN)].astype(F32)
            for g in range(2)
        ]
        totals = [jnp.zeros((ROWS, LANES), F32) for g in range(2)]
        for rest in range(8):
            rolled = [pltpu.roll(e, SPAN - rest, 0) if rest else e for e in spans]
            for start in range(0, TAPS + 1, 8):
                tap = start + rest if forward else TAPS - start - rest
                if not 0 <= tap < TAPS:
                    continue
                key = source + (start + rest)
                keep = (key >= low) & (key < high)
                for g in range(2):
                    at = (tap // 4 * 2 + g) * LANES
                    piece = jnp.where(keep, rolled[g][start : start + ROWS], 0.0).astype(BF)
                    totals[g] += lax.dot_general(
                        piece,
                        w_ref[tap % 4, at : at + LANES],
                        (((1,), (0 if forward else 1,)), ((), ())),
                        preferred_element_type=F32,
                    )
        for g in range(2):
            if b == 0:
                own_ref[g] = totals[g]
            else:
                other_ref[g] = totals[g].astype(BF)


def taps_body(w_ref, out_ref):
    out_ref[0] = jnp.zeros((2 * LANES, LANES), BF)
    for g in range(2):
        out_ref[0, g * LANES : g * LANES + HD, :HD] = w_ref[g]
    for i in range(1, 8):
        out_ref[i] = out_ref[0]


def taps_sent(weight):
    return vmem_call(
        taps_body, jax.ShapeDtypeStruct((8, 2 * LANES, LANES), BF), inputs=1
    )(weight)


def joined_body(w_ref, pair_ref, qkv_ref, up_ref, out_ref):
    for i in range(4):
        for z in range(8):
            out_ref[i, z * 2 * LANES : (z + 1) * 2 * LANES] = w_ref[z]


def joined(taps, pair, w_qkv, grad_out):
    return vmem_call(
        joined_body, jax.ShapeDtypeStruct((4, 16 * LANES, LANES), BF), inputs=1, earlier=3
    )(taps, pair, w_qkv, grad_out)


def paired(padded):
    return jnp.stack([padded, swap(padded, 32)])


def convolved(forward, scalars, pair, taps):
    own, other = vmem_call(
        functools.partial(conv_body, forward),
        (
            jax.ShapeDtypeStruct((2, ROWS, LANES), F32),
            jax.ShapeDtypeStruct((2, ROWS, LANES), BF),
        ),
        scalars=1,
        inputs=2,
        flops=32 * 2 * 2 * 2 * ROWS * HD * HD,
    )(scalars, pair, taps)
    return own, swap(other, 32)


def with_halo(rows):
    devices = 64
    up = [(i, i + 1) for i in range(devices - 1)]
    down = [(i + 1, i) for i in range(devices - 1)]
    before = lax.ppermute(rows[:, ROWS - HALF :], "tm", up)
    after = lax.ppermute(rows[:, :HALF], "tm", down)
    return jnp.concatenate([before, rows, after], axis=1)


CHUNK = 256


N = CHUNK // ROWS
ALL = 8 * ROWS
CONTRACT = (((1,), (1,)), ((), ()))


def scored(c, q_ref, kv_ref):
    keys = kv_ref[:, :, :LANES].reshape(ALL, LANES)
    values = kv_ref[:, :, LANES:].reshape(ALL, LANES)
    q = q_ref[c * N : (c + 1) * N, :, :LANES].reshape(CHUNK, LANES)
    d = q_ref[c * N : (c + 1) * N, :, LANES:].reshape(CHUNK, LANES)
    scores = lax.dot_general(keys, q, CONTRACT, preferred_element_type=F32)
    dprobs = lax.dot_general(values, d, CONTRACT, preferred_element_type=F32)
    return keys, values, q, d, scores * SCALE2, dprobs


def stats_body(q_ref, kv_ref, out_ref):
    for c in range(ALL // CHUNK):
        _, _, _, _, scores, dprobs = scored(c, q_ref, kv_ref)
        peak = jnp.max(scores, axis=0, keepdims=True)
        weight = jnp.exp2(scores - peak)
        total = jnp.sum(weight, axis=0, keepdims=True)
        along = jnp.sum(weight * dprobs, axis=0, keepdims=True)
        for i in range(N):
            shard = c * N + i
            for j, value in enumerate((peak, total, along)):
                out_ref[0, j, shard : shard + 1] = value[:, i * ROWS : (i + 1) * ROWS]
    for i in range(1, 8):
        out_ref[i] = out_ref[0]


def grads_body(q_ref, kv_ref, stats_ref, od_ref, dkv_ref, dk_ref, dv_ref):
    for c in range(ALL // CHUNK):
        peaks, totals, alongs = (
            jnp.concatenate(
                [stats_ref[:, j, c * N + i : c * N + i + 1] for i in range(N)], axis=2
            )
            for j in range(3)
        )
        top = jnp.max(peaks, axis=0)
        factor = jnp.exp2(peaks - top[None])
        total = jnp.sum(totals * factor, axis=0)
        delta = jnp.sum(alongs * factor, axis=0) / total
        lse = top + jnp.log2(total)
        keys, values, q, d, scores, dprobs = scored(c, q_ref, kv_ref)
        probs = jnp.exp2(scores - lse)
        dscores = (probs * (dprobs - delta)).astype(BF)
        probs = probs.astype(BF)
        dv = jnp.dot(probs, d, preferred_element_type=F32)
        dk = jnp.dot(dscores, q, preferred_element_type=F32)
        if c == 0:
            dv_ref[...] = dv
            dk_ref[...] = dk
        else:
            dv_ref[...] += dv
            dk_ref[...] += dk
        inner = (((0,), (0,)), ((), ()))
        out_t = lax.dot_general(values, probs, inner, preferred_element_type=F32)
        dq_t = lax.dot_general(keys, dscores, inner, preferred_element_type=F32) * SCALE
        for i in range(N):
            at = c * N + i
            od_ref[at, 0] = out_t[:HD, i * ROWS : (i + 1) * ROWS].astype(BF)
            od_ref[at, 1] = dq_t[:HD, i * ROWS : (i + 1) * ROWS].astype(BF)
    for i in range(8):
        piece = slice(i * ROWS, (i + 1) * ROWS)
        dkv_ref[i, :, :LANES] = (dk_ref[piece] * SCALE).astype(BF)
        dkv_ref[i, :, LANES:] = dv_ref[piece].astype(BF)


def attention_stats(queries, keys):
    return vmem_call(
        stats_body,
        jax.ShapeDtypeStruct((8, 3, 8, ROWS), F32),
        inputs=2,
        flops=2 * 2 * ALL * ALL * LANES,
    )(queries, keys)


def attention_grads(queries, keys, stats):
    return vmem_call(
        grads_body,
        (
            jax.ShapeDtypeStruct((8, 2, HD, ROWS), BF),
            jax.ShapeDtypeStruct((8, ROWS, 2 * LANES), BF),
        ),
        scratch=[pltpu.VMEM((ALL, LANES), F32)] * 2,
        inputs=3,
        flops=6 * 2 * ALL * ALL * LANES,
    )(queries, keys, stats)


GROUPS = 16
WIDTH = GROUPS * HD
SLAB = 32


def gelu_parts(inputs):
    normal_cdf = 0.5 * (1.0 + lax.erf(inputs * INV_ROOT_TWO))
    density = jnp.exp(-0.5 * inputs * inputs) * INV_ROOT_TAU
    return inputs * normal_cdf, normal_cdf + inputs * density


def hidden_body(own_ref, other_ref, frames_ref, hidden_ref, slope_ref, sent_ref):
    for g in range(2):
        conv = own_ref[g] + other_ref[g].astype(F32)
        activated, slope = gelu_parts(conv)
        hidden = (frames_ref[g].astype(F32) + activated).T[:HD]
        hidden_ref[g] = hidden
        slope_ref[g] = slope.T[:HD]
        sent_ref[g] = hidden.astype(BF)


def hidden_rows(own, other, frames_g):
    shape = jax.ShapeDtypeStruct((2, HD, ROWS), F32)
    return vmem_call(
        hidden_body, (shape, shape, jax.ShapeDtypeStruct((2, HD, ROWS), BF)), inputs=3
    )(own, other, frames_g)


def project_body(
    sc_ref, all_ref, hidden_ref, w_ref, up_ref, kv_ref, q_ref, normed_ref, unit_ref, inv_ref
):
    total = jnp.zeros((HD, ROWS), F32)
    square = jnp.zeros((HD, ROWS), F32)
    for g in range(GROUPS):
        hidden = all_ref[g].astype(F32)
        total += hidden
        square += hidden * hidden
    center = jnp.sum(total, axis=0, keepdims=True) / WIDTH
    square = jnp.sum(square, axis=0, keepdims=True) / WIDTH
    inv_std = lax.rsqrt(square - center * center + EPS)
    inv_ref[...] = inv_std
    projected = jnp.zeros((ROWS, 3 * HD), F32)
    for g in range(GROUPS):
        normed = ((all_ref[g].astype(F32) - center) * inv_std).astype(BF)
        normed_ref[g] = normed
        projected += lax.dot_general(
            normed,
            w_ref[g * HD : (g + 1) * HD],
            (((0,), (0,)), ((), ())),
            preferred_element_type=F32,
        )
    for g in range(2):
        unit_ref[g] = (hidden_ref[g] - center) * inv_std
    projected = projected.astype(BF)
    pos = sc_ref[0] * ROWS + lax.broadcasted_iota(jnp.int32, (ROWS, LANES - HD), 0)
    lane = lax.broadcasted_iota(jnp.int32, (ROWS, LANES - HD), 1)
    seg = jnp.zeros_like(pos)
    for u in range(3):
        seg += jnp.where(pos >= sc_ref[1 + u], 1, 0)
    nil = jnp.zeros((ROWS, LANES - HD), BF)
    k_mark = jnp.where(seg == lane, 0.0, FAR).astype(BF)
    q_mark = jnp.where(seg == lane, 1.0, 0.0).astype(BF)
    for i in range(8):
        q_ref[i, :, :HD] = projected[:, :HD]
        q_ref[i, :, HD:LANES] = q_mark
        q_ref[i, :, LANES : LANES + HD] = up_ref[...]
        q_ref[i, :, LANES + HD :] = nil
        kv_ref[i, :, :HD] = projected[:, HD : 2 * HD]
        kv_ref[i, :, HD:LANES] = k_mark
        kv_ref[i, :, LANES : LANES + HD] = projected[:, 2 * HD :]
        kv_ref[i, :, LANES + HD :] = nil


def project(scalars, all_t, hidden_t, w_qkv, grad_out):
    return vmem_call(
        project_body,
        (
            jax.ShapeDtypeStruct((8, ROWS, 2 * LANES), BF),
            jax.ShapeDtypeStruct((8, ROWS, 2 * LANES), BF),
            jax.ShapeDtypeStruct((GROUPS, HD, ROWS), BF),
            jax.ShapeDtypeStruct((2, HD, ROWS), F32),
            jax.ShapeDtypeStruct((1, ROWS), F32),
        ),
        scalars=1,
        inputs=4,
        flops=2 * ROWS * WIDTH * 3 * HD,
    )(scalars, all_t, hidden_t, w_qkv, grad_out)


def sums_of(plain, along):
    plain_high = plain.astype(BF).astype(F32)
    along_high = along.astype(BF).astype(F32)
    rows = [plain_high, along_high, plain - plain_high, along - along_high]
    return jnp.concatenate(rows + [jnp.zeros((4, ROWS), F32)], axis=0).astype(BF)


def share_body(od_ref, dkv_ref, normed_ref, w_ref, parts_ref, wide_ref, out_ref, grad_ref):
    out, dq = od_ref[0, 0].astype(F32), od_ref[0, 1].astype(F32)
    for i in range(1, 8):
        out += od_ref[i, 0].astype(F32)
        dq += od_ref[i, 1].astype(F32)
    dkv = dkv_ref[0].astype(F32)
    for i in range(1, 8):
        dkv += dkv_ref[i].astype(F32)
    out_ref[...] = out.T.astype(BF)
    grad_ref[:, :HD] = dq.T.astype(BF)
    grad_ref[:, HD : 2 * HD] = dkv[:, :HD].astype(BF)
    grad_ref[:, 2 * HD :] = dkv[:, LANES : LANES + HD].astype(BF)
    grad = grad_ref[...]
    plain = jnp.zeros((HD, ROWS), F32)
    along = jnp.zeros((HD, ROWS), F32)
    for g in range(GROUPS):
        share = lax.dot_general(
            w_ref[g * HD : (g + 1) * HD], grad, CONTRACT, preferred_element_type=F32
        )
        plain += share
        along += share * normed_ref[g].astype(F32)
        parts_ref[g // 2 % 2, g // 4, g % 2, :HD] = share.astype(BF)
    plain = jnp.sum(plain, axis=0, keepdims=True)
    along = jnp.sum(along, axis=0, keepdims=True)
    sums = sums_of(plain, along)
    for g in range(GROUPS):
        parts_ref[g // 2 % 2, g // 4, g % 2, HD:] = sums
    slab = HD // 4
    wide_ref[...] = jnp.zeros_like(wide_ref)
    for g in range(GROUPS):
        wide = jnp.dot(normed_ref[g], grad, preferred_element_type=F32)
        for x in range(4):
            wide_ref[g * 4 + x, :slab, : 3 * HD] = wide[x * slab : (x + 1) * slab].astype(BF)


def shares(od, dkv, normed_t, w_qkv):
    return vmem_call(
        share_body,
        (
            jax.ShapeDtypeStruct((2, 4, 2, LANES, ROWS), BF),
            jax.ShapeDtypeStruct((64, SLAB, 3 * LANES), BF),
            jax.ShapeDtypeStruct((ROWS, HD), BF),
        ),
        scratch=[pltpu.VMEM((ROWS, 3 * HD), BF)],
        inputs=4,
        flops=4 * ROWS * WIDTH * 3 * HD,
    )(od, dkv, normed_t, w_qkv)


def core_body(parts_ref, out_ref):
    for h in range(4):
        for g in range(2):
            total = parts_ref[0, h, g].astype(F32) + parts_ref[1, h, g].astype(F32)
            out_ref[h, g, :HD] = total[:HD].astype(BF)
            if g == 0:
                plain = total[HD : HD + 1] + total[HD + 2 : HD + 3]
                along = total[HD + 1 : HD + 2] + total[HD + 3 : HD + 4]
            out_ref[h, g, HD:] = sums_of(plain, along)


def core_sum(parts):
    return vmem_call(core_body, jax.ShapeDtypeStruct((4, 2, LANES, ROWS), BF), inputs=1)(parts)


def error_body(parts_ref, unit_ref, inv_ref, slope_ref, grad_ref, error_ref):
    sums = []
    for g in range(2):
        total = parts_ref[0, g].astype(F32)
        for i in range(1, 4):
            total += parts_ref[i, g].astype(F32)
        sums.append(total)
    plain = (sums[0][HD : HD + 1] + sums[0][HD + 2 : HD + 3]) / WIDTH
    along = (sums[0][HD + 1 : HD + 2] + sums[0][HD + 3 : HD + 4]) / WIDTH
    for g in range(2):
        grad = inv_ref[...] * (sums[g][:HD] - plain - unit_ref[g] * along)
        nil = jnp.zeros((LANES - HD, ROWS), F32)
        grad_ref[g] = jnp.concatenate([grad, nil], axis=0).T
        error_ref[g] = jnp.concatenate([slope_ref[g] * grad, nil], axis=0).T.astype(BF)


def errors(parts, unit_t, inv_std, slope_t):
    return vmem_call(
        error_body,
        (
            jax.ShapeDtypeStruct((2, ROWS, LANES), F32),
            jax.ShapeDtypeStruct((2, ROWS, LANES), BF),
        ),
        inputs=4,
    )(parts, unit_t, inv_std, slope_t)


def on_device(frames, conv_weight, w_qkv, lengths, grad_out):
    index = lax.axis_index("tm")
    ends = jnp.cumsum(lengths).astype(jnp.int32)

    def scalars(*first):
        return jnp.concatenate([jnp.stack(first).astype(jnp.int32), ends])

    where = scalars(index // 32, index)

    frames_g = frames.reshape(ROWS, 2, HD).transpose(1, 0, 2)
    frames_g = jnp.pad(frames_g, ((0, 0), (0, 0), (0, LANES - HD)))
    pair = paired(with_halo(frames_g).reshape(2 * PADDED, LANES))
    taps = exchange_z(taps_sent(conv_weight[0]))
    taps = exchange_x(joined(taps, pair, w_qkv, grad_out))
    own, other = convolved(True, where, pair, taps)
    hidden_t, slope_t, sent = hidden_rows(own, other, frames_g)

    all_t = lax.all_gather(sent, "head", axis=0, tiled=True)
    keys, queries, normed_t, unit_t, inv_std = project(
        scalars(index), all_t, hidden_t, w_qkv, grad_out
    )

    queries = exchange_xy(queries)
    keys = exchange_z(keys)
    stats = exchange_xy(attention_stats(queries, keys))
    od, dkv = attention_grads(queries, keys, stats)
    od = exchange_xy(od)
    dkv = exchange_z(dkv)

    parts, wide, attended = shares(od, dkv, normed_t, w_qkv)
    parts = core_sum(exchange_head(parts, CORE_GROUPS))
    parts = exchange_head(parts, HIGH_GROUPS)
    hidden_grad, error = errors(parts, unit_t, inv_std, slope_t)

    wide = lax.all_to_all(wide, "tm", 0, 0)
    pair = paired(with_halo(error).reshape(2 * PADDED, LANES))
    own, other = convolved(False, where, pair, taps)
    frame_grad = (hidden_grad + own + other.astype(F32)).astype(BF)[:, :, :HD]
    weight_grad = jnp.sum(wide[:, : HD // 4, : 3 * HD].astype(F32), axis=0)
    return attended, frame_grad.transpose(1, 0, 2).reshape(ROWS, 2 * HD), weight_grad


def solution(mesh):
    return jax.shard_map(
        on_device,
        mesh=mesh,
        in_specs=(
            P("tm", "head"),
            P("tm", "head", None, None),
            P(None, "head"),
            P(),
            P("tm", "head"),
        ),
        out_specs=(P("tm", "head"), P("tm", "head"), P("tm", "head")),
        check_vma=False,
    )
```

```python
import functools
import math

import jax
import jax.numpy as jnp
from jax import lax
from jax.experimental import pallas as pl
from jax.experimental.pallas import tpu as pltpu
from jax.sharding import PartitionSpec as P

HD = 120
KERNEL = 64
HALF = KERNEL // 2
ROWS = 128
LANES = 128
SCALE = HD ** (-0.5)
SCALE2 = SCALE * math.log2(math.e)
FAR = -(2.0**100)
EPS = 1e-05
INV_ROOT_TWO = 0.7071067811865476
INV_ROOT_TAU = 0.3989422804014327

BF = jnp.bfloat16
F32 = jnp.float32

XY_GROUPS = [[y * 32 + z * 4 + x for y in range(2) for x in range(4)] for z in range(8)]
X_GROUPS = [[y * 32 + z * 4 + x for x in range(4)] for y in range(2) for z in range(8)]
CORE_GROUPS = [[h * 2 + c for c in range(2)] for h in range(4)]
HIGH_GROUPS = [[h * 2 + c for h in range(4)] for c in range(2)]
Z_GROUPS = [[y * 32 + z * 4 + x for z in range(8)] for y in range(2) for x in range(4)]


def exchange_xy(parts):
    return lax.all_to_all(parts, "tm", 0, 0, axis_index_groups=XY_GROUPS)


def exchange_x(parts):
    return lax.all_to_all(parts, "tm", 0, 0, axis_index_groups=X_GROUPS)


def swap(array, bit):
    return lax.ppermute(array, "tm", [(i, i ^ bit) for i in range(64)])


def exchange_z(parts):
    return lax.all_to_all(parts, "tm", 0, 0, axis_index_groups=Z_GROUPS)


def exchange_head(parts, groups):
    return lax.all_to_all(parts, "head", 0, 0, axis_index_groups=groups)


BITS = (32, 2, 1)
SLOTS = (0, 4, 2, 6, 1, 5, 3, 7)


def doubled(array):
    array = array[None]
    for bit in BITS:
        array = jnp.concatenate([array, swap(array, bit)], axis=0)
    return array


def vmem_call(body, out_shape, scratch=(), scalars=0, inputs=0, earlier=0, flops=0):
    return pl.pallas_call(
        body,
        out_shape=out_shape,
        in_specs=[pl.BlockSpec(memory_space=pltpu.SMEM)] * scalars
        + [pl.BlockSpec(memory_space=pltpu.VMEM)] * inputs
        + [pl.BlockSpec(memory_space=pl.ANY)] * earlier,
        out_specs=jax.tree.map(lambda _: pl.BlockSpec(memory_space=pltpu.VMEM), out_shape),
        scratch_shapes=list(scratch),
        compiler_params=pltpu.CompilerParams(vmem_limit_bytes=48 * 1024 * 1024),
        cost_estimate=pl.CostEstimate(flops=flops, bytes_accessed=1 << 20, transcendentals=0),
    )


def bounds_of(pos, ends):
    low = jnp.zeros_like(pos)
    high = jnp.full_like(pos, ends[0])
    for u in range(3):
        inside = pos >= ends[u]
        low = jnp.where(inside, ends[u], low)
        high = jnp.where(inside, ends[u + 1], high)
    return low, high


PADDED = ROWS + KERNEL
TAPS = KERNEL // 2
SPAN = ROWS + TAPS


def conv_body(forward, sc_ref, x_ref, w_ref, *refs):
    own_ref, other_ref = refs[-2:]
    ends = [sc_ref[2 + u] for u in range(4)]
    first = TAPS * (sc_ref[0] if forward else 1 - sc_ref[0])
    row = lax.broadcasted_iota(jnp.int32, (ROWS, LANES), 0)
    for b in range(2):
        shard = sc_ref[1] if b == 0 else sc_ref[1] ^ 32
        pos = shard * ROWS + row
        low, high = bounds_of(pos, ends)
        source = pos + (first - HALF)
        spans = [
            x_ref[b, pl.ds(pl.multiple_of(g * PADDED + first, TAPS), SPAN)].astype(F32)
            for g in range(2)
        ]
        totals = [jnp.zeros((ROWS, LANES), F32) for g in range(2)]
        for rest in range(8):
            rolled = [pltpu.roll(e, SPAN - rest, 0) if rest else e for e in spans]
            for start in range(0, TAPS + 1, 8):
                tap = start + rest if forward else TAPS - start - rest
                if not 0 <= tap < TAPS:
                    continue
                key = source + (start + rest)
                keep = (key >= low) & (key < high)
                for g in range(2):
                    at = (tap // 4 * 2 + g) * LANES
                    piece = jnp.where(keep, rolled[g][start : start + ROWS], 0.0).astype(BF)
                    totals[g] += lax.dot_general(
                        piece,
                        w_ref[tap % 4, at : at + LANES],
                        (((1,), (0 if forward else 1,)), ((), ())),
                        preferred_element_type=F32,
                    )
        for g in range(2):
            if b == 0:
                own_ref[g] = totals[g]
            else:
                other_ref[g] = totals[g].astype(BF)


def taps_body(w_ref, out_ref):
    out_ref[0] = jnp.zeros((2 * LANES, LANES), BF)
    for g in range(2):
        out_ref[0, g * LANES : g * LANES + HD, :HD] = w_ref[g]
    for i in range(1, 8):
        out_ref[i] = out_ref[0]


def taps_sent(weight):
    return vmem_call(
        taps_body, jax.ShapeDtypeStruct((8, 2 * LANES, LANES), BF), inputs=1
    )(weight)


def joined_body(w_ref, own_ref, other_ref, qkv_ref, out_ref):
    for i in range(4):
        for z in range(8):
            out_ref[i, z * 2 * LANES : (z + 1) * 2 * LANES] = w_ref[z]
        for b, rows_ref in enumerate((own_ref, other_ref)):
            start = 16 * LANES + b * ROWS
            out_ref[i, start : start + ROWS] = rows_ref[...]


def joined(taps, own, other, w_qkv):
    return vmem_call(
        joined_body,
        jax.ShapeDtypeStruct((4, 16 * LANES + 2 * ROWS, LANES), BF),
        inputs=3,
        earlier=1,
    )(taps, own, other, w_qkv)


def paired(rows, more=None):
    shards = range(64)
    up = [(i, i + 1) for i in shards[:-1]]
    down = [(i, i - 1) for i in shards[1:]]
    last, head = rows[:, ROWS - HALF :], rows[:, :HALF]
    sent = rows.reshape(2 * ROWS, LANES)
    if more is not None:
        sent = jnp.concatenate([sent, more], axis=0)
    got = swap(sent, 32)
    sides = [
        [lax.ppermute(last, "tm", [(i, j ^ bit) for i, j in up]) for bit in (0, 32)],
        [lax.ppermute(head, "tm", [(i, j ^ bit) for i, j in down]) for bit in (0, 32)],
    ]
    other = got[: 2 * ROWS].reshape(2, ROWS, LANES)
    pair = [
        jnp.concatenate([sides[0][b], middle, sides[1][b]], axis=1)
        for b, middle in enumerate((rows, other))
    ]
    return jnp.stack(pair).reshape(2, 2 * PADDED, LANES), got[2 * ROWS :]


def convolved(forward, scalars, pair, taps, *earlier):
    own, other = vmem_call(
        functools.partial(conv_body, forward),
        (
            jax.ShapeDtypeStruct((2, ROWS, LANES), F32),
            jax.ShapeDtypeStruct((2, ROWS, LANES), BF),
        ),
        scalars=1,
        inputs=2,
        earlier=len(earlier),
        flops=32 * 2 * 2 * 2 * ROWS * HD * HD,
    )(scalars, pair, taps, *earlier)
    return own, swap(other, 32)


CHUNK = 256


N = CHUNK // ROWS
ALL = 8 * ROWS
CONTRACT = (((1,), (1,)), ((), ()))


def upstream_rows(sc_ref, f_ref, d_ref):
    for i, e in enumerate(SLOTS):
        row = 16 * LANES + e // 4 * ROWS
        d_ref[i * ROWS : (i + 1) * ROWS] = f_ref[(sc_ref[0] % 4) ^ (e % 4), row : row + ROWS]


def scored(c, q_ref, kv_ref, d_ref):
    keys = kv_ref[:, :, :LANES].reshape(ALL, LANES)
    values = kv_ref[:, :, LANES:].reshape(ALL, LANES)
    q = q_ref[c * N : (c + 1) * N].reshape(CHUNK, LANES)
    d = d_ref[c * CHUNK : (c + 1) * CHUNK]
    scores = lax.dot_general(keys, q, CONTRACT, preferred_element_type=F32)
    dprobs = lax.dot_general(values, d, CONTRACT, preferred_element_type=F32)
    return keys, values, q, d, scores * SCALE2, dprobs


def stats_body(sc_ref, q_ref, kv_ref, f_ref, out_ref, d_ref):
    upstream_rows(sc_ref, f_ref, d_ref)
    for c in range(ALL // CHUNK):
        _, _, _, _, scores, dprobs = scored(c, q_ref, kv_ref, d_ref)
        peak = jnp.max(scores, axis=0, keepdims=True)
        weight = jnp.exp2(scores - peak)
        total = jnp.sum(weight, axis=0, keepdims=True)
        along = jnp.sum(weight * dprobs, axis=0, keepdims=True)
        for i in range(N):
            columns = slice(i * ROWS, (i + 1) * ROWS)
            shard = pl.ds(sc_ref[0] ^ SLOTS[c * N + i], 1)
            for j, value in enumerate((peak, total, along)):
                out_ref[0, j, shard] = value[:, columns]
    for i in range(1, 8):
        out_ref[i] = out_ref[0]


def grads_body(
    sc_ref, q_ref, kv_ref, f_ref, stats_ref, od_ref, dkv_ref, d_ref, dk_ref, dv_ref
):
    upstream_rows(sc_ref, f_ref, d_ref)
    for c in range(ALL // CHUNK):
        peaks, totals, alongs = (
            jnp.concatenate(
                [stats_ref[:, j, pl.ds(sc_ref[0] ^ SLOTS[c * N + i], 1)] for i in range(N)],
                axis=2,
            )
            for j in range(3)
        )
        top = jnp.max(peaks, axis=0)
        factor = jnp.exp2(peaks - top[None])
        total = jnp.sum(totals * factor, axis=0)
        delta = jnp.sum(alongs * factor, axis=0) / total
        lse = top + jnp.log2(total)
        keys, values, q, d, scores, dprobs = scored(c, q_ref, kv_ref, d_ref)
        probs = jnp.exp2(scores - lse)
        dscores = (probs * (dprobs - delta)).astype(BF)
        probs = probs.astype(BF)
        dv = jnp.dot(probs, d, preferred_element_type=F32)
        dk = jnp.dot(dscores, q, preferred_element_type=F32)
        if c == 0:
            dv_ref[...] = dv
            dk_ref[...] = dk
        else:
            dv_ref[...] += dv
            dk_ref[...] += dk
        inner = (((0,), (0,)), ((), ()))
        out_t = lax.dot_general(values, probs, inner, preferred_element_type=F32)
        dq_t = lax.dot_general(keys, dscores, inner, preferred_element_type=F32) * SCALE
        for i in range(N):
            at = sc_ref[0] ^ SLOTS[c * N + i]
            od_ref[at, 0] = out_t[:HD, i * ROWS : (i + 1) * ROWS].astype(BF)
            od_ref[at, 1] = dq_t[:HD, i * ROWS : (i + 1) * ROWS].astype(BF)
    for i in range(8):
        piece = slice(i * ROWS, (i + 1) * ROWS)
        dkv_ref[i, :, :LANES] = (dk_ref[piece] * SCALE).astype(BF)
        dkv_ref[i, :, LANES:] = dv_ref[piece].astype(BF)


def attention_stats(scalars, queries, keys, gathered):
    return vmem_call(
        stats_body,
        jax.ShapeDtypeStruct((8, 3, 8, ROWS), F32),
        scratch=[pltpu.VMEM((ALL, LANES), BF)],
        scalars=1,
        inputs=3,
        flops=2 * 2 * ALL * ALL * LANES,
    )(scalars, queries, keys, gathered)


def attention_grads(scalars, queries, keys, gathered, stats):
    return vmem_call(
        grads_body,
        (
            jax.ShapeDtypeStruct((8, 2, HD, ROWS), BF),
            jax.ShapeDtypeStruct((8, ROWS, 2 * LANES), BF),
        ),
        scratch=[
            pltpu.VMEM((ALL, LANES), BF),
            pltpu.VMEM((ALL, LANES), F32),
            pltpu.VMEM((ALL, LANES), F32),
        ],
        scalars=1,
        inputs=4,
        flops=6 * 2 * ALL * ALL * LANES,
    )(scalars, queries, keys, gathered, stats)


GROUPS = 16
WIDTH = GROUPS * HD
SLAB = 32


def gelu_parts(inputs):
    normal_cdf = 0.5 * (1.0 + lax.erf(inputs * INV_ROOT_TWO))
    density = jnp.exp(-0.5 * inputs * inputs) * INV_ROOT_TAU
    return inputs * normal_cdf, normal_cdf + inputs * density


def hidden_body(own_ref, other_ref, frames_ref, hidden_ref, slope_ref, sent_ref):
    for g in range(2):
        conv = own_ref[g] + other_ref[g].astype(F32)
        activated, slope = gelu_parts(conv)
        hidden = (frames_ref[g].astype(F32) + activated).T[:HD]
        hidden_ref[g] = hidden
        slope_ref[g] = slope.T[:HD]
        sent_ref[g] = hidden.astype(BF)


def hidden_rows(own, other, frames_g):
    shape = jax.ShapeDtypeStruct((2, HD, ROWS), F32)
    return vmem_call(
        hidden_body, (shape, shape, jax.ShapeDtypeStruct((2, HD, ROWS), BF)), inputs=3
    )(own, other, frames_g)


def project_body(
    sc_ref, all_ref, hidden_ref, w_ref, kv_ref, q_ref, normed_ref, unit_ref, inv_ref
):
    total = jnp.zeros((HD, ROWS), F32)
    square = jnp.zeros((HD, ROWS), F32)
    for g in range(GROUPS):
        hidden = all_ref[g].astype(F32)
        total += hidden
        square += hidden * hidden
    center = jnp.sum(total, axis=0, keepdims=True) / WIDTH
    square = jnp.sum(square, axis=0, keepdims=True) / WIDTH
    inv_std = lax.rsqrt(square - center * center + EPS)
    inv_ref[...] = inv_std
    projected = jnp.zeros((ROWS, 3 * HD), F32)
    for g in range(GROUPS):
        normed = ((all_ref[g].astype(F32) - center) * inv_std).astype(BF)
        normed_ref[g] = normed
        projected += lax.dot_general(
            normed,
            w_ref[g * HD : (g + 1) * HD],
            (((0,), (0,)), ((), ())),
            preferred_element_type=F32,
        )
    for g in range(2):
        unit_ref[g] = (hidden_ref[g] - center) * inv_std
    projected = projected.astype(BF)
    pos = sc_ref[0] * ROWS + lax.broadcasted_iota(jnp.int32, (ROWS, LANES - HD), 0)
    lane = lax.broadcasted_iota(jnp.int32, (ROWS, LANES - HD), 1)
    seg = jnp.zeros_like(pos)
    for u in range(3):
        seg += jnp.where(pos >= sc_ref[1 + u], 1, 0)
    nil = jnp.zeros((ROWS, LANES - HD), BF)
    q_ref[:, :HD] = projected[:, :HD]
    q_ref[:, HD:] = jnp.where(seg == lane, 1.0, 0.0).astype(BF)
    k_mark = jnp.where(seg == lane, 0.0, FAR).astype(BF)
    for i in range(8):
        kv_ref[i, :, :HD] = projected[:, HD : 2 * HD]
        kv_ref[i, :, HD:LANES] = k_mark
        kv_ref[i, :, LANES : LANES + HD] = projected[:, 2 * HD :]
        kv_ref[i, :, LANES + HD :] = nil


def project(scalars, all_t, hidden_t, w_qkv):
    return vmem_call(
        project_body,
        (
            jax.ShapeDtypeStruct((8, ROWS, 2 * LANES), BF),
            jax.ShapeDtypeStruct((ROWS, LANES), BF),
            jax.ShapeDtypeStruct((GROUPS, HD, ROWS), BF),
            jax.ShapeDtypeStruct((2, HD, ROWS), F32),
            jax.ShapeDtypeStruct((1, ROWS), F32),
        ),
        scalars=1,
        inputs=3,
        flops=2 * ROWS * WIDTH * 3 * HD,
    )(scalars, all_t, hidden_t, w_qkv)


def sums_of(plain, along):
    plain_high = plain.astype(BF).astype(F32)
    along_high = along.astype(BF).astype(F32)
    rows = [plain_high, along_high, plain - plain_high, along - along_high]
    return jnp.concatenate(rows + [jnp.zeros((4, ROWS), F32)], axis=0).astype(BF)


def share_body(od_ref, dkv_ref, normed_ref, w_ref, parts_ref, wide_ref, out_ref, grad_ref):
    out, dq = od_ref[0, 0].astype(F32), od_ref[0, 1].astype(F32)
    for i in range(1, 8):
        out += od_ref[i, 0].astype(F32)
        dq += od_ref[i, 1].astype(F32)
    dkv = dkv_ref[0].astype(F32)
    for i in range(1, 8):
        dkv += dkv_ref[i].astype(F32)
    out_ref[...] = out.T.astype(BF)
    grad_ref[:, :HD] = dq.T.astype(BF)
    grad_ref[:, HD : 2 * HD] = dkv[:, :HD].astype(BF)
    grad_ref[:, 2 * HD :] = dkv[:, LANES : LANES + HD].astype(BF)
    grad = grad_ref[...]
    plain = jnp.zeros((HD, ROWS), F32)
    along = jnp.zeros((HD, ROWS), F32)
    for g in range(GROUPS):
        share = lax.dot_general(
            w_ref[g * HD : (g + 1) * HD], grad, CONTRACT, preferred_element_type=F32
        )
        plain += share
        along += share * normed_ref[g].astype(F32)
        parts_ref[g // 2 % 2, g // 4, g % 2, :HD] = share.astype(BF)
    plain = jnp.sum(plain, axis=0, keepdims=True)
    along = jnp.sum(along, axis=0, keepdims=True)
    sums = sums_of(plain, along)
    for g in range(GROUPS):
        parts_ref[g // 2 % 2, g // 4, g % 2, HD:] = sums
    slab = HD // 4
    wide_ref[...] = jnp.zeros_like(wide_ref)
    for g in range(GROUPS):
        wide = jnp.dot(normed_ref[g], grad, preferred_element_type=F32)
        for x in range(4):
            piece = wide[x * slab : (x + 1) * slab].astype(BF)
            row = g % 8 * SLAB
            wide_ref[g // 8 * 4 + x, row : row + slab, : 3 * HD] = piece


def shares(od, dkv, normed_t, w_qkv):
    return vmem_call(
        share_body,
        (
            jax.ShapeDtypeStruct((2, 4, 2, LANES, ROWS), BF),
            jax.ShapeDtypeStruct((8, 8 * SLAB, 3 * LANES), BF),
            jax.ShapeDtypeStruct((ROWS, HD), BF),
        ),
        scratch=[pltpu.VMEM((ROWS, 3 * HD), BF)],
        inputs=4,
        flops=4 * ROWS * WIDTH * 3 * HD,
    )(od, dkv, normed_t, w_qkv)


def wide_body(wide_ref, out_ref):
    for z in range(8):
        rows = slice(z * SLAB, (z + 1) * SLAB)
        total = wide_ref[0, rows].astype(F32)
        for i in range(1, 8):
            total += wide_ref[i, rows].astype(F32)
        out_ref[z] = total.astype(BF)


def wide_sum(wide):
    return vmem_call(
        wide_body, jax.ShapeDtypeStruct((8, SLAB, 3 * LANES), BF), inputs=1
    )(wide)


def core_body(parts_ref, out_ref):
    for h in range(4):
        for g in range(2):
            total = parts_ref[0, h, g].astype(F32) + parts_ref[1, h, g].astype(F32)
            out_ref[h, g, :HD] = total[:HD].astype(BF)
            if g == 0:
                plain = total[HD : HD + 1] + total[HD + 2 : HD + 3]
                along = total[HD + 1 : HD + 2] + total[HD + 3 : HD + 4]
            out_ref[h, g, HD:] = sums_of(plain, along)


def core_sum(parts):
    return vmem_call(core_body, jax.ShapeDtypeStruct((4, 2, LANES, ROWS), BF), inputs=1)(parts)


def error_body(parts_ref, unit_ref, inv_ref, slope_ref, grad_ref, error_ref):
    sums = []
    for g in range(2):
        total = parts_ref[0, g].astype(F32)
        for i in range(1, 4):
            total += parts_ref[i, g].astype(F32)
        sums.append(total)
    plain = (sums[0][HD : HD + 1] + sums[0][HD + 2 : HD + 3]) / WIDTH
    along = (sums[0][HD + 1 : HD + 2] + sums[0][HD + 3 : HD + 4]) / WIDTH
    for g in range(2):
        grad = inv_ref[...] * (sums[g][:HD] - plain - unit_ref[g] * along)
        nil = jnp.zeros((LANES - HD, ROWS), F32)
        grad_ref[g] = jnp.concatenate([grad, nil], axis=0).T
        error_ref[g] = jnp.concatenate([slope_ref[g] * grad, nil], axis=0).T.astype(BF)


def errors(parts, unit_t, inv_std, slope_t):
    return vmem_call(
        error_body,
        (
            jax.ShapeDtypeStruct((2, ROWS, LANES), F32),
            jax.ShapeDtypeStruct((2, ROWS, LANES), BF),
        ),
        inputs=4,
    )(parts, unit_t, inv_std, slope_t)


def on_device(frames, conv_weight, w_qkv, lengths, grad_out):
    index = lax.axis_index("tm")
    ends = jnp.cumsum(lengths).astype(jnp.int32)

    def scalars(*first):
        return jnp.concatenate([jnp.stack(first).astype(jnp.int32), ends])

    y, x = index // 32, index % 4
    where = scalars(y, index)
    order = scalars(y * 4 + x)

    frames_g = frames.reshape(ROWS, 2, HD).transpose(1, 0, 2)
    frames_g = jnp.pad(frames_g, ((0, 0), (0, 0), (0, LANES - HD)))
    upstream = jnp.pad(grad_out, ((0, 0), (0, LANES - HD)))
    pair, other_upstream = paired(frames_g, upstream)
    taps = exchange_z(taps_sent(conv_weight[0]))
    taps = exchange_x(joined(taps, upstream, other_upstream, w_qkv))
    own, other = convolved(True, where, pair, taps)
    hidden_t, slope_t, sent = hidden_rows(own, other, frames_g)

    all_t = lax.all_gather(sent, "head", axis=0, tiled=True)
    keys, queries, normed_t, unit_t, inv_std = project(
        scalars(index), all_t, hidden_t, w_qkv
    )

    keys = exchange_z(keys)
    queries = doubled(queries)
    stats = exchange_xy(attention_stats(order, queries, keys, taps))
    od, dkv = attention_grads(order, queries, keys, taps, stats)
    od = exchange_xy(od)
    dkv = exchange_z(dkv)

    parts, wide, attended = shares(od, dkv, normed_t, w_qkv)
    parts = core_sum(exchange_head(parts, CORE_GROUPS))
    parts = exchange_head(parts, HIGH_GROUPS)
    hidden_grad, error = errors(parts, unit_t, inv_std, slope_t)

    wide = wide_sum(exchange_xy(wide))
    pair, _ = paired(error)
    own, other = convolved(False, where, pair, taps, wide)
    frame_grad = (hidden_grad + own + other.astype(F32)).astype(BF)[:, :, :HD]
    wide = exchange_z(wide)
    weight_grad = jnp.sum(wide[:, : HD // 4, : 3 * HD].astype(F32), axis=0)
    return attended, frame_grad.transpose(1, 0, 2).reshape(ROWS, 2 * HD), weight_grad


def solution(mesh):
    return jax.shard_map(
        on_device,
        mesh=mesh,
        in_specs=(
            P("tm", "head"),
            P("tm", "head", None, None),
            P(None, "head"),
            P(),
            P("tm", "head"),
        ),
        out_specs=(P("tm", "head"), P("tm", "head"), P("tm", "head")),
        check_vma=False,
    )
```

```python
import functools
import math

import jax
import jax.numpy as jnp
from jax import lax
from jax.experimental import pallas as pl
from jax.experimental.pallas import tpu as pltpu
from jax.sharding import PartitionSpec as P

HD = 120
KERNEL = 64
HALF = KERNEL // 2
ROWS = 128
LANES = 128
SCALE = HD ** (-0.5)
SCALE2 = SCALE * math.log2(math.e)
FAR = -(2.0**100)
EPS = 1e-05
INV_ROOT_TWO = 0.7071067811865476
INV_ROOT_TAU = 0.3989422804014327

BF = jnp.bfloat16
F32 = jnp.float32

XY_GROUPS = [[y * 32 + z * 4 + x for y in range(2) for x in range(4)] for z in range(8)]
X_GROUPS = [[y * 32 + z * 4 + x for x in range(4)] for y in range(2) for z in range(8)]
CORE_GROUPS = [[h * 2 + c for c in range(2)] for h in range(4)]
HIGH_GROUPS = [[h * 2 + c for h in range(4)] for c in range(2)]
Z_GROUPS = [[y * 32 + z * 4 + x for z in range(8)] for y in range(2) for x in range(4)]


def exchange_xy(parts):
    return lax.all_to_all(parts, "tm", 0, 0, axis_index_groups=XY_GROUPS)


def exchange_x(parts):
    return lax.all_to_all(parts, "tm", 0, 0, axis_index_groups=X_GROUPS)


def swap(array, bit):
    return lax.ppermute(array, "tm", [(i, i ^ bit) for i in range(64)])


def exchange_z(parts):
    return lax.all_to_all(parts, "tm", 0, 0, axis_index_groups=Z_GROUPS)


def exchange_head(parts, groups):
    return lax.all_to_all(parts, "head", 0, 0, axis_index_groups=groups)


BITS = (32, 2, 1)
SLOTS = (0, 4, 2, 6, 1, 5, 3, 7)


def doubled(array):
    array = array[None]
    for bit in BITS:
        array = jnp.concatenate([array, swap(array, bit)], axis=0)
    return array


def vmem_call(body, out_shape, scratch=(), scalars=0, inputs=0, earlier=0, flops=0):
    return pl.pallas_call(
        body,
        out_shape=out_shape,
        in_specs=[pl.BlockSpec(memory_space=pltpu.SMEM)] * scalars
        + [pl.BlockSpec(memory_space=pltpu.VMEM)] * inputs
        + [pl.BlockSpec(memory_space=pl.ANY)] * earlier,
        out_specs=jax.tree.map(lambda _: pl.BlockSpec(memory_space=pltpu.VMEM), out_shape),
        scratch_shapes=list(scratch),
        compiler_params=pltpu.CompilerParams(vmem_limit_bytes=48 * 1024 * 1024),
        cost_estimate=pl.CostEstimate(flops=flops, bytes_accessed=1 << 20, transcendentals=0),
    )


def bounds_of(pos, ends):
    low = jnp.zeros_like(pos)
    high = jnp.full_like(pos, ends[0])
    for u in range(3):
        inside = pos >= ends[u]
        low = jnp.where(inside, ends[u], low)
        high = jnp.where(inside, ends[u + 1], high)
    return low, high


PADDED = ROWS + KERNEL
TAPS = KERNEL // 2
SPAN = ROWS + TAPS


def conv_body(forward, sc_ref, *refs):
    y, x = sc_ref[0], sc_ref[1]
    ends = [sc_ref[3 + u] for u in range(4)]
    if forward:
        rows, taps, outs = refs[:4], [(refs[4], 0), (refs[5], 0)], refs[6:]
    else:
        rows = [refs[0].at[0], refs[0].at[1]]
        taps = [(refs[1], 0), (refs[2], 0), (refs[3], 0), (refs[3], 16 * LANES)]
        outs = refs[-2:]
    first = TAPS * (y if forward else 1 - y)
    row = lax.broadcasted_iota(jnp.int32, (ROWS, LANES), 0)
    for b, rows_ref in enumerate(rows):
        pos = (sc_ref[2] ^ (0, 32, 2, 34)[b]) * ROWS + row
        low, high = bounds_of(pos, ends)
        spans = [
            rows_ref[pl.ds(pl.multiple_of(g * PADDED + first, TAPS), SPAN)].astype(F32)
            for g in range(2)
        ]
        totals = [jnp.zeros((ROWS, LANES), F32) for g in range(2)]
        for m, (w_ref, base) in enumerate(taps):
            shift = x ^ m if forward else 4 - (x ^ m)
            source = pos + (first + shift - HALF)
            for odd in range(2):
                rolled = [pltpu.roll(e, SPAN - 4 * odd - shift, 0) for e in spans]
                for step in range(odd, 8, 2):
                    key = source + 4 * step
                    keep = (key >= low) & (key < high)
                    z = step if forward else 7 - step
                    start = 8 * (step // 2)
                    for g in range(2):
                        at = base + (z * 2 + g) * LANES
                        piece = jnp.where(keep, rolled[g][start : start + ROWS], 0.0).astype(BF)
                        totals[g] += lax.dot_general(
                            piece,
                            w_ref[at : at + LANES],
                            (((1,), (0 if forward else 1,)), ((), ())),
                            preferred_element_type=F32,
                        )
        for g in range(2):
            outs[b][g] = totals[g] if b == 0 else totals[g].astype(BF)


def convolved(forward, scalars, *arrays, earlier=()):
    own = jax.ShapeDtypeStruct((2, ROWS, LANES), F32)
    other = jax.ShapeDtypeStruct((2, ROWS, LANES), BF)
    own, *others = vmem_call(
        functools.partial(conv_body, forward),
        (own, other, other, other) if forward else (own, other),
        scalars=1,
        inputs=len(arrays),
        earlier=len(earlier),
        flops=32 * 2 * 2 * 2 * ROWS * HD * HD,
    )(scalars, *arrays, *earlier)
    return own, *(swap(array, bit) for array, bit in zip(others, (32, 2, 34)))


def taps_body(w_ref, out_ref):
    out_ref[0] = jnp.zeros((2 * LANES, LANES), BF)
    for g in range(2):
        out_ref[0, g * LANES : g * LANES + HD, :HD] = w_ref[g]
    for i in range(1, 8):
        out_ref[i] = out_ref[0]


def taps_sent(weight):
    return vmem_call(
        taps_body, jax.ShapeDtypeStruct((8, 2 * LANES, LANES), BF), inputs=1
    )(weight)


def near_body(w_ref, b0_ref, b1_ref, b2_ref, b3_ref, qkv_ref, out_ref):
    for z in range(8):
        out_ref[z * 2 * LANES : (z + 1) * 2 * LANES] = w_ref[z]
    for b, rows_ref in enumerate((b0_ref, b1_ref, b2_ref, b3_ref)):
        start = 16 * LANES + b * ROWS
        out_ref[start : start + ROWS] = rows_ref[2 * PADDED :]


def near_taps(taps, blocks, w_qkv):
    return vmem_call(
        near_body,
        jax.ShapeDtypeStruct((16 * LANES + 4 * ROWS, LANES), BF),
        inputs=5,
        earlier=1,
    )(taps, *blocks, w_qkv)


def half_body(near_ref, next_ref, earlier_ref, out_ref):
    out_ref[: 16 * LANES] = near_ref[: 16 * LANES]
    out_ref[16 * LANES :] = next_ref[: 16 * LANES]


def half_taps(near, following, earlier):
    return vmem_call(
        half_body, jax.ShapeDtypeStruct((32 * LANES, LANES), BF), inputs=2, earlier=1
    )(near, following, earlier)


def halos_of(rows, *bits):
    shards = range(64)
    up = [(i, i + 1) for i in shards[:-1]]
    down = [(i, i - 1) for i in shards[1:]]
    last, head = rows[:, ROWS - HALF :], rows[:, :HALF]
    before = [lax.ppermute(last, "tm", [(i, j ^ bit) for i, j in up]) for bit in bits]
    behind = [lax.ppermute(head, "tm", [(i, j ^ bit) for i, j in down]) for bit in bits]
    return list(zip(before, behind))


def four_blocks(rows, more):
    ((before, behind),) = halos_of(rows, 0)
    padded = jnp.concatenate([before, rows, behind], axis=1).reshape(2 * PADDED, LANES)
    block = jnp.concatenate([padded, more], axis=0)
    return [block] + [swap(block, bit) for bit in (32, 2, 34)]


def paired(rows):
    other = swap(rows.reshape(2 * ROWS, LANES), 32).reshape(2, ROWS, LANES)
    pair = [
        jnp.concatenate([before, middle, behind], axis=1)
        for (before, behind), middle in zip(halos_of(rows, 0, 32), (rows, other))
    ]
    return jnp.stack(pair).reshape(2, 2 * PADDED, LANES)


CHUNK = 256


N = CHUNK // ROWS
ALL = 8 * ROWS
CONTRACT = (((1,), (1,)), ((), ()))


def scored(c, q_ref, kv_ref, near_ref, next_ref):
    keys = kv_ref[:, :, :LANES].reshape(ALL, LANES)
    values = kv_ref[:, :, LANES:].reshape(ALL, LANES)
    q = q_ref[c * N : (c + 1) * N].reshape(CHUNK, LANES)
    half = ALL // CHUNK // 2
    start = 16 * LANES + c % half * CHUNK
    d = (near_ref if c < half else next_ref)[start : start + CHUNK]
    scores = lax.dot_general(keys, q, CONTRACT, preferred_element_type=F32)
    dprobs = lax.dot_general(values, d, CONTRACT, preferred_element_type=F32)
    return keys, values, q, d, scores * SCALE2, dprobs


def stats_body(sc_ref, q_ref, kv_ref, near_ref, next_ref, out_ref):
    for c in range(ALL // CHUNK):
        _, _, _, _, scores, dprobs = scored(c, q_ref, kv_ref, near_ref, next_ref)
        peak = jnp.max(scores, axis=0, keepdims=True)
        weight = jnp.exp2(scores - peak)
        total = jnp.sum(weight, axis=0, keepdims=True)
        along = jnp.sum(weight * dprobs, axis=0, keepdims=True)
        for i in range(N):
            columns = slice(i * ROWS, (i + 1) * ROWS)
            shard = pl.ds(sc_ref[0] ^ SLOTS[c * N + i], 1)
            for j, value in enumerate((peak, total, along)):
                out_ref[0, j, shard] = value[:, columns]
    for i in range(1, 8):
        out_ref[i] = out_ref[0]


def grads_body(
    sc_ref, q_ref, kv_ref, near_ref, next_ref, stats_ref, od_ref, dkv_ref, dk_ref, dv_ref
):
    for c in range(ALL // CHUNK):
        peaks, totals, alongs = (
            jnp.concatenate(
                [stats_ref[:, j, pl.ds(sc_ref[0] ^ SLOTS[c * N + i], 1)] for i in range(N)],
                axis=2,
            )
            for j in range(3)
        )
        top = jnp.max(peaks, axis=0)
        factor = jnp.exp2(peaks - top[None])
        total = jnp.sum(totals * factor, axis=0)
        delta = jnp.sum(alongs * factor, axis=0) / total
        lse = top + jnp.log2(total)
        keys, values, q, d, scores, dprobs = scored(c, q_ref, kv_ref, near_ref, next_ref)
        probs = jnp.exp2(scores - lse)
        dscores = (probs * (dprobs - delta)).astype(BF)
        probs = probs.astype(BF)
        dv = jnp.dot(probs, d, preferred_element_type=F32)
        dk = jnp.dot(dscores, q, preferred_element_type=F32)
        if c == 0:
            dv_ref[...] = dv
            dk_ref[...] = dk
        else:
            dv_ref[...] += dv
            dk_ref[...] += dk
        inner = (((0,), (0,)), ((), ()))
        out_t = lax.dot_general(values, probs, inner, preferred_element_type=F32)
        dq_t = lax.dot_general(keys, dscores, inner, preferred_element_type=F32) * SCALE
        for i in range(N):
            at = sc_ref[0] ^ SLOTS[c * N + i]
            od_ref[at, 0] = out_t[:HD, i * ROWS : (i + 1) * ROWS].astype(BF)
            od_ref[at, 1] = dq_t[:HD, i * ROWS : (i + 1) * ROWS].astype(BF)
    for i in range(8):
        piece = slice(i * ROWS, (i + 1) * ROWS)
        dkv_ref[i, :, :LANES] = (dk_ref[piece] * SCALE).astype(BF)
        dkv_ref[i, :, LANES:] = dv_ref[piece].astype(BF)


def attention_stats(scalars, queries, keys, near, following):
    return vmem_call(
        stats_body,
        jax.ShapeDtypeStruct((8, 3, 8, ROWS), F32),
        scalars=1,
        inputs=4,
        flops=2 * 2 * ALL * ALL * LANES,
    )(scalars, queries, keys, near, following)


def attention_grads(scalars, queries, keys, near, following, stats):
    return vmem_call(
        grads_body,
        (
            jax.ShapeDtypeStruct((8, 2, HD, ROWS), BF),
            jax.ShapeDtypeStruct((8, ROWS, 2 * LANES), BF),
        ),
        scratch=[
            pltpu.VMEM((ALL, LANES), F32),
            pltpu.VMEM((ALL, LANES), F32),
        ],
        scalars=1,
        inputs=5,
        flops=6 * 2 * ALL * ALL * LANES,
    )(scalars, queries, keys, near, following, stats)


GROUPS = 16
WIDTH = GROUPS * HD
SLAB = 32


def gelu_parts(inputs):
    normal_cdf = 0.5 * (1.0 + lax.erf(inputs * INV_ROOT_TWO))
    density = jnp.exp(-0.5 * inputs * inputs) * INV_ROOT_TAU
    return inputs * normal_cdf, normal_cdf + inputs * density


def hidden_body(own_ref, y_ref, x_ref, both_ref, frames_ref, hidden_ref, slope_ref, sent_ref):
    for g in range(2):
        conv = own_ref[g] + y_ref[g].astype(F32) + x_ref[g].astype(F32) + both_ref[g].astype(F32)
        activated, slope = gelu_parts(conv)
        hidden = (frames_ref[g].astype(F32) + activated).T[:HD]
        hidden_ref[g] = hidden
        slope_ref[g] = slope.T[:HD]
        sent_ref[g] = hidden.astype(BF)


def hidden_rows(parts, frames_g):
    shape = jax.ShapeDtypeStruct((2, HD, ROWS), F32)
    return vmem_call(
        hidden_body, (shape, shape, jax.ShapeDtypeStruct((2, HD, ROWS), BF)), inputs=5
    )(*parts, frames_g)


def project_body(
    sc_ref, all_ref, hidden_ref, w_ref, kv_ref, q_ref, normed_ref, unit_ref, inv_ref
):
    total = jnp.zeros((HD, ROWS), F32)
    square = jnp.zeros((HD, ROWS), F32)
    for g in range(GROUPS):
        hidden = all_ref[g].astype(F32)
        total += hidden
        square += hidden * hidden
    center = jnp.sum(total, axis=0, keepdims=True) / WIDTH
    square = jnp.sum(square, axis=0, keepdims=True) / WIDTH
    inv_std = lax.rsqrt(square - center * center + EPS)
    inv_ref[...] = inv_std
    projected = jnp.zeros((ROWS, 3 * HD), F32)
    for g in range(GROUPS):
        normed = ((all_ref[g].astype(F32) - center) * inv_std).astype(BF)
        normed_ref[g] = normed
        projected += lax.dot_general(
            normed,
            w_ref[g * HD : (g + 1) * HD],
            (((0,), (0,)), ((), ())),
            preferred_element_type=F32,
        )
    for g in range(2):
        unit_ref[g] = (hidden_ref[g] - center) * inv_std
    projected = projected.astype(BF)
    pos = sc_ref[0] * ROWS + lax.broadcasted_iota(jnp.int32, (ROWS, LANES - HD), 0)
    lane = lax.broadcasted_iota(jnp.int32, (ROWS, LANES - HD), 1)
    seg = jnp.zeros_like(pos)
    for u in range(3):
        seg += jnp.where(pos >= sc_ref[1 + u], 1, 0)
    nil = jnp.zeros((ROWS, LANES - HD), BF)
    q_ref[:, :HD] = projected[:, :HD]
    q_ref[:, HD:] = jnp.where(seg == lane, 1.0, 0.0).astype(BF)
    k_mark = jnp.where(seg == lane, 0.0, FAR).astype(BF)
    for i in range(8):
        kv_ref[i, :, :HD] = projected[:, HD : 2 * HD]
        kv_ref[i, :, HD:LANES] = k_mark
        kv_ref[i, :, LANES : LANES + HD] = projected[:, 2 * HD :]
        kv_ref[i, :, LANES + HD :] = nil


def project(scalars, all_t, hidden_t, w_qkv):
    return vmem_call(
        project_body,
        (
            jax.ShapeDtypeStruct((8, ROWS, 2 * LANES), BF),
            jax.ShapeDtypeStruct((ROWS, LANES), BF),
            jax.ShapeDtypeStruct((GROUPS, HD, ROWS), BF),
            jax.ShapeDtypeStruct((2, HD, ROWS), F32),
            jax.ShapeDtypeStruct((1, ROWS), F32),
        ),
        scalars=1,
        inputs=3,
        flops=2 * ROWS * WIDTH * 3 * HD,
    )(scalars, all_t, hidden_t, w_qkv)


def sums_of(plain, along):
    plain_high = plain.astype(BF).astype(F32)
    along_high = along.astype(BF).astype(F32)
    rows = [plain_high, along_high, plain - plain_high, along - along_high]
    return jnp.concatenate(rows + [jnp.zeros((4, ROWS), F32)], axis=0).astype(BF)


def share_body(od_ref, dkv_ref, normed_ref, w_ref, far_ref, parts_ref, wide_ref, out_ref, grad_ref):
    out, dq = od_ref[0, 0].astype(F32), od_ref[0, 1].astype(F32)
    for i in range(1, 8):
        out += od_ref[i, 0].astype(F32)
        dq += od_ref[i, 1].astype(F32)
    dkv = dkv_ref[0].astype(F32)
    for i in range(1, 8):
        dkv += dkv_ref[i].astype(F32)
    out_ref[...] = out.T.astype(BF)
    grad_ref[:, :HD] = dq.T.astype(BF)
    grad_ref[:, HD : 2 * HD] = dkv[:, :HD].astype(BF)
    grad_ref[:, 2 * HD :] = dkv[:, LANES : LANES + HD].astype(BF)
    grad = grad_ref[...]
    plain = jnp.zeros((HD, ROWS), F32)
    along = jnp.zeros((HD, ROWS), F32)
    for g in range(GROUPS):
        share = lax.dot_general(
            w_ref[g * HD : (g + 1) * HD], grad, CONTRACT, preferred_element_type=F32
        )
        plain += share
        along += share * normed_ref[g].astype(F32)
        parts_ref[g // 2 % 2, g // 4, g % 2, :HD] = share.astype(BF)
    plain = jnp.sum(plain, axis=0, keepdims=True)
    along = jnp.sum(along, axis=0, keepdims=True)
    sums = sums_of(plain, along)
    for g in range(GROUPS):
        parts_ref[g // 2 % 2, g // 4, g % 2, HD:] = sums
    slab = HD // 4
    wide_ref[...] = jnp.zeros_like(wide_ref)
    for g in range(GROUPS):
        wide = jnp.dot(normed_ref[g], grad, preferred_element_type=F32)
        for x in range(4):
            piece = wide[x * slab : (x + 1) * slab].astype(BF)
            row = g % 8 * SLAB
            wide_ref[g // 8 * 4 + x, row : row + slab, : 3 * HD] = piece


def shares(od, dkv, normed_t, w_qkv, earlier):
    return vmem_call(
        share_body,
        (
            jax.ShapeDtypeStruct((2, 4, 2, LANES, ROWS), BF),
            jax.ShapeDtypeStruct((8, 8 * SLAB, 3 * LANES), BF),
            jax.ShapeDtypeStruct((ROWS, HD), BF),
        ),
        scratch=[pltpu.VMEM((ROWS, 3 * HD), BF)],
        inputs=4,
        earlier=1,
        flops=4 * ROWS * WIDTH * 3 * HD,
    )(od, dkv, normed_t, w_qkv, earlier)


def wide_body(wide_ref, out_ref):
    for z in range(8):
        rows = slice(z * SLAB, (z + 1) * SLAB)
        total = wide_ref[0, rows].astype(F32)
        for i in range(1, 8):
            total += wide_ref[i, rows].astype(F32)
        out_ref[z] = total.astype(BF)


def wide_sum(wide):
    return vmem_call(
        wide_body, jax.ShapeDtypeStruct((8, SLAB, 3 * LANES), BF), inputs=1
    )(wide)


def core_body(parts_ref, out_ref):
    for h in range(4):
        for g in range(2):
            total = parts_ref[0, h, g].astype(F32) + parts_ref[1, h, g].astype(F32)
            out_ref[h, g, :HD] = total[:HD].astype(BF)
            if g == 0:
                plain = total[HD : HD + 1] + total[HD + 2 : HD + 3]
                along = total[HD + 1 : HD + 2] + total[HD + 3 : HD + 4]
            out_ref[h, g, HD:] = sums_of(plain, along)


def core_sum(parts):
    return vmem_call(core_body, jax.ShapeDtypeStruct((4, 2, LANES, ROWS), BF), inputs=1)(parts)


def error_body(parts_ref, unit_ref, inv_ref, slope_ref, grad_ref, error_ref):
    sums = []
    for g in range(2):
        total = parts_ref[0, g].astype(F32)
        for i in range(1, 4):
            total += parts_ref[i, g].astype(F32)
        sums.append(total)
    plain = (sums[0][HD : HD + 1] + sums[0][HD + 2 : HD + 3]) / WIDTH
    along = (sums[0][HD + 1 : HD + 2] + sums[0][HD + 3 : HD + 4]) / WIDTH
    for g in range(2):
        grad = inv_ref[...] * (sums[g][:HD] - plain - unit_ref[g] * along)
        nil = jnp.zeros((LANES - HD, ROWS), F32)
        grad_ref[g] = jnp.concatenate([grad, nil], axis=0).T
        error_ref[g] = jnp.concatenate([slope_ref[g] * grad, nil], axis=0).T.astype(BF)


def errors(parts, unit_t, inv_std, slope_t):
    return vmem_call(
        error_body,
        (
            jax.ShapeDtypeStruct((2, ROWS, LANES), F32),
            jax.ShapeDtypeStruct((2, ROWS, LANES), BF),
        ),
        inputs=4,
    )(parts, unit_t, inv_std, slope_t)


def on_device(frames, conv_weight, w_qkv, lengths, grad_out):
    index = lax.axis_index("tm")
    ends = jnp.cumsum(lengths).astype(jnp.int32)

    def scalars(*first):
        return jnp.concatenate([jnp.stack(first).astype(jnp.int32), ends])

    y, x = index // 32, index % 4
    where = scalars(y, x, index)
    order = scalars(y * 4 + x)

    frames_g = frames.reshape(ROWS, 2, HD).transpose(1, 0, 2)
    frames_g = jnp.pad(frames_g, ((0, 0), (0, 0), (0, LANES - HD)))
    upstream = jnp.pad(grad_out, ((0, 0), (0, LANES - HD)))
    blocks = four_blocks(frames_g, upstream)
    near = near_taps(exchange_z(taps_sent(conv_weight[0])), blocks, w_qkv)
    following = swap(near, 1)
    parts = convolved(True, where, *blocks, near, following)
    hidden_t, slope_t, sent = hidden_rows(parts, frames_g)

    all_t = lax.all_gather(sent, "head", axis=0, tiled=True)
    keys, queries, normed_t, unit_t, inv_std = project(
        scalars(index), all_t, hidden_t, w_qkv
    )

    keys = exchange_z(keys)
    queries = doubled(queries)
    stats = exchange_xy(attention_stats(order, queries, keys, near, following))
    od, dkv = attention_grads(order, queries, keys, near, following, stats)
    od = exchange_xy(od)
    far = swap(half_taps(near, following, od), 2)
    dkv = exchange_z(dkv)

    parts, wide, attended = shares(od, dkv, normed_t, w_qkv, far)
    parts = core_sum(exchange_head(parts, CORE_GROUPS))
    parts = exchange_head(parts, HIGH_GROUPS)
    hidden_grad, error = errors(parts, unit_t, inv_std, slope_t)

    wide = wide_sum(exchange_xy(wide))
    own, other = convolved(
        False, where, paired(error), near, following, far, earlier=(wide,)
    )
    frame_grad = (hidden_grad + own + other.astype(F32)).astype(BF)[:, :, :HD]
    wide = exchange_z(wide)
    weight_grad = jnp.sum(wide[:, : HD // 4, : 3 * HD].astype(F32), axis=0)
    return attended, frame_grad.transpose(1, 0, 2).reshape(ROWS, 2 * HD), weight_grad


def solution(mesh):
    return jax.shard_map(
        on_device,
        mesh=mesh,
        in_specs=(
            P("tm", "head"),
            P("tm", "head", None, None),
            P(None, "head"),
            P(),
            P("tm", "head"),
        ),
        out_specs=(P("tm", "head"), P("tm", "head"), P("tm", "head")),
        check_vma=False,
    )
```

```python
import functools
import math

import jax
import jax.numpy as jnp
from jax import lax
from jax.experimental import pallas as pl
from jax.experimental.pallas import tpu as pltpu
from jax.sharding import PartitionSpec as P

HD = 120
KERNEL = 64
HALF = KERNEL // 2
ROWS = 128
LANES = 128
SCALE = HD ** (-0.5)
SCALE2 = SCALE * math.log2(math.e)
FAR = -(2.0**100)
EPS = 1e-05
INV_ROOT_TWO = 0.7071067811865476
INV_ROOT_TAU = 0.3989422804014327

BF = jnp.bfloat16
F32 = jnp.float32

XY_GROUPS = [[y * 32 + z * 4 + x for y in range(2) for x in range(4)] for z in range(8)]
X_GROUPS = [[y * 32 + z * 4 + x for x in range(4)] for y in range(2) for z in range(8)]
CORE_GROUPS = [[h * 2 + c for c in range(2)] for h in range(4)]
HIGH_GROUPS = [[h * 2 + c for h in range(4)] for c in range(2)]
Z_GROUPS = [[y * 32 + z * 4 + x for z in range(8)] for y in range(2) for x in range(4)]


def exchange_xy(parts):
    return lax.all_to_all(parts, "tm", 0, 0, axis_index_groups=XY_GROUPS)


def exchange_x(parts):
    return lax.all_to_all(parts, "tm", 0, 0, axis_index_groups=X_GROUPS)


def swap(array, bit):
    return lax.ppermute(array, "tm", [(i, i ^ bit) for i in range(64)])


def exchange_z(parts):
    return lax.all_to_all(parts, "tm", 0, 0, axis_index_groups=Z_GROUPS)


def exchange_head(parts, groups):
    return lax.all_to_all(parts, "head", 0, 0, axis_index_groups=groups)


BITS = (2, 32, 1)
SLOTS = (0, 2, 4, 6, 1, 3, 5, 7)


def doubled(array):
    array = array[None]
    for bit in BITS:
        array = jnp.concatenate([array, swap(array, bit)], axis=0)
    return array


def vmem_call(body, out_shape, scratch=(), scalars=0, inputs=0, earlier=0, flops=0):
    return pl.pallas_call(
        body,
        out_shape=out_shape,
        in_specs=[pl.BlockSpec(memory_space=pltpu.SMEM)] * scalars
        + [pl.BlockSpec(memory_space=pltpu.VMEM)] * inputs
        + [pl.BlockSpec(memory_space=pl.ANY)] * earlier,
        out_specs=jax.tree.map(lambda _: pl.BlockSpec(memory_space=pltpu.VMEM), out_shape),
        scratch_shapes=list(scratch),
        compiler_params=pltpu.CompilerParams(vmem_limit_bytes=48 * 1024 * 1024),
        cost_estimate=pl.CostEstimate(flops=flops, bytes_accessed=1 << 20, transcendentals=0),
    )


def bounds_of(pos, ends):
    low = jnp.zeros_like(pos)
    high = jnp.full_like(pos, ends[0])
    for u in range(3):
        inside = pos >= ends[u]
        low = jnp.where(inside, ends[u], low)
        high = jnp.where(inside, ends[u + 1], high)
    return low, high


PADDED = ROWS + KERNEL
TAPS = KERNEL // 2
SPAN = ROWS + TAPS


PART = 8 * LANES
LATER = PART + 2 * ROWS


def conv_body(forward, sc_ref, x_ref, *refs):
    near_ref, gy_ref, gx_ref, low_ref, high_ref = refs[:5]
    own_ref, other_ref = refs[-2:]
    y, x = sc_ref[0], sc_ref[1]
    ends = [sc_ref[3 + u] for u in range(4)]
    row = lax.broadcasted_iota(jnp.int32, (ROWS, LANES), 0)
    for b in range(2):
        pos = (sc_ref[2] ^ (0, 2)[b]) * ROWS + row
        low, high = bounds_of(pos, ends)
        totals = [jnp.zeros((ROWS, LANES), F32) for g in range(2)]
        for my in range(2):
            first = TAPS * (y ^ my if forward else 1 - (y ^ my))
            spans = [
                x_ref[b, pl.ds(pl.multiple_of(g * PADDED + first, TAPS), SPAN)].astype(F32)
                for g in range(2)
            ]
            for mx in range(2):
                shift = x ^ mx if forward else 4 - (x ^ mx)
                source = pos + (first + shift - HALF)
                for odd in range(2):
                    rolled = [pltpu.roll(e, SPAN - 4 * odd - shift, 0) for e in spans]
                    for step in range(odd, 8, 2):
                        key = source + 4 * step
                        keep = (key >= low) & (key < high)
                        z = step if forward else 7 - step
                        start = 8 * (step // 2)
                        if my and mx:
                            w_ref, base = (low_ref, 0) if z < 4 else (high_ref, 0)
                        else:
                            w_ref = (near_ref, gx_ref)[mx] if not my else gy_ref
                            base = 0 if z < 4 else LATER
                        for g in range(2):
                            at = base + (z % 4 * 2 + g) * LANES
                            piece = jnp.where(
                                keep, rolled[g][start : start + ROWS], 0.0
                            ).astype(BF)
                            totals[g] += lax.dot_general(
                                piece,
                                w_ref[at : at + LANES],
                                (((1,), (0 if forward else 1,)), ((), ())),
                                preferred_element_type=F32,
                            )
        for g in range(2):
            if b == 0:
                own_ref[g] = totals[g]
            else:
                other_ref[g] = totals[g].astype(BF)


def taps_body(w_ref, out_ref):
    out_ref[0] = jnp.zeros((2 * LANES, LANES), BF)
    for g in range(2):
        out_ref[0, g * LANES : g * LANES + HD, :HD] = w_ref[g]
    for i in range(1, 8):
        out_ref[i] = out_ref[0]


def taps_sent(weight):
    return vmem_call(
        taps_body, jax.ShapeDtypeStruct((8, 2 * LANES, LANES), BF), inputs=1
    )(weight)


def near_body(w_ref, own_ref, other_ref, qkv_ref, out_ref):
    for z in range(8):
        start = z * 2 * LANES if z < 4 else LATER + (z - 4) * 2 * LANES
        out_ref[start : start + 2 * LANES] = w_ref[z]
    out_ref[PART : PART + ROWS] = own_ref[...]
    out_ref[PART + ROWS : LATER] = other_ref[...]


def near_taps(taps, own, other, w_qkv):
    return vmem_call(
        near_body,
        jax.ShapeDtypeStruct((LATER + PART, LANES), BF),
        inputs=3,
        earlier=1,
    )(taps, own, other, w_qkv)


def paired(rows, more=None):
    shards = range(64)
    up = [(i, i + 1) for i in shards[:-1]]
    down = [(i, i - 1) for i in shards[1:]]
    last, head = rows[:, ROWS - HALF :], rows[:, :HALF]
    sent = rows.reshape(2 * ROWS, LANES)
    if more is not None:
        sent = jnp.concatenate([sent, more], axis=0)
    got = swap(sent, 2)
    sides = [
        [lax.ppermute(last, "tm", [(i, j ^ bit) for i, j in up]) for bit in (0, 2)],
        [lax.ppermute(head, "tm", [(i, j ^ bit) for i, j in down]) for bit in (0, 2)],
    ]
    other = got[: 2 * ROWS].reshape(2, ROWS, LANES)
    pair = [
        jnp.concatenate([sides[0][b], middle, sides[1][b]], axis=1)
        for b, middle in enumerate((rows, other))
    ]
    return jnp.stack(pair).reshape(2, 2 * PADDED, LANES), got[2 * ROWS :]


def convolved(forward, scalars, pair, taps, *earlier):
    own, other = vmem_call(
        functools.partial(conv_body, forward),
        (
            jax.ShapeDtypeStruct((2, ROWS, LANES), F32),
            jax.ShapeDtypeStruct((2, ROWS, LANES), BF),
        ),
        scalars=1,
        inputs=6,
        earlier=len(earlier),
        flops=32 * 2 * 2 * 2 * ROWS * HD * HD,
    )(scalars, pair, *taps, *earlier)
    return own, swap(other, 2)


CHUNK = 256


N = CHUNK // ROWS
ALL = 8 * ROWS
CONTRACT = (((1,), (1,)), ((), ()))


def scored(c, q_ref, kv_ref, up_refs):
    keys = kv_ref[:, :, :LANES].reshape(ALL, LANES)
    values = kv_ref[:, :, LANES:].reshape(ALL, LANES)
    q = q_ref[c * N : (c + 1) * N].reshape(CHUNK, LANES)
    d = up_refs[c][PART:LATER]
    scores = lax.dot_general(keys, q, CONTRACT, preferred_element_type=F32)
    dprobs = lax.dot_general(values, d, CONTRACT, preferred_element_type=F32)
    return keys, values, q, d, scores * SCALE2, dprobs


def stats_body(sc_ref, q_ref, kv_ref, *refs):
    *up_refs, out_ref = refs
    for c in range(ALL // CHUNK):
        _, _, _, _, scores, dprobs = scored(c, q_ref, kv_ref, up_refs)
        peak = jnp.max(scores, axis=0, keepdims=True)
        weight = jnp.exp2(scores - peak)
        total = jnp.sum(weight, axis=0, keepdims=True)
        along = jnp.sum(weight * dprobs, axis=0, keepdims=True)
        for i in range(N):
            columns = slice(i * ROWS, (i + 1) * ROWS)
            shard = pl.ds(sc_ref[0] ^ SLOTS[c * N + i], 1)
            for j, value in enumerate((peak, total, along)):
                out_ref[0, j, shard] = value[:, columns]
    for i in range(1, 8):
        out_ref[i] = out_ref[0]


def grads_body(sc_ref, q_ref, kv_ref, *refs):
    *up_refs, stats_ref, od_ref, dkv_ref, dk_ref, dv_ref = refs
    for c in range(ALL // CHUNK):
        peaks, totals, alongs = (
            jnp.concatenate(
                [stats_ref[:, j, pl.ds(sc_ref[0] ^ SLOTS[c * N + i], 1)] for i in range(N)],
                axis=2,
            )
            for j in range(3)
        )
        top = jnp.max(peaks, axis=0)
        factor = jnp.exp2(peaks - top[None])
        total = jnp.sum(totals * factor, axis=0)
        delta = jnp.sum(alongs * factor, axis=0) / total
        lse = top + jnp.log2(total)
        keys, values, q, d, scores, dprobs = scored(c, q_ref, kv_ref, up_refs)
        probs = jnp.exp2(scores - lse)
        dscores = (probs * (dprobs - delta)).astype(BF)
        probs = probs.astype(BF)
        dv = jnp.dot(probs, d, preferred_element_type=F32)
        dk = jnp.dot(dscores, q, preferred_element_type=F32)
        if c == 0:
            dv_ref[...] = dv
            dk_ref[...] = dk
        else:
            dv_ref[...] += dv
            dk_ref[...] += dk
        inner = (((0,), (0,)), ((), ()))
        out_t = lax.dot_general(values, probs, inner, preferred_element_type=F32)
        dq_t = lax.dot_general(keys, dscores, inner, preferred_element_type=F32) * SCALE
        for i in range(N):
            at = sc_ref[0] ^ SLOTS[c * N + i]
            od_ref[at, 0] = out_t[:HD, i * ROWS : (i + 1) * ROWS].astype(BF)
            od_ref[at, 1] = dq_t[:HD, i * ROWS : (i + 1) * ROWS].astype(BF)
    for i in range(8):
        piece = slice(i * ROWS, (i + 1) * ROWS)
        dkv_ref[i, :, :LANES] = (dk_ref[piece] * SCALE).astype(BF)
        dkv_ref[i, :, LANES:] = dv_ref[piece].astype(BF)


def attention_stats(scalars, queries, keys, upstream):
    return vmem_call(
        stats_body,
        jax.ShapeDtypeStruct((8, 3, 8, ROWS), F32),
        scalars=1,
        inputs=6,
        flops=2 * 2 * ALL * ALL * LANES,
    )(scalars, queries, keys, *upstream)


def attention_grads(scalars, queries, keys, upstream, stats):
    return vmem_call(
        grads_body,
        (
            jax.ShapeDtypeStruct((8, 2, HD, ROWS), BF),
            jax.ShapeDtypeStruct((8, ROWS, 2 * LANES), BF),
        ),
        scratch=[
            pltpu.VMEM((ALL, LANES), F32),
            pltpu.VMEM((ALL, LANES), F32),
        ],
        scalars=1,
        inputs=7,
        flops=6 * 2 * ALL * ALL * LANES,
    )(scalars, queries, keys, *upstream, stats)


GROUPS = 16
WIDTH = GROUPS * HD
SLAB = 32


def gelu_parts(inputs):
    normal_cdf = 0.5 * (1.0 + lax.erf(inputs * INV_ROOT_TWO))
    density = jnp.exp(-0.5 * inputs * inputs) * INV_ROOT_TAU
    return inputs * normal_cdf, normal_cdf + inputs * density


def hidden_body(own_ref, other_ref, frames_ref, hidden_ref, slope_ref, sent_ref):
    for g in range(2):
        conv = own_ref[g] + other_ref[g].astype(F32)
        activated, slope = gelu_parts(conv)
        hidden = (frames_ref[g].astype(F32) + activated).T[:HD]
        hidden_ref[g] = hidden
        slope_ref[g] = slope.T[:HD]
        sent_ref[g] = hidden.astype(BF)


def hidden_rows(own, other, frames_g):
    shape = jax.ShapeDtypeStruct((2, HD, ROWS), F32)
    return vmem_call(
        hidden_body, (shape, shape, jax.ShapeDtypeStruct((2, HD, ROWS), BF)), inputs=3
    )(own, other, frames_g)


def project_body(
    sc_ref, all_ref, hidden_ref, w_ref, kv_ref, q_ref, normed_ref, unit_ref, inv_ref
):
    total = jnp.zeros((HD, ROWS), F32)
    square = jnp.zeros((HD, ROWS), F32)
    for g in range(GROUPS):
        hidden = all_ref[g].astype(F32)
        total += hidden
        square += hidden * hidden
    center = jnp.sum(total, axis=0, keepdims=True) / WIDTH
    square = jnp.sum(square, axis=0, keepdims=True) / WIDTH
    inv_std = lax.rsqrt(square - center * center + EPS)
    inv_ref[...] = inv_std
    projected = jnp.zeros((ROWS, 3 * HD), F32)
    for g in range(GROUPS):
        normed = ((all_ref[g].astype(F32) - center) * inv_std).astype(BF)
        normed_ref[g] = normed
        projected += lax.dot_general(
            normed,
            w_ref[g * HD : (g + 1) * HD],
            (((0,), (0,)), ((), ())),
            preferred_element_type=F32,
        )
    for g in range(2):
        unit_ref[g] = (hidden_ref[g] - center) * inv_std
    projected = projected.astype(BF)
    pos = sc_ref[0] * ROWS + lax.broadcasted_iota(jnp.int32, (ROWS, LANES - HD), 0)
    lane = lax.broadcasted_iota(jnp.int32, (ROWS, LANES - HD), 1)
    seg = jnp.zeros_like(pos)
    for u in range(3):
        seg += jnp.where(pos >= sc_ref[1 + u], 1, 0)
    nil = jnp.zeros((ROWS, LANES - HD), BF)
    q_ref[:, :HD] = projected[:, :HD]
    q_ref[:, HD:] = jnp.where(seg == lane, 1.0, 0.0).astype(BF)
    k_mark = jnp.where(seg == lane, 0.0, FAR).astype(BF)
    for i in range(8):
        kv_ref[i, :, :HD] = projected[:, HD : 2 * HD]
        kv_ref[i, :, HD:LANES] = k_mark
        kv_ref[i, :, LANES : LANES + HD] = projected[:, 2 * HD :]
        kv_ref[i, :, LANES + HD :] = nil


def project(scalars, all_t, hidden_t, w_qkv):
    return vmem_call(
        project_body,
        (
            jax.ShapeDtypeStruct((8, ROWS, 2 * LANES), BF),
            jax.ShapeDtypeStruct((ROWS, LANES), BF),
            jax.ShapeDtypeStruct((GROUPS, HD, ROWS), BF),
            jax.ShapeDtypeStruct((2, HD, ROWS), F32),
            jax.ShapeDtypeStruct((1, ROWS), F32),
        ),
        scalars=1,
        inputs=3,
        flops=2 * ROWS * WIDTH * 3 * HD,
    )(scalars, all_t, hidden_t, w_qkv)


def sums_of(plain, along):
    plain_high = plain.astype(BF).astype(F32)
    along_high = along.astype(BF).astype(F32)
    rows = [plain_high, along_high, plain - plain_high, along - along_high]
    return jnp.concatenate(rows + [jnp.zeros((4, ROWS), F32)], axis=0).astype(BF)


def share_body(od_ref, dkv_ref, normed_ref, w_ref, parts_ref, wide_ref, out_ref, grad_ref):
    out, dq = od_ref[0, 0].astype(F32), od_ref[0, 1].astype(F32)
    for i in range(1, 8):
        out += od_ref[i, 0].astype(F32)
        dq += od_ref[i, 1].astype(F32)
    dkv = dkv_ref[0].astype(F32)
    for i in range(1, 8):
        dkv += dkv_ref[i].astype(F32)
    out_ref[...] = out.T.astype(BF)
    grad_ref[:, :HD] = dq.T.astype(BF)
    grad_ref[:, HD : 2 * HD] = dkv[:, :HD].astype(BF)
    grad_ref[:, 2 * HD :] = dkv[:, LANES : LANES + HD].astype(BF)
    grad = grad_ref[...]
    plain = jnp.zeros((HD, ROWS), F32)
    along = jnp.zeros((HD, ROWS), F32)
    for g in range(GROUPS):
        share = lax.dot_general(
            w_ref[g * HD : (g + 1) * HD], grad, CONTRACT, preferred_element_type=F32
        )
        plain += share
        along += share * normed_ref[g].astype(F32)
        parts_ref[g // 2 % 2, g // 4, g % 2, :HD] = share.astype(BF)
    plain = jnp.sum(plain, axis=0, keepdims=True)
    along = jnp.sum(along, axis=0, keepdims=True)
    sums = sums_of(plain, along)
    for g in range(GROUPS):
        parts_ref[g // 2 % 2, g // 4, g % 2, HD:] = sums
    slab = HD // 4
    wide_ref[...] = jnp.zeros_like(wide_ref)
    for g in range(GROUPS):
        wide = jnp.dot(normed_ref[g], grad, preferred_element_type=F32)
        for x in range(4):
            piece = wide[x * slab : (x + 1) * slab].astype(BF)
            row = g % 8 * SLAB
            wide_ref[g // 8 * 4 + x, row : row + slab, : 3 * HD] = piece


def shares(od, dkv, normed_t, w_qkv):
    return vmem_call(
        share_body,
        (
            jax.ShapeDtypeStruct((2, 4, 2, LANES, ROWS), BF),
            jax.ShapeDtypeStruct((8, 8 * SLAB, 3 * LANES), BF),
            jax.ShapeDtypeStruct((ROWS, HD), BF),
        ),
        scratch=[pltpu.VMEM((ROWS, 3 * HD), BF)],
        inputs=4,
        flops=4 * ROWS * WIDTH * 3 * HD,
    )(od, dkv, normed_t, w_qkv)


def wide_body(wide_ref, out_ref):
    for z in range(8):
        rows = slice(z * SLAB, (z + 1) * SLAB)
        total = wide_ref[0, rows].astype(F32)
        for i in range(1, 8):
            total += wide_ref[i, rows].astype(F32)
        out_ref[z] = total.astype(BF)


def wide_sum(wide):
    return vmem_call(
        wide_body, jax.ShapeDtypeStruct((8, SLAB, 3 * LANES), BF), inputs=1
    )(wide)


def core_body(parts_ref, out_ref):
    for h in range(4):
        for g in range(2):
            total = parts_ref[0, h, g].astype(F32) + parts_ref[1, h, g].astype(F32)
            out_ref[h, g, :HD] = total[:HD].astype(BF)
            if g == 0:
                plain = total[HD : HD + 1] + total[HD + 2 : HD + 3]
                along = total[HD + 1 : HD + 2] + total[HD + 3 : HD + 4]
            out_ref[h, g, HD:] = sums_of(plain, along)


def core_sum(parts):
    return vmem_call(core_body, jax.ShapeDtypeStruct((4, 2, LANES, ROWS), BF), inputs=1)(parts)


def error_body(parts_ref, unit_ref, inv_ref, slope_ref, grad_ref, error_ref):
    sums = []
    for g in range(2):
        total = parts_ref[0, g].astype(F32)
        for i in range(1, 4):
            total += parts_ref[i, g].astype(F32)
        sums.append(total)
    plain = (sums[0][HD : HD + 1] + sums[0][HD + 2 : HD + 3]) / WIDTH
    along = (sums[0][HD + 1 : HD + 2] + sums[0][HD + 3 : HD + 4]) / WIDTH
    for g in range(2):
        grad = inv_ref[...] * (sums[g][:HD] - plain - unit_ref[g] * along)
        nil = jnp.zeros((LANES - HD, ROWS), F32)
        grad_ref[g] = jnp.concatenate([grad, nil], axis=0).T
        error_ref[g] = jnp.concatenate([slope_ref[g] * grad, nil], axis=0).T.astype(BF)


def errors(parts, unit_t, inv_std, slope_t):
    return vmem_call(
        error_body,
        (
            jax.ShapeDtypeStruct((2, ROWS, LANES), F32),
            jax.ShapeDtypeStruct((2, ROWS, LANES), BF),
        ),
        inputs=4,
    )(parts, unit_t, inv_std, slope_t)


def on_device(frames, conv_weight, w_qkv, lengths, grad_out):
    index = lax.axis_index("tm")
    ends = jnp.cumsum(lengths).astype(jnp.int32)

    def scalars(*first):
        return jnp.concatenate([jnp.stack(first).astype(jnp.int32), ends])

    y, x = index // 32, index % 4
    where = scalars(y, x, index)
    order = scalars(y * 4 + x)

    frames_g = frames.reshape(ROWS, 2, HD).transpose(1, 0, 2)
    frames_g = jnp.pad(frames_g, ((0, 0), (0, 0), (0, LANES - HD)))
    upstream = jnp.pad(grad_out, ((0, 0), (0, LANES - HD)))
    pair, other_upstream = paired(frames_g, upstream)
    taps = exchange_z(taps_sent(conv_weight[0]))
    near = near_taps(taps, upstream, other_upstream, w_qkv)
    by_y, by_x = swap(near, 32), swap(near, 1)
    both = swap(by_x[:LATER], 32), swap(by_y[LATER:], 1)
    taps = near, by_y, by_x, *both
    upstream = near, by_y, by_x, both[0]
    own, other = convolved(True, where, pair, taps)
    hidden_t, slope_t, sent = hidden_rows(own, other, frames_g)

    all_t = lax.all_gather(sent, "head", axis=0, tiled=True)
    keys, queries, normed_t, unit_t, inv_std = project(
        scalars(index), all_t, hidden_t, w_qkv
    )

    keys = exchange_z(keys)
    queries = doubled(queries)
    stats = exchange_xy(attention_stats(order, queries, keys, upstream))
    od, dkv = attention_grads(order, queries, keys, upstream, stats)
    od = exchange_xy(od)
    dkv = exchange_z(dkv)

    parts, wide, attended = shares(od, dkv, normed_t, w_qkv)
    parts = core_sum(exchange_head(parts, CORE_GROUPS))
    parts = exchange_head(parts, HIGH_GROUPS)
    hidden_grad, error = errors(parts, unit_t, inv_std, slope_t)

    wide = wide_sum(exchange_xy(wide))
    pair, _ = paired(error)
    own, other = convolved(False, where, pair, taps, wide)
    frame_grad = (hidden_grad + own + other.astype(F32)).astype(BF)[:, :, :HD]
    wide = exchange_z(wide)
    weight_grad = jnp.sum(wide[:, : HD // 4, : 3 * HD].astype(F32), axis=0)
    return attended, frame_grad.transpose(1, 0, 2).reshape(ROWS, 2 * HD), weight_grad


def solution(mesh):
    return jax.shard_map(
        on_device,
        mesh=mesh,
        in_specs=(
            P("tm", "head"),
            P("tm", "head", None, None),
            P(None, "head"),
            P(),
            P("tm", "head"),
        ),
        out_specs=(P("tm", "head"), P("tm", "head"), P("tm", "head")),
        check_vma=False,
    )
```

```python
import functools
import math

import jax
import jax.numpy as jnp
from jax import lax
from jax.experimental import pallas as pl
from jax.experimental.pallas import tpu as pltpu
from jax.sharding import PartitionSpec as P

HD = 120
KERNEL = 64
HALF = KERNEL // 2
ROWS = 128
LANES = 128
SCALE = HD ** (-0.5)
SCALE2 = SCALE * math.log2(math.e)
FAR = -(2.0**100)
EPS = 1e-05
INV_ROOT_TWO = 0.7071067811865476
INV_ROOT_TAU = 0.3989422804014327

BF = jnp.bfloat16
F32 = jnp.float32

XY_GROUPS = [[y * 32 + z * 4 + x for y in range(2) for x in range(4)] for z in range(8)]
X_GROUPS = [[y * 32 + z * 4 + x for x in range(4)] for y in range(2) for z in range(8)]
CORE_GROUPS = [[h * 2 + c for c in range(2)] for h in range(4)]
HIGH_GROUPS = [[h * 2 + c for h in range(4)] for c in range(2)]
Z_GROUPS = [[y * 32 + z * 4 + x for z in range(8)] for y in range(2) for x in range(4)]


def exchange_xy(parts):
    return lax.all_to_all(parts, "tm", 0, 0, axis_index_groups=XY_GROUPS)


def exchange_x(parts):
    return lax.all_to_all(parts, "tm", 0, 0, axis_index_groups=X_GROUPS)


def swap(array, bit):
    return lax.ppermute(array, "tm", [(i, i ^ bit) for i in range(64)])


def exchange_z(parts):
    return lax.all_to_all(parts, "tm", 0, 0, axis_index_groups=Z_GROUPS)


def exchange_head(parts, groups):
    return lax.all_to_all(parts, "head", 0, 0, axis_index_groups=groups)


BITS = (1, 2, 32)
SLOTS = (0, 1, 2, 3, 4, 5, 6, 7)


def doubled(array):
    array = array[None]
    for bit in BITS:
        array = jnp.concatenate([array, swap(array, bit)], axis=0)
    return array


def vmem_call(body, out_shape, scratch=(), scalars=0, inputs=0, earlier=0, flops=0):
    return pl.pallas_call(
        body,
        out_shape=out_shape,
        in_specs=[pl.BlockSpec(memory_space=pltpu.SMEM)] * scalars
        + [pl.BlockSpec(memory_space=pltpu.VMEM)] * inputs
        + [pl.BlockSpec(memory_space=pl.ANY)] * earlier,
        out_specs=jax.tree.map(lambda _: pl.BlockSpec(memory_space=pltpu.VMEM), out_shape),
        scratch_shapes=list(scratch),
        compiler_params=pltpu.CompilerParams(vmem_limit_bytes=48 * 1024 * 1024),
        cost_estimate=pl.CostEstimate(flops=flops, bytes_accessed=1 << 20, transcendentals=0),
    )


def bounds_of(pos, ends):
    low = jnp.zeros_like(pos)
    high = jnp.full_like(pos, ends[0])
    for u in range(3):
        inside = pos >= ends[u]
        low = jnp.where(inside, ends[u], low)
        high = jnp.where(inside, ends[u + 1], high)
    return low, high


PADDED = ROWS + KERNEL
TAPS = KERNEL // 2
SPAN = ROWS + TAPS


def conv_body(forward, sc_ref, x_ref, w_ref, *refs):
    own_ref, other_ref = refs[-2:]
    ends = [sc_ref[2 + u] for u in range(4)]
    first = TAPS * (sc_ref[0] if forward else 1 - sc_ref[0])
    row = lax.broadcasted_iota(jnp.int32, (ROWS, LANES), 0)
    for b in range(2):
        shard = sc_ref[1] if b == 0 else sc_ref[1] ^ 32
        pos = shard * ROWS + row
        low, high = bounds_of(pos, ends)
        source = pos + (first - HALF)
        spans = [
            x_ref[b, pl.ds(pl.multiple_of(g * PADDED + first, TAPS), SPAN)].astype(F32)
            for g in range(2)
        ]
        totals = [jnp.zeros((ROWS, LANES), F32) for g in range(2)]
        for rest in range(8):
            rolled = [pltpu.roll(e, SPAN - rest, 0) if rest else e for e in spans]
            for start in range(0, TAPS + 1, 8):
                tap = start + rest if forward else TAPS - start - rest
                if not 0 <= tap < TAPS:
                    continue
                key = source + (start + rest)
                keep = (key >= low) & (key < high)
                for g in range(2):
                    at = (tap // 4 * 2 + g) * LANES
                    piece = jnp.where(keep, rolled[g][start : start + ROWS], 0.0).astype(BF)
                    totals[g] += lax.dot_general(
                        piece,
                        w_ref[tap % 4, at : at + LANES],
                        (((1,), (0 if forward else 1,)), ((), ())),
                        preferred_element_type=F32,
                    )
        for g in range(2):
            if b == 0:
                own_ref[g] = totals[g]
            else:
                other_ref[g] = totals[g].astype(BF)


def taps_body(w_ref, out_ref):
    out_ref[0] = jnp.zeros((2 * LANES, LANES), BF)
    for g in range(2):
        out_ref[0, g * LANES : g * LANES + HD, :HD] = w_ref[g]
    for i in range(1, 8):
        out_ref[i] = out_ref[0]


def taps_sent(weight):
    return vmem_call(
        taps_body, jax.ShapeDtypeStruct((8, 2 * LANES, LANES), BF), inputs=1
    )(weight)


def joined_body(w_ref, own_ref, other_ref, qkv_ref, out_ref):
    for i in range(4):
        for z in range(8):
            out_ref[i, z * 2 * LANES : (z + 1) * 2 * LANES] = w_ref[z]
        for b, rows_ref in enumerate((own_ref, other_ref)):
            start = 16 * LANES + b * ROWS
            out_ref[i, start : start + ROWS] = rows_ref[...]


def joined(taps, own, other, w_qkv):
    return vmem_call(
        joined_body,
        jax.ShapeDtypeStruct((4, 16 * LANES + 2 * ROWS, LANES), BF),
        inputs=3,
        earlier=1,
    )(taps, own, other, w_qkv)


def paired(rows, more=None):
    shards = range(64)
    up = [(i, i + 1) for i in shards[:-1]]
    down = [(i, i - 1) for i in shards[1:]]
    last, head = rows[:, ROWS - HALF :], rows[:, :HALF]
    sent = rows.reshape(2 * ROWS, LANES)
    if more is not None:
        sent = jnp.concatenate([sent, more], axis=0)
    got = swap(sent, 32)
    sides = [
        [lax.ppermute(last, "tm", [(i, j ^ bit) for i, j in up]) for bit in (0, 32)],
        [lax.ppermute(head, "tm", [(i, j ^ bit) for i, j in down]) for bit in (0, 32)],
    ]
    other = got[: 2 * ROWS].reshape(2, ROWS, LANES)
    pair = [
        jnp.concatenate([sides[0][b], middle, sides[1][b]], axis=1)
        for b, middle in enumerate((rows, other))
    ]
    return jnp.stack(pair).reshape(2, 2 * PADDED, LANES), got[2 * ROWS :]


def convolved(forward, scalars, pair, taps, *earlier):
    own, other = vmem_call(
        functools.partial(conv_body, forward),
        (
            jax.ShapeDtypeStruct((2, ROWS, LANES), F32),
            jax.ShapeDtypeStruct((2, ROWS, LANES), BF),
        ),
        scalars=1,
        inputs=2,
        earlier=len(earlier),
        flops=32 * 2 * 2 * 2 * ROWS * HD * HD,
    )(scalars, pair, taps, *earlier)
    return own, swap(other, 32)


CHUNK = 256


N = CHUNK // ROWS
ALL = 8 * ROWS
CONTRACT = (((1,), (1,)), ((), ()))


def upstream_rows(sc_ref, f_ref, d_ref):
    for i, e in enumerate(SLOTS):
        row = 16 * LANES + e // 4 * ROWS
        d_ref[i * ROWS : (i + 1) * ROWS] = f_ref[(sc_ref[0] % 4) ^ (e % 4), row : row + ROWS]


def scored(c, q_ref, kv_ref, d_ref):
    keys = kv_ref[:, :, :LANES].reshape(ALL, LANES)
    values = kv_ref[:, :, LANES:].reshape(ALL, LANES)
    q = q_ref[c * N : (c + 1) * N].reshape(CHUNK, LANES)
    d = d_ref[c * CHUNK : (c + 1) * CHUNK]
    scores = lax.dot_general(keys, q, CONTRACT, preferred_element_type=F32)
    dprobs = lax.dot_general(values, d, CONTRACT, preferred_element_type=F32)
    return keys, values, q, d, scores * SCALE2, dprobs


def stats_body(sc_ref, q_ref, kv_ref, f_ref, out_ref, d_ref):
    upstream_rows(sc_ref, f_ref, d_ref)
    for c in range(ALL // CHUNK):
        _, _, _, _, scores, dprobs = scored(c, q_ref, kv_ref, d_ref)
        peak = jnp.max(scores, axis=0, keepdims=True)
        weight = jnp.exp2(scores - peak)
        total = jnp.sum(weight, axis=0, keepdims=True)
        along = jnp.sum(weight * dprobs, axis=0, keepdims=True)
        for i in range(N):
            columns = slice(i * ROWS, (i + 1) * ROWS)
            shard = pl.ds(sc_ref[0] ^ SLOTS[c * N + i], 1)
            for j, value in enumerate((peak, total, along)):
                out_ref[0, j, shard] = value[:, columns]
    for i in range(1, 8):
        out_ref[i] = out_ref[0]


def grads_body(
    sc_ref, q_ref, kv_ref, f_ref, stats_ref, od_ref, dkv_ref, d_ref, dk_ref, dv_ref
):
    upstream_rows(sc_ref, f_ref, d_ref)
    for c in range(ALL // CHUNK):
        peaks, totals, alongs = (
            jnp.concatenate(
                [stats_ref[:, j, pl.ds(sc_ref[0] ^ SLOTS[c * N + i], 1)] for i in range(N)],
                axis=2,
            )
            for j in range(3)
        )
        top = jnp.max(peaks, axis=0)
        factor = jnp.exp2(peaks - top[None])
        total = jnp.sum(totals * factor, axis=0)
        delta = jnp.sum(alongs * factor, axis=0) / total
        lse = top + jnp.log2(total)
        keys, values, q, d, scores, dprobs = scored(c, q_ref, kv_ref, d_ref)
        probs = jnp.exp2(scores - lse)
        dscores = (probs * (dprobs - delta)).astype(BF)
        probs = probs.astype(BF)
        dv = jnp.dot(probs, d, preferred_element_type=F32)
        dk = jnp.dot(dscores, q, preferred_element_type=F32)
        if c == 0:
            dv_ref[...] = dv
            dk_ref[...] = dk
        else:
            dv_ref[...] += dv
            dk_ref[...] += dk
        inner = (((0,), (0,)), ((), ()))
        out_t = lax.dot_general(values, probs, inner, preferred_element_type=F32)
        dq_t = lax.dot_general(keys, dscores, inner, preferred_element_type=F32) * SCALE
        for i in range(N):
            at = sc_ref[0] ^ SLOTS[c * N + i]
            od_ref[at, 0] = out_t[:HD, i * ROWS : (i + 1) * ROWS].astype(BF)
            od_ref[at, 1] = dq_t[:HD, i * ROWS : (i + 1) * ROWS].astype(BF)
    for i in range(8):
        piece = slice(i * ROWS, (i + 1) * ROWS)
        dkv_ref[i, :, :LANES] = (dk_ref[piece] * SCALE).astype(BF)
        dkv_ref[i, :, LANES:] = dv_ref[piece].astype(BF)


def attention_stats(scalars, queries, keys, gathered):
    return vmem_call(
        stats_body,
        jax.ShapeDtypeStruct((8, 3, 8, ROWS), F32),
        scratch=[pltpu.VMEM((ALL, LANES), BF)],
        scalars=1,
        inputs=3,
        flops=2 * 2 * ALL * ALL * LANES,
    )(scalars, queries, keys, gathered)


def attention_grads(scalars, queries, keys, gathered, stats):
    return vmem_call(
        grads_body,
        (
            jax.ShapeDtypeStruct((8, 2, HD, ROWS), BF),
            jax.ShapeDtypeStruct((8, ROWS, 2 * LANES), BF),
        ),
        scratch=[
            pltpu.VMEM((ALL, LANES), BF),
            pltpu.VMEM((ALL, LANES), F32),
            pltpu.VMEM((ALL, LANES), F32),
        ],
        scalars=1,
        inputs=4,
        flops=6 * 2 * ALL * ALL * LANES,
    )(scalars, queries, keys, gathered, stats)


GROUPS = 16
WIDTH = GROUPS * HD
SLAB = 32


def gelu_parts(inputs):
    normal_cdf = 0.5 * (1.0 + lax.erf(inputs * INV_ROOT_TWO))
    density = jnp.exp(-0.5 * inputs * inputs) * INV_ROOT_TAU
    return inputs * normal_cdf, normal_cdf + inputs * density


def hidden_body(own_ref, other_ref, frames_ref, hidden_ref, slope_ref, sent_ref):
    for g in range(2):
        conv = own_ref[g] + other_ref[g].astype(F32)
        activated, slope = gelu_parts(conv)
        hidden = (frames_ref[g].astype(F32) + activated).T[:HD]
        hidden_ref[g] = hidden
        slope_ref[g] = slope.T[:HD]
        sent_ref[g] = hidden.astype(BF)


def hidden_rows(own, other, frames_g):
    shape = jax.ShapeDtypeStruct((2, HD, ROWS), F32)
    return vmem_call(
        hidden_body, (shape, shape, jax.ShapeDtypeStruct((2, HD, ROWS), BF)), inputs=3
    )(own, other, frames_g)


def project_body(
    sc_ref, all_ref, hidden_ref, w_ref, kv_ref, q_ref, normed_ref, unit_ref, inv_ref
):
    total = jnp.zeros((HD, ROWS), F32)
    square = jnp.zeros((HD, ROWS), F32)
    for g in range(GROUPS):
        hidden = all_ref[g].astype(F32)
        total += hidden
        square += hidden * hidden
    center = jnp.sum(total, axis=0, keepdims=True) / WIDTH
    square = jnp.sum(square, axis=0, keepdims=True) / WIDTH
    inv_std = lax.rsqrt(square - center * center + EPS)
    inv_ref[...] = inv_std
    projected = jnp.zeros((ROWS, 3 * HD), F32)
    for g in range(GROUPS):
        normed = ((all_ref[g].astype(F32) - center) * inv_std).astype(BF)
        normed_ref[g] = normed
        projected += lax.dot_general(
            normed,
            w_ref[g * HD : (g + 1) * HD],
            (((0,), (0,)), ((), ())),
            preferred_element_type=F32,
        )
    for g in range(2):
        unit_ref[g] = (hidden_ref[g] - center) * inv_std
    projected = projected.astype(BF)
    pos = sc_ref[0] * ROWS + lax.broadcasted_iota(jnp.int32, (ROWS, LANES - HD), 0)
    lane = lax.broadcasted_iota(jnp.int32, (ROWS, LANES - HD), 1)
    seg = jnp.zeros_like(pos)
    for u in range(3):
        seg += jnp.where(pos >= sc_ref[1 + u], 1, 0)
    nil = jnp.zeros((ROWS, LANES - HD), BF)
    q_ref[:, :HD] = projected[:, :HD]
    q_ref[:, HD:] = jnp.where(seg == lane, 1.0, 0.0).astype(BF)
    k_mark = jnp.where(seg == lane, 0.0, FAR).astype(BF)
    for i in range(8):
        kv_ref[i, :, :HD] = projected[:, HD : 2 * HD]
        kv_ref[i, :, HD:LANES] = k_mark
        kv_ref[i, :, LANES : LANES + HD] = projected[:, 2 * HD :]
        kv_ref[i, :, LANES + HD :] = nil


def project(scalars, all_t, hidden_t, w_qkv):
    return vmem_call(
        project_body,
        (
            jax.ShapeDtypeStruct((8, ROWS, 2 * LANES), BF),
            jax.ShapeDtypeStruct((ROWS, LANES), BF),
            jax.ShapeDtypeStruct((GROUPS, HD, ROWS), BF),
            jax.ShapeDtypeStruct((2, HD, ROWS), F32),
            jax.ShapeDtypeStruct((1, ROWS), F32),
        ),
        scalars=1,
        inputs=3,
        flops=2 * ROWS * WIDTH * 3 * HD,
    )(scalars, all_t, hidden_t, w_qkv)


def sums_of(plain, along):
    plain_high = plain.astype(BF).astype(F32)
    along_high = along.astype(BF).astype(F32)
    rows = [plain_high, along_high, plain - plain_high, along - along_high]
    return jnp.concatenate(rows + [jnp.zeros((4, ROWS), F32)], axis=0).astype(BF)


def share_body(od_ref, dkv_ref, normed_ref, w_ref, parts_ref, wide_ref, out_ref, grad_ref):
    out, dq = od_ref[0, 0].astype(F32), od_ref[0, 1].astype(F32)
    for i in range(1, 8):
        out += od_ref[i, 0].astype(F32)
        dq += od_ref[i, 1].astype(F32)
    dkv = dkv_ref[0].astype(F32)
    for i in range(1, 8):
        dkv += dkv_ref[i].astype(F32)
    out_ref[...] = out.T.astype(BF)
    grad_ref[:, :HD] = dq.T.astype(BF)
    grad_ref[:, HD : 2 * HD] = dkv[:, :HD].astype(BF)
    grad_ref[:, 2 * HD :] = dkv[:, LANES : LANES + HD].astype(BF)
    grad = grad_ref[...]
    plain = jnp.zeros((HD, ROWS), F32)
    along = jnp.zeros((HD, ROWS), F32)
    for g in range(GROUPS):
        share = lax.dot_general(
            w_ref[g * HD : (g + 1) * HD], grad, CONTRACT, preferred_element_type=F32
        )
        plain += share
        along += share * normed_ref[g].astype(F32)
        parts_ref[g // 2 % 2, g // 4, g % 2, :HD] = share.astype(BF)
    plain = jnp.sum(plain, axis=0, keepdims=True)
    along = jnp.sum(along, axis=0, keepdims=True)
    sums = sums_of(plain, along)
    for g in range(GROUPS):
        parts_ref[g // 2 % 2, g // 4, g % 2, HD:] = sums
    slab = HD // 4
    wide_ref[...] = jnp.zeros_like(wide_ref)
    for g in range(GROUPS):
        wide = jnp.dot(normed_ref[g], grad, preferred_element_type=F32)
        for x in range(4):
            piece = wide[x * slab : (x + 1) * slab].astype(BF)
            row = g % 8 * SLAB
            wide_ref[g // 8 * 4 + x, row : row + slab, : 3 * HD] = piece


def shares(od, dkv, normed_t, w_qkv):
    return vmem_call(
        share_body,
        (
            jax.ShapeDtypeStruct((2, 4, 2, LANES, ROWS), BF),
            jax.ShapeDtypeStruct((8, 8 * SLAB, 3 * LANES), BF),
            jax.ShapeDtypeStruct((ROWS, HD), BF),
        ),
        scratch=[pltpu.VMEM((ROWS, 3 * HD), BF)],
        inputs=4,
        flops=4 * ROWS * WIDTH * 3 * HD,
    )(od, dkv, normed_t, w_qkv)


def wide_body(wide_ref, out_ref):
    for z in range(8):
        rows = slice(z * SLAB, (z + 1) * SLAB)
        total = wide_ref[0, rows].astype(F32)
        for i in range(1, 8):
            total += wide_ref[i, rows].astype(F32)
        out_ref[z] = total.astype(BF)


def wide_sum(wide):
    return vmem_call(
        wide_body, jax.ShapeDtypeStruct((8, SLAB, 3 * LANES), BF), inputs=1
    )(wide)


def core_body(parts_ref, out_ref):
    for h in range(4):
        for g in range(2):
            total = parts_ref[0, h, g].astype(F32) + parts_ref[1, h, g].astype(F32)
            out_ref[h, g, :HD] = total[:HD].astype(BF)
            if g == 0:
                plain = total[HD : HD + 1] + total[HD + 2 : HD + 3]
                along = total[HD + 1 : HD + 2] + total[HD + 3 : HD + 4]
            out_ref[h, g, HD:] = sums_of(plain, along)


def core_sum(parts):
    return vmem_call(core_body, jax.ShapeDtypeStruct((4, 2, LANES, ROWS), BF), inputs=1)(parts)


def error_body(parts_ref, unit_ref, inv_ref, slope_ref, grad_ref, error_ref):
    sums = []
    for g in range(2):
        total = parts_ref[0, g].astype(F32)
        for i in range(1, 4):
            total += parts_ref[i, g].astype(F32)
        sums.append(total)
    plain = (sums[0][HD : HD + 1] + sums[0][HD + 2 : HD + 3]) / WIDTH
    along = (sums[0][HD + 1 : HD + 2] + sums[0][HD + 3 : HD + 4]) / WIDTH
    for g in range(2):
        grad = inv_ref[...] * (sums[g][:HD] - plain - unit_ref[g] * along)
        nil = jnp.zeros((LANES - HD, ROWS), F32)
        grad_ref[g] = jnp.concatenate([grad, nil], axis=0).T
        error_ref[g] = jnp.concatenate([slope_ref[g] * grad, nil], axis=0).T.astype(BF)


def errors(parts, unit_t, inv_std, slope_t):
    return vmem_call(
        error_body,
        (
            jax.ShapeDtypeStruct((2, ROWS, LANES), F32),
            jax.ShapeDtypeStruct((2, ROWS, LANES), BF),
        ),
        inputs=4,
    )(parts, unit_t, inv_std, slope_t)


def on_device(frames, conv_weight, w_qkv, lengths, grad_out):
    index = lax.axis_index("tm")
    ends = jnp.cumsum(lengths).astype(jnp.int32)

    def scalars(*first):
        return jnp.concatenate([jnp.stack(first).astype(jnp.int32), ends])

    y, x = index // 32, index % 4
    where = scalars(y, index)
    order = scalars(y * 4 + x)

    frames_g = frames.reshape(ROWS, 2, HD).transpose(1, 0, 2)
    frames_g = jnp.pad(frames_g, ((0, 0), (0, 0), (0, LANES - HD)))
    upstream = jnp.pad(grad_out, ((0, 0), (0, LANES - HD)))
    pair, other_upstream = paired(frames_g, upstream)
    taps = exchange_z(taps_sent(conv_weight[0]))
    taps = exchange_x(joined(taps, upstream, other_upstream, w_qkv))
    own, other = convolved(True, where, pair, taps)
    hidden_t, slope_t, sent = hidden_rows(own, other, frames_g)

    all_t = lax.all_gather(sent, "head", axis=0, tiled=True)
    keys, queries, normed_t, unit_t, inv_std = project(
        scalars(index), all_t, hidden_t, w_qkv
    )

    keys = exchange_z(keys)
    queries = doubled(queries)
    stats = exchange_xy(attention_stats(order, queries, keys, taps))
    od, dkv = attention_grads(order, queries, keys, taps, stats)
    dkv = exchange_z(dkv)
    od = exchange_xy(od)

    parts, wide, attended = shares(od, dkv, normed_t, w_qkv)
    parts = core_sum(exchange_head(parts, CORE_GROUPS))
    parts = exchange_head(parts, HIGH_GROUPS)
    hidden_grad, error = errors(parts, unit_t, inv_std, slope_t)

    wide = wide_sum(exchange_xy(wide))
    pair, _ = paired(error)
    own, other = convolved(False, where, pair, taps, wide)
    frame_grad = (hidden_grad + own + other.astype(F32)).astype(BF)[:, :, :HD]
    wide = exchange_z(wide)
    weight_grad = jnp.sum(wide[:, : HD // 4, : 3 * HD].astype(F32), axis=0)
    return attended, frame_grad.transpose(1, 0, 2).reshape(ROWS, 2 * HD), weight_grad


def solution(mesh):
    return jax.shard_map(
        on_device,
        mesh=mesh,
        in_specs=(
            P("tm", "head"),
            P("tm", "head", None, None),
            P(None, "head"),
            P(),
            P("tm", "head"),
        ),
        out_specs=(P("tm", "head"), P("tm", "head"), P("tm", "head")),
        check_vma=False,
    )
```
